32 devices in a mesh: groups: 2 (over y), blk: 16 (over z, x, core).
Axes of the slice: x: 2, y: 2, z: 4, core: 2. Of those that a mesh axis runs over, the one named last changes fastest.
Arguments:
- snapshots: bfloat16 [64, 64, 16, 128], P(None, ('groups', 'blk')), parts along dimension 1, may hold values from -200 to 200
- old_modes: bfloat16 [192, 64, 16, 128], P(None, ('groups', 'blk')), parts along dimension 1, may hold values from -60 to 60
- mode_scales: float32 [384], P('groups'), parts along dimension 0, may hold values from 0.3 to 3
- plane_counts: int32 [32], P(('groups', 'blk')), parts along dimension 0, may hold values from 1 to 2, 20 in all
- links: int32 [32, 2], P(('groups', 'blk')), parts along dimension 0, may hold values from 0 to 1, as said below
Outputs:
- new_modes: bfloat16 [256, 64, 16, 128], P(None, ('groups', 'blk')), parts along dimension 1
- factor: float32 [512, 256], P('groups'), parts along dimension 0
The draws below stay inside these ranges and needn't reach their ends.
There are 2 independent parts, one for each index of `groups`. The reference program is written for one: setup_inputs(seed, part) draws one part's arguments, and reference() takes and returns one part's arrays. A program takes and returns all parts, laid end to end along the dimension named above; each array names one. Nothing has to cross between parts.
Inputs may be any that keep to these rules, and one draw needn't show every extreme that they name: links[b, 1] equals links[b + 1 mod 16, 0]; 1 joins two blocks, 0 is a wall.
All inputs are finite; a program needn't handle non-finite values. No bound on the sum of `plane_counts` on one device may be relied on, other than what follows from the above.
Results may differ from the reference program's by a relative error of at most 0.0095.
Values may be sent and summed in bfloat16 or wider, within the bound.
No kernel may reach another device: no remote copies, remote signals or barrier semaphores. Data moves between devices by JAX's collectives and lax.ppermute only.
A program may use at most 128 MiB of HBM per device.

```python
import math
import jax
import jax.numpy as jnp
import numpy as np
from jax import lax

NEW = 64
KEEP = 192
LMAX = 2
CY = 16
CZ = 128
COLS = 256
BLOCKS = 16
PLANES = 32
CELLS = 65536


def common_fields(key):
    base = jax.random.fold_in(key, 11)
    key_one, key_two, key_three = jax.random.split(base, 3)
    mode_noise = jnp.clip(jax.random.normal(key_one, (KEEP, PLANES, CY, CZ), jnp.float32), -4.0, 4.0)
    shared = jnp.clip(jax.random.normal(key_two, (PLANES, CY, CZ), jnp.float32), -4.0, 4.0)
    low_end, high_end = (0.3, 3.0)
    position = jnp.arange(PLANES, dtype=jnp.float32) / (PLANES - 1)
    plane_scale = jnp.exp(jax.random.uniform(key_three, (PLANES,), jnp.float32, jnp.log(low_end), jnp.log(high_end)))
    plane_scale = plane_scale * jnp.sqrt(1.0 + 2.0 * position)
    return (mode_noise, shared, plane_scale)


def draw_old_modes(key, part):
    mode_noise, shared, plane_scale = common_fields(key)
    values = (mode_noise + 0.5 * shared[None]) * plane_scale[None, :, None, None]
    return values.astype(jnp.bfloat16)


def draw_snapshots(key, part):
    mode_noise, shared, plane_scale = common_fields(key)
    own_key, column_key = jax.random.split(jax.random.fold_in(key, 23))
    noise = jnp.clip(jax.random.normal(own_key, (NEW, PLANES, CY, CZ), jnp.float32), -4.0, 4.0)
    column_scale = jnp.exp(jax.random.uniform(column_key, (NEW,), jnp.float32, jnp.log(0.3), jnp.log(3.0)))
    values = noise + 0.8 * mode_noise[:NEW] + 0.5 * shared[None]
    values = values * plane_scale[None, :, None, None] * column_scale[:, None, None, None]
    return values.astype(jnp.bfloat16)


def draw_links(key, part):
    joined = (jax.random.randint(jax.random.fold_in(key, 5), (BLOCKS,), 0, 4) != 0).astype(jnp.int32)
    return jnp.stack([jnp.roll(joined, 1), joined], axis=1)


def length_profile(amount, total, most, skew):
    weights = [(1 << 20) // math.isqrt(rank ** skew) + 1 for rank in range(2, amount + 1)]
    rest, holding = total - most - (amount - 1), [1] * (amount - 1)
    while rest > 0:
        movable = [i for i in range(amount - 1) if holding[i] < most]
        mass, remaining = sum([weights[i] for i in movable]), rest
        for i in movable:
            extra = min(most - holding[i], max(1, remaining * weights[i] // mass), rest)
            holding[i] = holding[i] + extra
            rest = rest - extra
    return np.array([most] + holding)


def uneven(stream_key, amount, total, limit, lean):
    if amount == 2:
        one = jax.random.randint(stream_key, (), max(1, total - limit), min(limit, total - 1) + 1)
        return jnp.stack([one, total - one])
    lengths = jnp.asarray(length_profile(amount, total, limit, lean), jnp.int32)
    pairs = (amount - 1) // 2
    donor, taker = lengths[1:1 + 2 * pairs:2], lengths[2:2 + 2 * pairs:2]
    room = jnp.minimum(donor - 1, limit - taker)
    shifted = jax.random.randint(jax.random.fold_in(stream_key, 1), (pairs,), 0, 1 << 20) % (room + 1)
    lengths = lengths.at[1:1 + 2 * pairs:2].set(donor - shifted).at[2:2 + 2 * pairs:2].set(taker + shifted)
    return lengths[jax.random.permutation(jax.random.fold_in(stream_key, 2), amount)]


def setup_inputs(seed: int = 0, part: int = 0) -> dict:
    seeds = jax.random.split(jax.random.key(seed), 6)
    own_keys = jax.random.split(jax.random.fold_in(seeds[5], part), 6)
    snapshots = draw_snapshots(jax.random.fold_in(jax.random.fold_in(seeds[5], part), 71), part)
    old_modes = draw_old_modes(jax.random.fold_in(jax.random.fold_in(seeds[5], part), 71), part)
    mode_scales = jnp.clip(jnp.exp(jax.random.uniform(own_keys[2], (KEEP,), jnp.float32, math.log(0.3), math.log(3.0))), 0.3, 3.0)
    plane_counts = uneven(own_keys[3], BLOCKS, BLOCKS * LMAX * 5 // 8, LMAX, 2).astype(jnp.int32)
    links = draw_links(jax.random.fold_in(jax.random.fold_in(seeds[5], part), 71), part)
    return dict(snapshots=snapshots, old_modes=old_modes, mode_scales=mode_scales, plane_counts=plane_counts, links=links)


def smooth_along(field, along):
    widths = [(0, 0)] * field.ndim
    widths[along] = (1, 1)
    padded = jnp.pad(field, widths)
    length = field.shape[along]
    lower = lax.slice_in_dim(padded, 0, length, axis=along)
    upper = lax.slice_in_dim(padded, 2, length + 2, axis=along)
    return 0.25 * lower + 0.5 * field + 0.25 * upper

def reference(snapshots, old_modes, mode_scales, plane_counts, links):
    shaped = snapshots.astype(jnp.float32).reshape(NEW, BLOCKS, LMAX, CY, CZ)
    plane_ids = jnp.arange(LMAX, dtype=jnp.int32)
    alive = (plane_ids[None, :] < plane_counts[:, None]).astype(jnp.float32)
    last_pick = (plane_ids[None, :] == plane_counts[:, None] - 1).astype(jnp.float32)
    masked = shaped * alive[None, :, :, None, None]
    last_plane = jnp.sum(masked * last_pick[None, :, :, None, None], axis=2)
    first_plane = masked[:, :, 0]
    left_halo = jnp.roll(last_plane, 1, axis=1) * links[:, 0].astype(jnp.float32)[None, :, None, None]
    right_halo = jnp.roll(first_plane, -1, axis=1) * links[:, 1].astype(jnp.float32)[None, :, None, None]
    behind = jnp.concatenate([left_halo[:, :, None], masked[:, :, :-1]], axis=2)
    forward = jnp.concatenate([masked[:, :, 1:], jnp.zeros_like(masked[:, :, :1])], axis=2)
    forward = forward + last_pick[None, :, :, None, None] * right_halo[:, :, None]
    along_planes = 0.25 * behind + 0.5 * masked + 0.25 * forward
    smoothed = smooth_along(smooth_along(along_planes, 3), 4)
    filtered = (smoothed * alive[None, :, :, None, None]).astype(jnp.bfloat16)
    filtered = filtered.reshape(NEW, PLANES * CY * CZ)
    alive_flat = alive.reshape(PLANES)
    scaled = (mode_scales[:, None, None, None] * old_modes.astype(jnp.float32) * alive_flat[None, :, None, None]).astype(jnp.bfloat16)
    stacked = jnp.concatenate([filtered, scaled.reshape(KEEP, PLANES * CY * CZ)], axis=0)
    gram = jnp.dot(stacked.astype(jnp.float32), stacked.T.astype(jnp.float32), preferred_element_type=jnp.float32) / CELLS
    factor = jnp.linalg.cholesky(gram).T
    inverse = jax.scipy.linalg.solve_triangular(factor, jnp.eye(COLS, dtype=jnp.float32), lower=False)
    result = jnp.dot(inverse.T, stacked.astype(jnp.float32), precision=lax.Precision.HIGHEST)
    return (result.reshape(COLS, PLANES, CY, CZ).astype(jnp.bfloat16), factor)
```

```python
import jax
import jax.numpy as jnp
from jax import lax
from jax.experimental import pallas as pl
from jax.experimental.pallas import tpu as pltpu
from jax.sharding import PartitionSpec as P

PANEL = 16
LANES = 128
SUBS = 8


def with_halo(x, sides, width):
    for axis, dim in sides:
        peers, length = (lax.axis_size(axis), x.shape[dim])
        up = [(i, (i + 1) % peers) for i in range(peers)]
        down = [(j, i) for i, j in up]
        last = lax.slice_in_dim(x, length - width, length, axis=dim)
        leading = lax.slice_in_dim(x, 0, width, axis=dim)
        before = lax.ppermute(last, axis, up)
        after = lax.ppermute(leading, axis, down)
        x = jnp.concatenate([before, x, after], axis=dim)
    return x


def smooth_along(field, along):
    widths = [(0, 0)] * field.ndim
    widths[along] = (1, 1)
    padded = jnp.pad(field, widths)
    length = field.shape[along]
    lower = lax.slice_in_dim(padded, 0, length, axis=along)
    upper = lax.slice_in_dim(padded, 2, length + 2, axis=along)
    return 0.25 * lower + 0.5 * field + 0.25 * upper


def gram_term(left_rows, right_rows):
    return lax.dot_general(
        left_rows, right_rows, (((1,), (1,)), ((), ())), preferred_element_type=jnp.float32
    )


def factor_panel(tile, tiles, panel, t_ref, f_ref, x_ref, cols, rows, vpad):
    first = pl.multiple_of(panel * PANEL, PANEL)
    off = pl.multiple_of(first - tile * LANES, PANEL)
    here = pl.ds(first, PANEL)
    lane = lax.broadcasted_iota(jnp.int32, (PANEL, LANES), 1)
    sub = lax.broadcasted_iota(jnp.int32, (PANEL, LANES), 0)
    inside = (lane >= off) & (lane < off + PANEL)
    own = t_ref[here, tile * LANES:(tile + 1) * LANES]
    for s in range(tiles):
        if s == tile:
            block = jnp.where(inside, jnp.where(lane - off == sub, 1.0, 0.0), own)
        else:
            block = t_ref[here, s * LANES:(s + 1) * LANES]
        rows[pl.ds(s, PANEL, stride=SUBS), :] = block
    rows[pl.ds(tiles, PANEL, stride=SUBS), :] = own
    turned = pltpu.roll(own, lax.rem(LANES - off, LANES), axis=1)
    for j in range(PANEL):
        cols[j] = jnp.broadcast_to(turned[:, j:j + 1], (PANEL, LANES))
    entry = [
        [jnp.broadcast_to(cols[j, i:i + 1, :], (SUBS, LANES)) for j in range(i + 1)]
        for i in range(PANEL)
    ]
    y = [rows[i * SUBS:(i + 1) * SUBS, :] for i in range(PANEL)]
    unit = [[None] * PANEL for _ in range(PANEL)]
    recip = []
    for k in range(PANEL):
        recip.append(1.0 / entry[k][k])
        for i in range(k + 1, PANEL):
            unit[i][k] = entry[i][k] * recip[k]
        for j in range(k + 1, PANEL):
            for i in range(j, PANEL):
                entry[i][j] = entry[i][j] - unit[i][k] * entry[j][k]
        for i in range(k + 1, PANEL):
            y[i] = y[i] - unit[i][k] * y[k]
    v = [recip[i] * y[i] for i in range(PANEL)]
    for j in reversed(range(PANEL)):
        for i in range(j):
            v[i] = v[i] - unit[j][i] * v[j]
    for i in range(PANEL):
        rows[i * SUBS:(i + 1) * SUBS, :] = v[i]
    for s in range(tiles):
        vpad[pl.ds(off, PANEL), s * LANES:(s + 1) * LANES] = rows[pl.ds(s, PANEL, stride=SUBS), :]
    for i in range(PANEL):
        rows[i * SUBS:(i + 1) * SUBS, :] = jnp.sqrt(recip[i]) * y[i]
    zero = jnp.zeros((PANEL, LANES), jnp.float32)
    for s in range(tiles):
        span = slice(s * LANES, (s + 1) * LANES)
        part = rows[pl.ds(s, PANEL, stride=SUBS), :]
        if s == tile:
            whole = rows[pl.ds(tiles, PANEL, stride=SUBS), :]
            f_ref[here, span] = jnp.where(lane >= off + sub, whole, 0.0)
            x_ref[here, span] = jnp.where(lane <= off + sub, part, 0.0)
        else:
            f_ref[here, span] = part if s > tile else zero
            x_ref[here, span] = part if s < tile else zero
    low = tile * LANES
    order = t_ref.shape[0]
    update = jnp.dot(
        t_ref[low:, low:low + LANES],
        vpad[...],
        precision=lax.Precision.HIGHEST,
        preferred_element_type=jnp.float32,
    )
    row_id = lax.broadcasted_iota(jnp.int32, (order - low, LANES), 0) + low
    lane_id = lax.broadcasted_iota(jnp.int32, (order - low, LANES), 1)
    below = row_id >= first + PANEL
    mine = (lane_id >= off) & (lane_id < off + PANEL)
    for s in range(tiles):
        span = slice(s * LANES, (s + 1) * LANES)
        held = t_ref[low:, span]
        base = jnp.where(mine, 0.0, held) if s == tile else held
        t_ref[low:, span] = jnp.where(below, base - update[:, span], held)
    vpad[pl.ds(off, PANEL), :] = jnp.zeros((PANEL, order), jnp.float32)


def factor_kernel(scale, gram_ref, f_ref, high_ref, low_ref, t_ref, x_ref, cols, rows, vpad):
    order = gram_ref.shape[0]
    tiles = order // LANES
    t_ref[...] = gram_ref[...] * scale
    vpad[...] = jnp.zeros(vpad.shape, jnp.float32)
    per_tile = LANES // PANEL
    rows[...] = jnp.zeros(rows.shape, jnp.float32)
    for tile in range(tiles):
        @pl.loop(tile * per_tile, (tile + 1) * per_tile)
        def _(panel):
            factor_panel(tile, tiles, panel, t_ref, f_ref, x_ref, cols, rows, vpad)
    whole = x_ref[...]
    high = whole.astype(jnp.bfloat16)
    high_ref[...] = high
    low_ref[...] = (whole - high.astype(jnp.float32)).astype(jnp.bfloat16)


def factor_and_inverse(gram_sum, cell_total):
    order = gram_sum.shape[0]
    square = (order, order)
    return pl.pallas_call(
        lambda *refs: factor_kernel(1.0 / cell_total, *refs),
        out_shape=[
            jax.ShapeDtypeStruct(square, jnp.float32),
            jax.ShapeDtypeStruct(square, jnp.bfloat16),
            jax.ShapeDtypeStruct(square, jnp.bfloat16),
        ],
        scratch_shapes=[
            pltpu.VMEM(square, jnp.float32),
            pltpu.VMEM(square, jnp.float32),
            pltpu.VMEM((PANEL, PANEL, LANES), jnp.float32),
            pltpu.VMEM((PANEL * SUBS, LANES), jnp.float32),
            pltpu.VMEM((LANES, order), jnp.float32),
        ],
        compiler_params=pltpu.CompilerParams(vmem_limit_bytes=32 * 1024 * 1024),
        name="factor",
    )(gram_sum)


def shards(snapshots, old_modes, mode_scales, plane_counts, links):
    new_count, plane_slots, rows_y, rows_z = snapshots.shape
    keep_count = old_modes.shape[0]
    columns = new_count + keep_count
    plane_count = plane_counts[0]
    plane_ids = lax.iota(jnp.int32, plane_slots)
    alive_mask = (plane_ids < plane_count).astype(jnp.float32)[None, :, None, None]
    last_pick = (plane_ids == plane_count - 1).astype(jnp.float32)[None, :, None, None]
    masked = snapshots.astype(jnp.float32) * alive_mask
    first_plane = masked[:, 0]
    last_plane = jnp.sum(masked * last_pick, axis=1)
    edge_planes = jnp.stack([first_plane, last_plane], axis=1).astype(jnp.bfloat16)
    widened = with_halo(edge_planes, (("blk", 1),), 1)
    left_halo = widened[:, 0].astype(jnp.float32) * links[0, 0].astype(jnp.float32)
    right_halo = widened[:, 3].astype(jnp.float32) * links[0, 1].astype(jnp.float32)
    behind = jnp.concatenate([left_halo[:, None], masked[:, :-1]], axis=1)
    forward = jnp.concatenate([masked[:, 1:], jnp.zeros_like(masked[:, :1])], axis=1)
    forward = forward + last_pick * right_halo[:, None]
    along_planes = 0.25 * behind + 0.5 * masked + 0.25 * forward
    filtered = (smooth_along(smooth_along(along_planes, 2), 3) * alive_mask).astype(jnp.bfloat16)
    scaled = (mode_scales[:, None, None, None] * old_modes.astype(jnp.float32) * alive_mask).astype(
        jnp.bfloat16
    )
    stacked = jnp.concatenate([filtered, scaled], axis=0).reshape(
        columns, plane_slots * rows_y * rows_z
    )
    cell_total = lax.axis_size("blk") * stacked.shape[1]
    local_gram = gram_term(stacked, stacked)
    gram_sum = lax.psum(local_gram, "blk")
    factor, inverse_high, inverse_low = factor_and_inverse(gram_sum, cell_total)
    result = jnp.dot(inverse_high, stacked, preferred_element_type=jnp.float32)
    result = result + jnp.dot(inverse_low, stacked, preferred_element_type=jnp.float32)
    return (result.reshape(columns, plane_slots, rows_y, rows_z).astype(jnp.bfloat16), factor)


def solution(mesh):
    return jax.shard_map(
        shards,
        mesh=mesh,
        in_specs=(
            P(None, ("groups", "blk"), None, None),
            P(None, ("groups", "blk"), None, None),
            P("groups"),
            P(("groups", "blk")),
            P(("groups", "blk"), None),
        ),
        out_specs=(P(None, ("groups", "blk"), None, None), P("groups", None)),
        check_vma=False,
    )
```

```python
import jax
import jax.numpy as jnp
from jax import lax
from jax.experimental import pallas as pl
from jax.experimental.pallas import tpu as pltpu
from jax.sharding import PartitionSpec as P

PANEL = 16
LANES = 128
SUBS = 8


def with_halo(x, sides, width):
    for axis, dim in sides:
        peers, length = (lax.axis_size(axis), x.shape[dim])
        up = [(i, (i + 1) % peers) for i in range(peers)]
        down = [(j, i) for i, j in up]
        last = lax.slice_in_dim(x, length - width, length, axis=dim)
        leading = lax.slice_in_dim(x, 0, width, axis=dim)
        before = lax.ppermute(last, axis, up)
        after = lax.ppermute(leading, axis, down)
        x = jnp.concatenate([before, x, after], axis=dim)
    return x


def smooth_along(field, along):
    widths = [(0, 0)] * field.ndim
    widths[along] = (1, 1)
    padded = jnp.pad(field, widths)
    length = field.shape[along]
    lower = lax.slice_in_dim(padded, 0, length, axis=along)
    upper = lax.slice_in_dim(padded, 2, length + 2, axis=along)
    return 0.25 * lower + 0.5 * field + 0.25 * upper


def gram_term(left_rows, right_rows):
    return lax.dot_general(
        left_rows, right_rows, (((1,), (1,)), ((), ())), preferred_element_type=jnp.float32
    )


def sum_over(matrix, axis):
    peers = lax.axis_size(axis)
    order = matrix.shape[0]
    chunks = matrix.reshape(peers, order // peers, order)
    arrived = lax.all_to_all(chunks, axis, 0, 0)
    own = jnp.sum(arrived, axis=0, keepdims=True)
    sums = lax.all_to_all(jnp.broadcast_to(own, chunks.shape), axis, 0, 0)
    return sums.reshape(order, order)


def factor_panel(tile, tiles, panel, t_ref, f_ref, x_ref, cols, rows, vpad):
    first = pl.multiple_of(panel * PANEL, PANEL)
    off = pl.multiple_of(first - tile * LANES, PANEL)
    here = pl.ds(first, PANEL)
    lane = lax.broadcasted_iota(jnp.int32, (PANEL, LANES), 1)
    sub = lax.broadcasted_iota(jnp.int32, (PANEL, LANES), 0)
    inside = (lane >= off) & (lane < off + PANEL)
    own = t_ref[here, tile * LANES:(tile + 1) * LANES]
    for s in range(tiles):
        if s == tile:
            block = jnp.where(inside, jnp.where(lane - off == sub, 1.0, 0.0), own)
        else:
            block = t_ref[here, s * LANES:(s + 1) * LANES]
        rows[pl.ds(s, PANEL, stride=SUBS), :] = block
    rows[pl.ds(tiles, PANEL, stride=SUBS), :] = own
    turned = pltpu.roll(own, lax.rem(LANES - off, LANES), axis=1)
    for j in range(PANEL):
        cols[j] = jnp.broadcast_to(turned[:, j:j + 1], (PANEL, LANES))
    entry = [
        [jnp.broadcast_to(cols[j, i:i + 1, :], (SUBS, LANES)) for j in range(i + 1)]
        for i in range(PANEL)
    ]
    y = [rows[i * SUBS:(i + 1) * SUBS, :] for i in range(PANEL)]
    unit = [[None] * PANEL for _ in range(PANEL)]
    recip = []
    for k in range(PANEL):
        recip.append(1.0 / entry[k][k])
        for i in range(k + 1, PANEL):
            unit[i][k] = entry[i][k] * recip[k]
        for j in range(k + 1, PANEL):
            for i in range(j, PANEL):
                entry[i][j] = entry[i][j] - unit[i][k] * entry[j][k]
        for i in range(k + 1, PANEL):
            y[i] = y[i] - unit[i][k] * y[k]
    v = [recip[i] * y[i] for i in range(PANEL)]
    for j in reversed(range(PANEL)):
        for i in range(j):
            v[i] = v[i] - unit[j][i] * v[j]
    for i in range(PANEL):
        rows[i * SUBS:(i + 1) * SUBS, :] = v[i]
    for s in range(tiles):
        vpad[pl.ds(off, PANEL), s * LANES:(s + 1) * LANES] = rows[pl.ds(s, PANEL, stride=SUBS), :]
    for i in range(PANEL):
        rows[i * SUBS:(i + 1) * SUBS, :] = jnp.sqrt(recip[i]) * y[i]
    zero = jnp.zeros((PANEL, LANES), jnp.float32)
    for s in range(tiles):
        span = slice(s * LANES, (s + 1) * LANES)
        part = rows[pl.ds(s, PANEL, stride=SUBS), :]
        if s == tile:
            whole = rows[pl.ds(tiles, PANEL, stride=SUBS), :]
            f_ref[here, span] = jnp.where(lane >= off + sub, whole, 0.0)
            x_ref[here, span] = jnp.where(lane <= off + sub, part, 0.0)
        else:
            f_ref[here, span] = part if s > tile else zero
            x_ref[here, span] = part if s < tile else zero
    low = tile * LANES
    order = t_ref.shape[0]
    update = jnp.dot(
        t_ref[low:, low:low + LANES],
        vpad[...],
        precision=lax.Precision.HIGHEST,
        preferred_element_type=jnp.float32,
    )
    row_id = lax.broadcasted_iota(jnp.int32, (order - low, LANES), 0) + low
    lane_id = lax.broadcasted_iota(jnp.int32, (order - low, LANES), 1)
    below = row_id >= first + PANEL
    mine = (lane_id >= off) & (lane_id < off + PANEL)
    for s in range(tiles):
        span = slice(s * LANES, (s + 1) * LANES)
        held = t_ref[low:, span]
        base = jnp.where(mine, 0.0, held) if s == tile else held
        t_ref[low:, span] = jnp.where(below, base - update[:, span], held)
    vpad[pl.ds(off, PANEL), :] = jnp.zeros((PANEL, order), jnp.float32)


def factor_kernel(scale, gram_ref, f_ref, high_ref, low_ref, t_ref, x_ref, cols, rows, vpad):
    order = gram_ref.shape[0]
    tiles = order // LANES
    t_ref[...] = gram_ref[...] * scale
    vpad[...] = jnp.zeros(vpad.shape, jnp.float32)
    per_tile = LANES // PANEL
    rows[...] = jnp.zeros(rows.shape, jnp.float32)
    for tile in range(tiles):
        @pl.loop(tile * per_tile, (tile + 1) * per_tile)
        def _(panel):
            factor_panel(tile, tiles, panel, t_ref, f_ref, x_ref, cols, rows, vpad)
    whole = x_ref[...]
    high = whole.astype(jnp.bfloat16)
    high_ref[...] = high
    low_ref[...] = (whole - high.astype(jnp.float32)).astype(jnp.bfloat16)


def factor_and_inverse(gram_sum, cell_total):
    order = gram_sum.shape[0]
    square = (order, order)
    return pl.pallas_call(
        lambda *refs: factor_kernel(1.0 / cell_total, *refs),
        out_shape=[
            jax.ShapeDtypeStruct(square, jnp.float32),
            jax.ShapeDtypeStruct(square, jnp.bfloat16),
            jax.ShapeDtypeStruct(square, jnp.bfloat16),
        ],
        scratch_shapes=[
            pltpu.VMEM(square, jnp.float32),
            pltpu.VMEM(square, jnp.float32),
            pltpu.VMEM((PANEL, PANEL, LANES), jnp.float32),
            pltpu.VMEM((PANEL * SUBS, LANES), jnp.float32),
            pltpu.VMEM((LANES, order), jnp.float32),
        ],
        compiler_params=pltpu.CompilerParams(vmem_limit_bytes=32 * 1024 * 1024),
        name="factor",
    )(gram_sum)


def shards(snapshots, old_modes, mode_scales, plane_counts, links):
    new_count, plane_slots, rows_y, rows_z = snapshots.shape
    keep_count = old_modes.shape[0]
    columns = new_count + keep_count
    plane_count = plane_counts[0]
    plane_ids = lax.iota(jnp.int32, plane_slots)
    alive_mask = (plane_ids < plane_count).astype(jnp.float32)[None, :, None, None]
    last_pick = (plane_ids == plane_count - 1).astype(jnp.float32)[None, :, None, None]
    masked = snapshots.astype(jnp.float32) * alive_mask
    first_plane = masked[:, 0]
    last_plane = jnp.sum(masked * last_pick, axis=1)
    edge_planes = jnp.stack([first_plane, last_plane], axis=1).astype(jnp.bfloat16)
    widened = with_halo(edge_planes, (("blk", 1),), 1)
    left_halo = widened[:, 0].astype(jnp.float32) * links[0, 0].astype(jnp.float32)
    right_halo = widened[:, 3].astype(jnp.float32) * links[0, 1].astype(jnp.float32)
    behind = jnp.concatenate([left_halo[:, None], masked[:, :-1]], axis=1)
    forward = jnp.concatenate([masked[:, 1:], jnp.zeros_like(masked[:, :1])], axis=1)
    forward = forward + last_pick * right_halo[:, None]
    along_planes = 0.25 * behind + 0.5 * masked + 0.25 * forward
    filtered = (smooth_along(smooth_along(along_planes, 2), 3) * alive_mask).astype(jnp.bfloat16)
    scaled = (mode_scales[:, None, None, None] * old_modes.astype(jnp.float32) * alive_mask).astype(
        jnp.bfloat16
    )
    stacked = jnp.concatenate([filtered, scaled], axis=0).reshape(
        columns, plane_slots * rows_y * rows_z
    )
    cell_total = lax.axis_size("blk") * stacked.shape[1]
    local_gram = gram_term(stacked, stacked)
    gram_sum = sum_over(local_gram, "blk")
    factor, inverse_high, inverse_low = factor_and_inverse(gram_sum, cell_total)
    result = jnp.dot(inverse_high, stacked, preferred_element_type=jnp.float32)
    result = result + jnp.dot(inverse_low, stacked, preferred_element_type=jnp.float32)
    return (result.reshape(columns, plane_slots, rows_y, rows_z).astype(jnp.bfloat16), factor)


def solution(mesh):
    return jax.shard_map(
        shards,
        mesh=mesh,
        in_specs=(
            P(None, ("groups", "blk"), None, None),
            P(None, ("groups", "blk"), None, None),
            P("groups"),
            P(("groups", "blk")),
            P(("groups", "blk"), None),
        ),
        out_specs=(P(None, ("groups", "blk"), None, None), P("groups", None)),
        check_vma=False,
    )
```

```python
import functools

import jax
import jax.numpy as jnp
from jax import lax
from jax.experimental import pallas as pl
from jax.experimental.pallas import tpu as pltpu
from jax.sharding import PartitionSpec as P

PANEL = 16
LANES = 128
SUBS = 8
SPREAD = 4
VMEM_BYTES = 40 * 1024 * 1024


def nt_dot(left_rows, right_rows):
    return lax.dot_general(
        left_rows, right_rows, (((1,), (1,)), ((), ())), preferred_element_type=jnp.float32
    )


def swap(x, axis, flip):
    peers = lax.axis_size(axis)
    return lax.ppermute(x, axis, [(i, i ^ flip) for i in range(peers)])


def relay(tall, s_ref, plane, rows_y):
    rows = s_ref.shape[0]
    for y in range(rows_y):
        column = (plane * rows_y + y) * LANES
        part = tall[pl.ds(y, rows, stride=rows_y), :]
        s_ref[:, column:column + LANES] = part.astype(jnp.bfloat16)


def scale_kernel(scales_ref, count_ref, old_ref, s_ref, gram_ref, tall):
    rows, planes, rows_y, _ = old_ref.shape
    for plane in range(planes):
        alive = jnp.where(plane < count_ref[0], 1.0, 0.0)

        @pl.loop(0, rows, unroll=8)
        def _(row):
            weight = scales_ref[row]
            at = pl.multiple_of(row * rows_y, rows_y)
            tall[pl.ds(at, rows_y), :] = old_ref[row, plane].astype(jnp.float32) * weight * alive

        relay(tall, s_ref, plane, rows_y)
    gram_ref[...] = nt_dot(s_ref[...], s_ref[...])


def scaled_rows(old_modes, mode_scales, plane_counts):
    rows, planes, rows_y, rows_z = old_modes.shape
    cells = planes * rows_y * rows_z
    smem = pl.BlockSpec(memory_space=pltpu.SMEM)
    vmem = pl.BlockSpec(memory_space=pltpu.VMEM)
    return pl.pallas_call(
        scale_kernel,
        out_shape=[
            jax.ShapeDtypeStruct((rows, cells), jnp.bfloat16),
            jax.ShapeDtypeStruct((rows, rows), jnp.float32),
        ],
        in_specs=[smem, smem, vmem],
        out_specs=[vmem, vmem],
        scratch_shapes=[pltpu.VMEM((rows * rows_y, rows_z), jnp.float32)],
        compiler_params=pltpu.CompilerParams(vmem_limit_bytes=VMEM_BYTES),
        cost_estimate=pl.CostEstimate(
            flops=2 * rows * rows * cells, bytes_accessed=8 * rows * cells, transcendentals=0
        ),
        name="scale_gram",
    )(mode_scales, plane_counts, old_modes)


def smooth(field, axis, place, length):
    lower = jnp.where(place == 0, 0.0, pltpu.roll(field, 1, axis=axis))
    upper = jnp.where(place == length - 1, 0.0, pltpu.roll(field, length - 1, axis=axis))
    return 0.25 * lower + 0.5 * field + 0.25 * upper


def packed_rows(order):
    chunk = -(-(order + SUBS) // (SPREAD * SUBS)) * SUBS
    return SPREAD * chunk


def filter_kernel(
    count_ref, links_ref, snap_ref, before_ref, after_ref, old_ref, oldgram_ref, s_ref, *rest
):
    chunk_refs, (tall, packed) = rest[:SPREAD], rest[SPREAD:]
    rows, planes, rows_y, rows_z = snap_ref.shape
    count = count_ref[0]
    join_low = links_ref[0, 0].astype(jnp.float32)
    join_high = links_ref[0, 1].astype(jnp.float32)
    place_y = lax.broadcasted_iota(jnp.int32, (rows_y, rows_z), 0)
    place_z = lax.broadcasted_iota(jnp.int32, (rows_y, rows_z), 1)
    for plane in range(planes):
        alive = jnp.where(plane < count, 1.0, 0.0)
        is_last = plane == count - 1

        @pl.loop(0, rows, unroll=8)
        def _(row):
            own = snap_ref[row, plane].astype(jnp.float32)
            if plane == 0:
                behind = before_ref[row, 0].astype(jnp.float32) * join_low
            else:
                behind = snap_ref[row, plane - 1].astype(jnp.float32)
            forward = after_ref[row, 0].astype(jnp.float32) * join_high
            if plane < planes - 1:
                forward = jnp.where(is_last, forward, snap_ref[row, plane + 1].astype(jnp.float32))
            field = 0.25 * behind + 0.5 * own + 0.25 * forward
            field = smooth(smooth(field, 0, place_y, rows_y), 1, place_z, rows_z) * alive
            at = pl.multiple_of(row * rows_y, rows_y)
            tall[pl.ds(at, rows_y), :] = field

        relay(tall, s_ref, plane, rows_y)
    fresh = s_ref[...]
    new_new = nt_dot(fresh, fresh)
    new_old = nt_dot(fresh, old_ref[...])
    split = LANES - rows
    old_old = oldgram_ref[...]
    top = jnp.concatenate([new_new, new_old[:, :split]], axis=1)
    hidden = jnp.zeros((split, rows), jnp.float32)
    middle = jnp.concatenate([hidden, old_old[:split, :split]], axis=1)
    upper_left = jnp.concatenate([top, middle], axis=0)
    upper_right = jnp.concatenate([new_old[:, split:], old_old[:split, split:]], axis=0)
    lower_right = old_old[split:, split:]
    i = lax.broadcasted_iota(jnp.int32, (LANES, LANES), 0)
    j = lax.broadcasted_iota(jnp.int32, (LANES, LANES), 1)
    packed[:LANES, :] = jnp.where(j >= i, upper_left, lower_right)
    packed[LANES:2 * LANES, :] = upper_right
    packed[2 * LANES:, :] = jnp.zeros((packed.shape[0] - 2 * LANES, LANES), jnp.float32)
    packed[2 * LANES:2 * LANES + 1, :] = jnp.sum(
        jnp.where(i == j, lower_right, 0.0), axis=0, keepdims=True
    )
    share = lax.axis_index("blk") % SPREAD
    height = packed.shape[0] // SPREAD
    for flip in range(SPREAD):
        at = pl.multiple_of((share ^ flip) * height, SUBS)
        chunk_refs[flip][...] = packed[pl.ds(at, height), :]


def filtered_rows(snapshots, before, after, plane_counts, links, s_old, old_gram):
    rows, planes, rows_y, rows_z = snapshots.shape
    cells = planes * rows_y * rows_z
    order = rows + s_old.shape[0]
    height = packed_rows(order)
    smem = pl.BlockSpec(memory_space=pltpu.SMEM)
    vmem = pl.BlockSpec(memory_space=pltpu.VMEM)
    chunk = jax.ShapeDtypeStruct((height // SPREAD, LANES), jnp.float32)
    return pl.pallas_call(
        filter_kernel,
        out_shape=[jax.ShapeDtypeStruct((rows, cells), jnp.bfloat16)] + [chunk] * SPREAD,
        in_specs=[smem, smem] + [vmem] * 5,
        out_specs=[vmem] * (1 + SPREAD),
        scratch_shapes=[
            pltpu.VMEM((rows * rows_y, rows_z), jnp.float32),
            pltpu.VMEM((height, LANES), jnp.float32),
        ],
        compiler_params=pltpu.CompilerParams(vmem_limit_bytes=VMEM_BYTES),
        cost_estimate=pl.CostEstimate(
            flops=2 * rows * order * cells, bytes_accessed=2 * order * cells, transcendentals=0
        ),
        name="filter_gram",
    )(plane_counts, links, snapshots, before, after, s_old, old_gram)


def sum_chunks(chunks, axis):
    peers = lax.axis_size(axis)
    arrived = [chunks[0]] + [swap(chunks[d], axis, d) for d in range(1, SPREAD)]
    total = (arrived[0] + arrived[1]) + (arrived[2] + arrived[3])
    step = SPREAD
    while step < peers:
        if step * 4 <= peers:
            one, two, three = (swap(total, axis, d * step) for d in (1, 2, 3))
            total = (total + one) + (two + three)
            step *= 4
        else:
            total = total + swap(total, axis, step)
            step *= 2
    return [total] + [swap(total, axis, d) for d in range(1, SPREAD)]


def factor_panel(tile, tiles, panel, t_ref, f_ref, x_ref, cols, rows, vpad):
    first = pl.multiple_of(panel * PANEL, PANEL)
    off = pl.multiple_of(first - tile * LANES, PANEL)
    here = pl.ds(first, PANEL)
    lane = lax.broadcasted_iota(jnp.int32, (PANEL, LANES), 1)
    sub = lax.broadcasted_iota(jnp.int32, (PANEL, LANES), 0)
    inside = (lane >= off) & (lane < off + PANEL)
    own = t_ref[here, tile * LANES:(tile + 1) * LANES]
    for s in range(tiles):
        if s == tile:
            block = jnp.where(inside, jnp.where(lane - off == sub, 1.0, 0.0), own)
        else:
            block = t_ref[here, s * LANES:(s + 1) * LANES]
        rows[pl.ds(s, PANEL, stride=SUBS), :] = block
    rows[pl.ds(tiles, PANEL, stride=SUBS), :] = own
    turned = pltpu.roll(own, lax.rem(LANES - off, LANES), axis=1)
    for j in range(PANEL):
        cols[j] = jnp.broadcast_to(turned[:, j:j + 1], (PANEL, LANES))
    entry = [
        [jnp.broadcast_to(cols[j, i:i + 1, :], (SUBS, LANES)) for j in range(i + 1)]
        for i in range(PANEL)
    ]
    y = [rows[i * SUBS:(i + 1) * SUBS, :] for i in range(PANEL)]
    unit = [[None] * PANEL for _ in range(PANEL)]
    recip = []
    for k in range(PANEL):
        recip.append(1.0 / entry[k][k])
        for i in range(k + 1, PANEL):
            unit[i][k] = entry[i][k] * recip[k]
        for j in range(k + 1, PANEL):
            for i in range(j, PANEL):
                entry[i][j] = entry[i][j] - unit[i][k] * entry[j][k]
        for i in range(k + 1, PANEL):
            y[i] = y[i] - unit[i][k] * y[k]
    v = [recip[i] * y[i] for i in range(PANEL)]
    for j in reversed(range(PANEL)):
        for i in range(j):
            v[i] = v[i] - unit[j][i] * v[j]
    for i in range(PANEL):
        rows[i * SUBS:(i + 1) * SUBS, :] = v[i]
    for s in range(tiles):
        vpad[pl.ds(off, PANEL), s * LANES:(s + 1) * LANES] = rows[pl.ds(s, PANEL, stride=SUBS), :]
    for i in range(PANEL):
        rows[i * SUBS:(i + 1) * SUBS, :] = jnp.sqrt(recip[i]) * y[i]
    zero = jnp.zeros((PANEL, LANES), jnp.float32)
    for s in range(tiles):
        span = slice(s * LANES, (s + 1) * LANES)
        part = rows[pl.ds(s, PANEL, stride=SUBS), :]
        if s == tile:
            whole = rows[pl.ds(tiles, PANEL, stride=SUBS), :]
            f_ref[here, span] = jnp.where(lane >= off + sub, whole, 0.0)
            x_ref[here, span] = jnp.where(lane <= off + sub, part, 0.0)
        else:
            f_ref[here, span] = part if s > tile else zero
            x_ref[here, span] = part if s < tile else zero
    low = tile * LANES
    order = t_ref.shape[0]
    update = jnp.dot(
        t_ref[low:, low:low + LANES],
        vpad[...],
        precision=lax.Precision.HIGHEST,
        preferred_element_type=jnp.float32,
    )
    row_id = lax.broadcasted_iota(jnp.int32, (order - low, LANES), 0) + low
    lane_id = lax.broadcasted_iota(jnp.int32, (order - low, LANES), 1)
    below = row_id >= first + PANEL
    mine = (lane_id >= off) & (lane_id < off + PANEL)
    for s in range(tiles):
        span = slice(s * LANES, (s + 1) * LANES)
        held = t_ref[low:, span]
        base = jnp.where(mine, 0.0, held) if s == tile else held
        t_ref[low:, span] = jnp.where(below, base - update[:, span], held)
    vpad[pl.ds(off, PANEL), :] = jnp.zeros((PANEL, order), jnp.float32)


def factor_kernel(scale, *refs):
    chunk_refs, refs = refs[:SPREAD], refs[SPREAD:]
    new_ref, old_ref, f_ref, out_ref, refs = *refs[:4], refs[4:]
    packed, t_ref, x_ref, cols, rows, vpad, stack, tall, staged, in_sem, out_sem = refs
    order = t_ref.shape[0]
    tiles = order // LANES
    new_count = new_ref.shape[0]
    load_new = pltpu.make_async_copy(new_ref, stack.at[pl.ds(0, new_count)], in_sem.at[0])
    load_old = pltpu.make_async_copy(
        old_ref, stack.at[pl.ds(new_count, order - new_count)], in_sem.at[1]
    )
    load_new.start()
    load_old.start()
    share = lax.axis_index("blk") % SPREAD
    height = packed.shape[0] // SPREAD
    for flip in range(SPREAD):
        at = pl.multiple_of((share ^ flip) * height, SUBS)
        packed[pl.ds(at, height), :] = chunk_refs[flip][...] * scale
    i = lax.broadcasted_iota(jnp.int32, (LANES, LANES), 0)
    j = lax.broadcasted_iota(jnp.int32, (LANES, LANES), 1)
    shared = packed[:LANES, :]
    right = packed[LANES:2 * LANES, :]
    upper = jnp.where(j >= i, shared, 0.0)
    lower = jnp.where(j < i, shared, 0.0)
    diagonal = packed[2 * LANES:2 * LANES + 1, :]
    t_ref[:LANES, :LANES] = jnp.where(j >= i, shared, upper.T)
    t_ref[:LANES, LANES:] = right
    t_ref[LANES:, :LANES] = right.T
    corner = jnp.where(j < i, shared, lower.T)
    t_ref[LANES:, LANES:] = jnp.where(i == j, diagonal, corner)
    vpad[...] = jnp.zeros(vpad.shape, jnp.float32)
    rows[...] = jnp.zeros(rows.shape, jnp.float32)
    per_tile = LANES // PANEL
    for tile in range(tiles):
        @pl.loop(tile * per_tile, (tile + 1) * per_tile)
        def _(panel):
            factor_panel(tile, tiles, panel, t_ref, f_ref, x_ref, cols, rows, vpad)
    inverse = x_ref[...]
    high = inverse.astype(jnp.bfloat16)
    low = (inverse - high.astype(jnp.float32)).astype(jnp.bfloat16)
    load_new.wait()
    load_old.wait()
    _, planes, rows_y, rows_z = out_ref.shape
    stores = []
    for plane in range(planes):
        for pair in range(0, rows_y, 2):
            column = (plane * rows_y + pair) * LANES
            block = stack[:, column:column + 2 * LANES]
            sums = jnp.dot(high, block, preferred_element_type=jnp.float32)
            sums = sums + jnp.dot(low, block, preferred_element_type=jnp.float32)
            for y in (0, 1):
                tall[pl.ds(pair + y, order, stride=rows_y), :] = sums[:, y * LANES:(y + 1) * LANES]

        @pl.loop(0, order, unroll=8)
        def _(row):
            at = pl.multiple_of(row * rows_y, rows_y)
            staged[plane, row] = tall[pl.ds(at, rows_y), :].astype(jnp.bfloat16)

        store = pltpu.make_async_copy(staged.at[plane], out_ref.at[:, plane], out_sem.at[plane])
        store.start()
        stores.append(store)
    for store in stores:
        store.wait()


def factor_and_modes(chunks, s_new, s_old, shape, cell_total):
    order, planes, rows_y, rows_z = shape
    height = chunks[0].shape[0] * SPREAD
    vmem = pl.BlockSpec(memory_space=pltpu.VMEM)
    hbm = pl.BlockSpec(memory_space=pl.ANY)
    square = (order, order)
    return pl.pallas_call(
        functools.partial(factor_kernel, 1.0 / cell_total),
        out_shape=[
            jax.ShapeDtypeStruct(square, jnp.float32),
            jax.ShapeDtypeStruct(shape, jnp.bfloat16),
        ],
        in_specs=[vmem] * SPREAD + [hbm, hbm],
        out_specs=[vmem, hbm],
        scratch_shapes=[
            pltpu.VMEM((height, LANES), jnp.float32),
            pltpu.VMEM(square, jnp.float32),
            pltpu.VMEM(square, jnp.float32),
            pltpu.VMEM((PANEL, PANEL, LANES), jnp.float32),
            pltpu.VMEM((PANEL * SUBS, LANES), jnp.float32),
            pltpu.VMEM((LANES, order), jnp.float32),
            pltpu.VMEM((order, planes * rows_y * rows_z), jnp.bfloat16),
            pltpu.VMEM((order * rows_y, rows_z), jnp.float32),
            pltpu.VMEM((planes, order, rows_y, rows_z), jnp.bfloat16),
            pltpu.SemaphoreType.DMA((2,)),
            pltpu.SemaphoreType.DMA((planes,)),
        ],
        compiler_params=pltpu.CompilerParams(vmem_limit_bytes=VMEM_BYTES),
        name="factor",
    )(*chunks, s_new, s_old)


def shards(snapshots, old_modes, mode_scales, plane_counts, links):
    new_count, planes, rows_y, rows_z = snapshots.shape
    order = new_count + old_modes.shape[0]
    peers = lax.axis_size("blk")
    up = [(i, (i + 1) % peers) for i in range(peers)]
    down = [(j, i) for i, j in up]
    first = lax.slice_in_dim(snapshots, 0, 1, axis=1)
    last = lax.dynamic_slice_in_dim(snapshots, plane_counts[0] - 1, 1, axis=1)
    after = lax.ppermute(first, "blk", down)
    before = lax.ppermute(last, "blk", up)
    s_old, old_gram = scaled_rows(old_modes, mode_scales, plane_counts)
    s_new, *chunks = filtered_rows(
        snapshots, before, after, plane_counts, links, s_old, old_gram
    )
    sums = sum_chunks(chunks, "blk")
    factor, modes = factor_and_modes(
        sums, s_new, s_old, (order, planes, rows_y, rows_z), peers * planes * rows_y * rows_z
    )
    return (modes, factor)


def solution(mesh):
    return jax.shard_map(
        shards,
        mesh=mesh,
        in_specs=(
            P(None, ("groups", "blk"), None, None),
            P(None, ("groups", "blk"), None, None),
            P("groups"),
            P(("groups", "blk")),
            P(("groups", "blk"), None),
        ),
        out_specs=(P(None, ("groups", "blk"), None, None), P("groups", None)),
        check_vma=False,
    )
```

```python
import functools

import jax
import jax.numpy as jnp
from jax import lax
from jax.experimental import pallas as pl
from jax.experimental.pallas import tpu as pltpu
from jax.sharding import PartitionSpec as P

PANEL = 16
LANES = 128
SUBS = 8
SPREAD = 4
VMEM_BYTES = 40 * 1024 * 1024


def nt_dot(left_rows, right_rows):
    return lax.dot_general(
        left_rows, right_rows, (((1,), (1,)), ((), ())), preferred_element_type=jnp.float32
    )


def relay(tall, s_ref, plane, rows_y):
    rows = s_ref.shape[0]
    for y in range(rows_y):
        column = (plane * rows_y + y) * LANES
        part = tall[pl.ds(y, rows, stride=rows_y), :]
        s_ref[:, column:column + LANES] = part.astype(jnp.bfloat16)


def scale_kernel(scales_ref, count_ref, old_ref, s_ref, gram_ref, tall):
    rows, planes, rows_y, _ = old_ref.shape
    for plane in range(planes):
        alive = jnp.where(plane < count_ref[0], 1.0, 0.0)

        @pl.loop(0, rows, unroll=8)
        def _(row):
            weight = scales_ref[row]
            at = pl.multiple_of(row * rows_y, rows_y)
            tall[pl.ds(at, rows_y), :] = old_ref[row, plane].astype(jnp.float32) * weight * alive

        relay(tall, s_ref, plane, rows_y)
    gram_ref[...] = nt_dot(s_ref[...], s_ref[...])


def scaled_rows(old_modes, mode_scales, plane_counts):
    rows, planes, rows_y, rows_z = old_modes.shape
    cells = planes * rows_y * rows_z
    smem = pl.BlockSpec(memory_space=pltpu.SMEM)
    vmem = pl.BlockSpec(memory_space=pltpu.VMEM)
    return pl.pallas_call(
        scale_kernel,
        out_shape=[
            jax.ShapeDtypeStruct((rows, cells), jnp.bfloat16),
            jax.ShapeDtypeStruct((rows, rows), jnp.float32),
        ],
        in_specs=[smem, smem, vmem],
        out_specs=[vmem, vmem],
        scratch_shapes=[pltpu.VMEM((rows * rows_y, rows_z), jnp.float32)],
        compiler_params=pltpu.CompilerParams(vmem_limit_bytes=VMEM_BYTES),
        cost_estimate=pl.CostEstimate(
            flops=2 * rows * rows * cells, bytes_accessed=8 * rows * cells, transcendentals=0
        ),
        name="scale_gram",
    )(mode_scales, plane_counts, old_modes)


def smooth(field, axis, place, length):
    lower = jnp.where(place == 0, 0.0, pltpu.roll(field, 1, axis=axis))
    upper = jnp.where(place == length - 1, 0.0, pltpu.roll(field, length - 1, axis=axis))
    return 0.25 * lower + 0.5 * field + 0.25 * upper


def packed_rows(order):
    chunk = -(-(order + SUBS) // (SPREAD * SUBS)) * SUBS
    return SPREAD * chunk


def filter_kernel(
    count_ref, links_ref, snap_ref, before_ref, after_ref, old_ref, oldgram_ref, s_ref, *rest
):
    packed, tall = rest
    rows, planes, rows_y, rows_z = snap_ref.shape
    count = count_ref[0]
    join_low = links_ref[0, 0].astype(jnp.float32)
    join_high = links_ref[0, 1].astype(jnp.float32)
    place_y = lax.broadcasted_iota(jnp.int32, (rows_y, rows_z), 0)
    place_z = lax.broadcasted_iota(jnp.int32, (rows_y, rows_z), 1)
    for plane in range(planes):
        alive = jnp.where(plane < count, 1.0, 0.0)
        is_last = plane == count - 1

        @pl.loop(0, rows, unroll=8)
        def _(row):
            own = snap_ref[row, plane].astype(jnp.float32)
            if plane == 0:
                behind = before_ref[row, 0].astype(jnp.float32) * join_low
            else:
                behind = snap_ref[row, plane - 1].astype(jnp.float32)
            forward = after_ref[row, 0].astype(jnp.float32) * join_high
            if plane < planes - 1:
                forward = jnp.where(is_last, forward, snap_ref[row, plane + 1].astype(jnp.float32))
            field = 0.25 * behind + 0.5 * own + 0.25 * forward
            field = smooth(smooth(field, 0, place_y, rows_y), 1, place_z, rows_z) * alive
            at = pl.multiple_of(row * rows_y, rows_y)
            tall[pl.ds(at, rows_y), :] = field

        relay(tall, s_ref, plane, rows_y)
    fresh = s_ref[...]
    new_new = nt_dot(fresh, fresh)
    new_old = nt_dot(fresh, old_ref[...])
    split = LANES - rows
    old_old = oldgram_ref[...]
    top = jnp.concatenate([new_new, new_old[:, :split]], axis=1)
    hidden = jnp.zeros((split, rows), jnp.float32)
    middle = jnp.concatenate([hidden, old_old[:split, :split]], axis=1)
    upper_left = jnp.concatenate([top, middle], axis=0)
    upper_right = jnp.concatenate([new_old[:, split:], old_old[:split, split:]], axis=0)
    lower_right = old_old[split:, split:]
    i = lax.broadcasted_iota(jnp.int32, (LANES, LANES), 0)
    j = lax.broadcasted_iota(jnp.int32, (LANES, LANES), 1)
    packed[:LANES, :] = jnp.where(j >= i, upper_left, lower_right)
    packed[LANES:2 * LANES, :] = upper_right
    packed[2 * LANES:, :] = jnp.zeros((packed.shape[0] - 2 * LANES, LANES), jnp.float32)
    packed[2 * LANES:2 * LANES + 1, :] = jnp.sum(
        jnp.where(i == j, lower_right, 0.0), axis=0, keepdims=True
    )


def filtered_rows(snapshots, before, after, plane_counts, links, s_old, old_gram):
    rows, planes, rows_y, rows_z = snapshots.shape
    cells = planes * rows_y * rows_z
    order = rows + s_old.shape[0]
    height = packed_rows(order)
    smem = pl.BlockSpec(memory_space=pltpu.SMEM)
    vmem = pl.BlockSpec(memory_space=pltpu.VMEM)
    return pl.pallas_call(
        filter_kernel,
        out_shape=[
            jax.ShapeDtypeStruct((rows, cells), jnp.bfloat16),
            jax.ShapeDtypeStruct((height, LANES), jnp.float32),
        ],
        in_specs=[smem, smem] + [vmem] * 5,
        out_specs=[vmem, vmem],
        scratch_shapes=[pltpu.VMEM((rows * rows_y, rows_z), jnp.float32)],
        compiler_params=pltpu.CompilerParams(vmem_limit_bytes=VMEM_BYTES),
        cost_estimate=pl.CostEstimate(
            flops=2 * rows * order * cells, bytes_accessed=2 * order * cells, transcendentals=0
        ),
        name="filter_gram",
    )(plane_counts, links, snapshots, before, after, s_old, old_gram)


def sum_over(packed, axis):
    peers = lax.axis_size(axis)
    near = [list(range(i, i + SPREAD)) for i in range(0, peers, SPREAD)]
    shares = packed.reshape(SPREAD, packed.shape[0] // SPREAD, LANES)
    arrived = lax.all_to_all(shares, axis, 0, 0, axis_index_groups=near)
    total = jnp.sum(arrived, axis=0)
    step = SPREAD
    while step < peers:
        width = min(SPREAD, peers // step)
        far = [
            [base + low + k * step for k in range(width)]
            for base in range(0, peers, step * width)
            for low in range(step)
        ]
        spread = jnp.broadcast_to(total[None], (width,) + total.shape)
        total = jnp.sum(lax.all_to_all(spread, axis, 0, 0, axis_index_groups=far), axis=0)
        step *= width
    spread = jnp.broadcast_to(total[None], (SPREAD,) + total.shape)
    sums = lax.all_to_all(spread, axis, 0, 0, axis_index_groups=near)
    return sums.reshape(packed.shape)


def factor_panel(tile, tiles, panel, t_ref, f_ref, x_ref, cols, rows, vpad):
    first = pl.multiple_of(panel * PANEL, PANEL)
    off = pl.multiple_of(first - tile * LANES, PANEL)
    here = pl.ds(first, PANEL)
    lane = lax.broadcasted_iota(jnp.int32, (PANEL, LANES), 1)
    sub = lax.broadcasted_iota(jnp.int32, (PANEL, LANES), 0)
    inside = (lane >= off) & (lane < off + PANEL)
    own = t_ref[here, tile * LANES:(tile + 1) * LANES]
    for s in range(tiles):
        if s == tile:
            block = jnp.where(inside, jnp.where(lane - off == sub, 1.0, 0.0), own)
        else:
            block = t_ref[here, s * LANES:(s + 1) * LANES]
        rows[pl.ds(s, PANEL, stride=SUBS), :] = block
    rows[pl.ds(tiles, PANEL, stride=SUBS), :] = own
    turned = pltpu.roll(own, lax.rem(LANES - off, LANES), axis=1)
    for j in range(PANEL):
        cols[j] = jnp.broadcast_to(turned[:, j:j + 1], (PANEL, LANES))
    entry = [
        [jnp.broadcast_to(cols[j, i:i + 1, :], (SUBS, LANES)) for j in range(i + 1)]
        for i in range(PANEL)
    ]
    y = [rows[i * SUBS:(i + 1) * SUBS, :] for i in range(PANEL)]
    unit = [[None] * PANEL for _ in range(PANEL)]
    recip = []
    for k in range(PANEL):
        recip.append(1.0 / entry[k][k])
        for i in range(k + 1, PANEL):
            unit[i][k] = entry[i][k] * recip[k]
        for j in range(k + 1, PANEL):
            for i in range(j, PANEL):
                entry[i][j] = entry[i][j] - unit[i][k] * entry[j][k]
        for i in range(k + 1, PANEL):
            y[i] = y[i] - unit[i][k] * y[k]
    v = [recip[i] * y[i] for i in range(PANEL)]
    for j in reversed(range(PANEL)):
        for i in range(j):
            v[i] = v[i] - unit[j][i] * v[j]
    for i in range(PANEL):
        rows[i * SUBS:(i + 1) * SUBS, :] = v[i]
    for s in range(tiles):
        vpad[pl.ds(off, PANEL), s * LANES:(s + 1) * LANES] = rows[pl.ds(s, PANEL, stride=SUBS), :]
    for i in range(PANEL):
        rows[i * SUBS:(i + 1) * SUBS, :] = jnp.sqrt(recip[i]) * y[i]
    zero = jnp.zeros((PANEL, LANES), jnp.float32)
    for s in range(tiles):
        span = slice(s * LANES, (s + 1) * LANES)
        part = rows[pl.ds(s, PANEL, stride=SUBS), :]
        if s == tile:
            whole = rows[pl.ds(tiles, PANEL, stride=SUBS), :]
            f_ref[here, span] = jnp.where(lane >= off + sub, whole, 0.0)
            x_ref[here, span] = jnp.where(lane <= off + sub, part, 0.0)
        else:
            f_ref[here, span] = part if s > tile else zero
            x_ref[here, span] = part if s < tile else zero
    low = tile * LANES
    order = t_ref.shape[0]
    update = jnp.dot(
        t_ref[low:, low:low + LANES],
        vpad[...],
        precision=lax.Precision.HIGHEST,
        preferred_element_type=jnp.float32,
    )
    row_id = lax.broadcasted_iota(jnp.int32, (order - low, LANES), 0) + low
    lane_id = lax.broadcasted_iota(jnp.int32, (order - low, LANES), 1)
    below = row_id >= first + PANEL
    mine = (lane_id >= off) & (lane_id < off + PANEL)
    for s in range(tiles):
        span = slice(s * LANES, (s + 1) * LANES)
        held = t_ref[low:, span]
        base = jnp.where(mine, 0.0, held) if s == tile else held
        t_ref[low:, span] = jnp.where(below, base - update[:, span], held)
    vpad[pl.ds(off, PANEL), :] = jnp.zeros((PANEL, order), jnp.float32)


def factor_kernel(scale, *refs):
    packed, new_ref, old_ref, f_ref, out_ref, *refs = refs
    t_ref, x_ref, cols, rows, vpad, stack, tall, staged, in_sem, out_sem = refs
    order = t_ref.shape[0]
    tiles = order // LANES
    new_count = new_ref.shape[0]
    load_new = pltpu.make_async_copy(new_ref, stack.at[pl.ds(0, new_count)], in_sem.at[0])
    load_old = pltpu.make_async_copy(
        old_ref, stack.at[pl.ds(new_count, order - new_count)], in_sem.at[1]
    )
    load_new.start()
    load_old.start()
    i = lax.broadcasted_iota(jnp.int32, (LANES, LANES), 0)
    j = lax.broadcasted_iota(jnp.int32, (LANES, LANES), 1)
    shared = packed[:LANES, :] * scale
    right = packed[LANES:2 * LANES, :] * scale
    upper = jnp.where(j >= i, shared, 0.0)
    lower = jnp.where(j < i, shared, 0.0)
    diagonal = packed[2 * LANES:2 * LANES + 1, :] * scale
    t_ref[:LANES, :LANES] = jnp.where(j >= i, shared, upper.T)
    t_ref[:LANES, LANES:] = right
    t_ref[LANES:, :LANES] = right.T
    corner = jnp.where(j < i, shared, lower.T)
    t_ref[LANES:, LANES:] = jnp.where(i == j, diagonal, corner)
    vpad[...] = jnp.zeros(vpad.shape, jnp.float32)
    rows[...] = jnp.zeros(rows.shape, jnp.float32)
    per_tile = LANES // PANEL
    for tile in range(tiles):
        @pl.loop(tile * per_tile, (tile + 1) * per_tile)
        def _(panel):
            factor_panel(tile, tiles, panel, t_ref, f_ref, x_ref, cols, rows, vpad)
    inverse = x_ref[...]
    high = inverse.astype(jnp.bfloat16)
    low = (inverse - high.astype(jnp.float32)).astype(jnp.bfloat16)
    load_new.wait()
    load_old.wait()
    _, planes, rows_y, rows_z = out_ref.shape
    stores = []
    for plane in range(planes):
        for pair in range(0, rows_y, 2):
            column = (plane * rows_y + pair) * LANES
            block = stack[:, column:column + 2 * LANES]
            sums = jnp.dot(high, block, preferred_element_type=jnp.float32)
            sums = sums + jnp.dot(low, block, preferred_element_type=jnp.float32)
            for y in (0, 1):
                tall[pl.ds(pair + y, order, stride=rows_y), :] = sums[:, y * LANES:(y + 1) * LANES]

        @pl.loop(0, order, unroll=8)
        def _(row):
            at = pl.multiple_of(row * rows_y, rows_y)
            staged[plane, row] = tall[pl.ds(at, rows_y), :].astype(jnp.bfloat16)

        store = pltpu.make_async_copy(staged.at[plane], out_ref.at[:, plane], out_sem.at[plane])
        store.start()
        stores.append(store)
    for store in stores:
        store.wait()


def factor_and_modes(packed, s_new, s_old, shape, cell_total):
    order, planes, rows_y, rows_z = shape
    vmem = pl.BlockSpec(memory_space=pltpu.VMEM)
    hbm = pl.BlockSpec(memory_space=pl.ANY)
    square = (order, order)
    return pl.pallas_call(
        functools.partial(factor_kernel, 1.0 / cell_total),
        out_shape=[
            jax.ShapeDtypeStruct(square, jnp.float32),
            jax.ShapeDtypeStruct(shape, jnp.bfloat16),
        ],
        in_specs=[vmem, hbm, hbm],
        out_specs=[vmem, hbm],
        scratch_shapes=[
            pltpu.VMEM(square, jnp.float32),
            pltpu.VMEM(square, jnp.float32),
            pltpu.VMEM((PANEL, PANEL, LANES), jnp.float32),
            pltpu.VMEM((PANEL * SUBS, LANES), jnp.float32),
            pltpu.VMEM((LANES, order), jnp.float32),
            pltpu.VMEM((order, planes * rows_y * rows_z), jnp.bfloat16),
            pltpu.VMEM((order * rows_y, rows_z), jnp.float32),
            pltpu.VMEM((planes, order, rows_y, rows_z), jnp.bfloat16),
            pltpu.SemaphoreType.DMA((2,)),
            pltpu.SemaphoreType.DMA((planes,)),
        ],
        compiler_params=pltpu.CompilerParams(vmem_limit_bytes=VMEM_BYTES),
        name="factor",
    )(packed, s_new, s_old)


def shards(snapshots, old_modes, mode_scales, plane_counts, links):
    new_count, planes, rows_y, rows_z = snapshots.shape
    order = new_count + old_modes.shape[0]
    peers = lax.axis_size("blk")
    up = [(i, (i + 1) % peers) for i in range(peers)]
    down = [(j, i) for i, j in up]
    first = lax.slice_in_dim(snapshots, 0, 1, axis=1)
    last = lax.dynamic_slice_in_dim(snapshots, plane_counts[0] - 1, 1, axis=1)
    after = lax.ppermute(first, "blk", down)
    before = lax.ppermute(last, "blk", up)
    s_old, old_gram = scaled_rows(old_modes, mode_scales, plane_counts)
    s_new, packed = filtered_rows(
        snapshots, before, after, plane_counts, links, s_old, old_gram
    )
    sums = sum_over(packed, "blk")
    factor, modes = factor_and_modes(
        sums, s_new, s_old, (order, planes, rows_y, rows_z), peers * planes * rows_y * rows_z
    )
    return (modes, factor)


def solution(mesh):
    return jax.shard_map(
        shards,
        mesh=mesh,
        in_specs=(
            P(None, ("groups", "blk"), None, None),
            P(None, ("groups", "blk"), None, None),
            P("groups"),
            P(("groups", "blk")),
            P(("groups", "blk"), None),
        ),
        out_specs=(P(None, ("groups", "blk"), None, None), P("groups", None)),
        check_vma=False,
    )
```

```python
import functools

import jax
import jax.numpy as jnp
from jax import lax
from jax.experimental import pallas as pl
from jax.experimental.pallas import tpu as pltpu
from jax.sharding import PartitionSpec as P

PANEL = 16
LANES = 128
SUBS = 8
SPREAD = 4
VMEM_BYTES = 40 * 1024 * 1024


def nt_dot(left_rows, right_rows):
    return lax.dot_general(
        left_rows, right_rows, (((1,), (1,)), ((), ())), preferred_element_type=jnp.float32
    )


def swap(x, axis, flip):
    peers = lax.axis_size(axis)
    return lax.ppermute(x, axis, [(i, i ^ flip) for i in range(peers)])


def relay(tall, s_ref, plane, rows_y):
    rows = s_ref.shape[1]
    for y in range(rows_y):
        part = tall[pl.ds(y, rows, stride=rows_y), :].astype(jnp.bfloat16)
        half = (y % 2) * LANES
        s_ref[(plane * rows_y + y) // 2, :, half:half + LANES] = part


def scale_kernel(scales_ref, count_ref, old_ref, s_ref, gram_ref, tall):
    rows, planes, rows_y, _ = old_ref.shape
    for plane in range(planes):
        alive = jnp.where(plane < count_ref[0], 1.0, 0.0)

        @pl.loop(0, rows, unroll=8)
        def _(row):
            weight = scales_ref[row]
            at = pl.multiple_of(row * rows_y, rows_y)
            tall[pl.ds(at, rows_y), :] = old_ref[row, plane].astype(jnp.float32) * weight * alive

        relay(tall, s_ref, plane, rows_y)
    gram_ref[...] = sum(nt_dot(s_ref[k], s_ref[k]) for k in range(s_ref.shape[0]))


def scaled_rows(old_modes, mode_scales, plane_counts):
    rows, planes, rows_y, rows_z = old_modes.shape
    cells = planes * rows_y * rows_z
    smem = pl.BlockSpec(memory_space=pltpu.SMEM)
    vmem = pl.BlockSpec(memory_space=pltpu.VMEM)
    return pl.pallas_call(
        scale_kernel,
        out_shape=[
            jax.ShapeDtypeStruct((planes * rows_y // 2, rows, 2 * rows_z), jnp.bfloat16),
            jax.ShapeDtypeStruct((rows, rows), jnp.float32),
        ],
        in_specs=[smem, smem, vmem],
        out_specs=[vmem, vmem],
        scratch_shapes=[pltpu.VMEM((rows * rows_y, rows_z), jnp.float32)],
        compiler_params=pltpu.CompilerParams(vmem_limit_bytes=VMEM_BYTES),
        cost_estimate=pl.CostEstimate(
            flops=2 * rows * rows * cells, bytes_accessed=8 * rows * cells, transcendentals=0
        ),
        name="scale_gram",
    )(mode_scales, plane_counts, old_modes)


def smooth(field, axis, place, length):
    lower = jnp.where(place == 0, 0.0, pltpu.roll(field, 1, axis=axis))
    upper = jnp.where(place == length - 1, 0.0, pltpu.roll(field, length - 1, axis=axis))
    return 0.25 * lower + 0.5 * field + 0.25 * upper


def packed_rows(order):
    chunk = -(-(order + SUBS) // (SPREAD * SUBS)) * SUBS
    return SPREAD * chunk


def filter_kernel(
    count_ref, links_ref, snap_ref, before_ref, after_ref, old_ref, oldgram_ref, s_ref, *rest
):
    chunk_refs, (tall, packed) = rest[:SPREAD], rest[SPREAD:]
    rows, planes, rows_y, rows_z = snap_ref.shape
    count = count_ref[0]
    join_low = links_ref[0, 0].astype(jnp.float32)
    join_high = links_ref[0, 1].astype(jnp.float32)
    place_y = lax.broadcasted_iota(jnp.int32, (rows_y, rows_z), 0)
    place_z = lax.broadcasted_iota(jnp.int32, (rows_y, rows_z), 1)
    for plane in range(planes):
        alive = jnp.where(plane < count, 1.0, 0.0)
        is_last = plane == count - 1

        @pl.loop(0, rows, unroll=8)
        def _(row):
            own = snap_ref[row, plane].astype(jnp.float32)
            if plane == 0:
                behind = before_ref[row, 0].astype(jnp.float32) * join_low
            else:
                behind = snap_ref[row, plane - 1].astype(jnp.float32)
            forward = after_ref[row, 0].astype(jnp.float32) * join_high
            if plane < planes - 1:
                forward = jnp.where(is_last, forward, snap_ref[row, plane + 1].astype(jnp.float32))
            field = 0.25 * behind + 0.5 * own + 0.25 * forward
            field = smooth(smooth(field, 0, place_y, rows_y), 1, place_z, rows_z) * alive
            at = pl.multiple_of(row * rows_y, rows_y)
            tall[pl.ds(at, rows_y), :] = field

        relay(tall, s_ref, plane, rows_y)
    pairs = range(s_ref.shape[0])
    new_new = sum(nt_dot(s_ref[k], s_ref[k]) for k in pairs)
    new_old = sum(nt_dot(s_ref[k], old_ref[k]) for k in pairs)
    split = LANES - rows
    old_old = oldgram_ref[...]
    top = jnp.concatenate([new_new, new_old[:, :split]], axis=1)
    hidden = jnp.zeros((split, rows), jnp.float32)
    middle = jnp.concatenate([hidden, old_old[:split, :split]], axis=1)
    upper_left = jnp.concatenate([top, middle], axis=0)
    upper_right = jnp.concatenate([new_old[:, split:], old_old[:split, split:]], axis=0)
    lower_right = old_old[split:, split:]
    i = lax.broadcasted_iota(jnp.int32, (LANES, LANES), 0)
    j = lax.broadcasted_iota(jnp.int32, (LANES, LANES), 1)
    packed[:LANES, :] = jnp.where(j >= i, upper_left, lower_right)
    packed[LANES:2 * LANES, :] = upper_right
    packed[2 * LANES:, :] = jnp.zeros((packed.shape[0] - 2 * LANES, LANES), jnp.float32)
    packed[2 * LANES:2 * LANES + 1, :] = jnp.sum(
        jnp.where(i == j, lower_right, 0.0), axis=0, keepdims=True
    )
    share = lax.axis_index("blk") % SPREAD
    height = packed.shape[0] // SPREAD
    for flip in range(SPREAD):
        at = pl.multiple_of((share ^ flip) * height, SUBS)
        chunk_refs[flip][...] = packed[pl.ds(at, height), :]


def filtered_rows(snapshots, before, after, plane_counts, links, s_old, old_gram):
    rows, planes, rows_y, rows_z = snapshots.shape
    cells = planes * rows_y * rows_z
    order = rows + s_old.shape[1]
    height = packed_rows(order)
    smem = pl.BlockSpec(memory_space=pltpu.SMEM)
    vmem = pl.BlockSpec(memory_space=pltpu.VMEM)
    chunk = jax.ShapeDtypeStruct((height // SPREAD, LANES), jnp.float32)
    return pl.pallas_call(
        filter_kernel,
        out_shape=[jax.ShapeDtypeStruct((planes * rows_y // 2, rows, 2 * rows_z), jnp.bfloat16)] + [chunk] * SPREAD,
        in_specs=[smem, smem] + [vmem] * 5,
        out_specs=[vmem] * (1 + SPREAD),
        scratch_shapes=[
            pltpu.VMEM((rows * rows_y, rows_z), jnp.float32),
            pltpu.VMEM((height, LANES), jnp.float32),
        ],
        compiler_params=pltpu.CompilerParams(vmem_limit_bytes=VMEM_BYTES),
        cost_estimate=pl.CostEstimate(
            flops=2 * rows * order * cells, bytes_accessed=2 * order * cells, transcendentals=0
        ),
        name="filter_gram",
    )(plane_counts, links, snapshots, before, after, s_old, old_gram)


def sum_chunks(chunks, axis):
    peers = lax.axis_size(axis)
    arrived = [chunks[0]] + [swap(chunks[d], axis, d) for d in range(1, SPREAD)]
    total = (arrived[0] + arrived[1]) + (arrived[2] + arrived[3])
    step = SPREAD
    while step < peers:
        if step * 4 <= peers:
            one, two, three = (swap(total, axis, d * step) for d in (1, 2, 3))
            total = (total + one) + (two + three)
            step *= 4
        else:
            total = total + swap(total, axis, step)
            step *= 2
    return [total] + [swap(total, axis, d) for d in range(1, SPREAD)]


def split_three(x):
    one = x.astype(jnp.bfloat16)
    rest = x - one.astype(jnp.float32)
    two = rest.astype(jnp.bfloat16)
    three = (rest - two.astype(jnp.float32)).astype(jnp.bfloat16)
    return one, two, three


LEFT = (0, 0, 0, 1, 1, 2)
RIGHT = (0, 1, 2, 0, 1, 0)


def eliminate_all(panel, t_ref, wide):
    tiles, order, _ = t_ref.shape
    first = panel * PANEL
    tile = jnp.maximum(panel, 0) // (LANES // PANEL)
    left = split_three(t_ref[tile])
    left = jnp.concatenate([left[k] for k in LEFT], axis=1)
    update = jnp.dot(left, wide[lax.rem(panel + 2, 2)], preferred_element_type=jnp.float32)
    row = lax.broadcasted_iota(jnp.int32, (order, LANES), 0)
    lane = lax.broadcasted_iota(jnp.int32, (order, LANES), 1)
    below = row >= first + 2 * PANEL
    for s in range(tiles):
        column = lane + s * LANES
        mine = (column >= first) & (column < first + PANEL)
        held = t_ref[s]
        fresh = jnp.where(mine, 0.0, held) - update[:, s * LANES:(s + 1) * LANES]
        t_ref[s] = jnp.where(below, fresh, held)


def factor_panel(panel, t_ref, f_ref, x_ref, cols, rows, wide, narrow):
    tiles, order, _ = t_ref.shape
    first = pl.multiple_of(panel * PANEL, PANEL)
    tile = panel // (LANES // PANEL)
    off = pl.multiple_of(first - tile * LANES, PANEL)
    here = pl.ds(first, PANEL)
    lane = lax.broadcasted_iota(jnp.int32, (PANEL, LANES), 1)
    sub = lax.broadcasted_iota(jnp.int32, (PANEL, LANES), 0)
    own = t_ref[tile, here, :]
    turn = lax.rem(LANES - off, LANES)
    turned = pltpu.roll(own, turn, axis=1)
    for j in range(PANEL):
        cols[j] = jnp.broadcast_to(turned[:, j:j + 1], (PANEL, LANES))
    for s in range(tiles):
        column = lane + s * LANES
        inside = (column >= first) & (column < first + PANEL)
        unit_rows = jnp.where(column - first == sub, 1.0, 0.0)
        rows[pl.ds(s, PANEL, stride=SUBS), :] = jnp.where(inside, unit_rows, t_ref[s, here, :])
    rows[pl.ds(tiles, PANEL, stride=SUBS), :] = own
    entry = [
        [jnp.broadcast_to(cols[j, i:i + 1, :], (SUBS, LANES)) for j in range(i + 1)]
        for i in range(PANEL)
    ]
    y = [rows[i * SUBS:(i + 1) * SUBS, :] for i in range(PANEL)]
    eliminate_all(panel - 1, t_ref, wide)
    after = jnp.minimum(first + PANEL, order - PANEL)
    after = pl.ds(pl.multiple_of(after, PANEL), PANEL)
    ahead = pltpu.roll(t_ref[tile, after, :], turn, axis=1)
    pieces = [jnp.where(lane < PANEL, piece.astype(jnp.float32), 0.0) for piece in split_three(ahead)]
    left = pieces[LEFT[0]]
    for k in range(1, len(LEFT)):
        left = left + pltpu.roll(pieces[LEFT[k]], k * PANEL, axis=1)
    left = left.astype(jnp.bfloat16)

    unit = [[None] * PANEL for _ in range(PANEL)]
    recip = []
    for k in range(PANEL):
        recip.append(1.0 / entry[k][k])
        for i in range(k + 1, PANEL):
            unit[i][k] = entry[i][k] * recip[k]
        for j in range(k + 1, PANEL):
            for i in range(j, PANEL):
                if i == j:
                    part = (entry[i][k] * entry[i][k]) * recip[k]
                else:
                    part = unit[i][k] * entry[j][k]
                entry[i][j] = entry[i][j] - part
        for i in range(k + 1, PANEL):
            y[i] = y[i] - unit[i][k] * y[k]
    v = [recip[i] * y[i] for i in range(PANEL)]
    for j in reversed(range(PANEL)):
        for i in range(j):
            v[i] = v[i] - unit[j][i] * v[j]
    for i in range(PANEL):
        rows[i * SUBS:(i + 1) * SUBS, :] = v[i]
    v = jnp.concatenate([rows[pl.ds(s, PANEL, stride=SUBS), :] for s in range(tiles)], axis=1)
    v = split_three(v)
    for k in range(len(RIGHT)):
        narrow[k * PANEL:(k + 1) * PANEL, :] = v[RIGHT[k]]
    update = jnp.dot(left, narrow[...], preferred_element_type=jnp.float32)
    more = first + PANEL < order
    for s in range(tiles):
        column = lane + s * LANES
        mine = (column >= first) & (column < first + PANEL)
        held = t_ref[s, after, :]
        fresh = jnp.where(mine, 0.0, held) - update[:, s * LANES:(s + 1) * LANES]
        t_ref[s, after, :] = jnp.where(more, fresh, held)
    side = lax.rem(panel, 2)
    old_off = lax.rem(off + LANES - 2 * PANEL, LANES)
    for k in range(len(RIGHT)):
        old_at = pl.multiple_of(old_off + k * LANES, PANEL)
        wide[side, pl.ds(old_at, PANEL), :] = jnp.zeros((PANEL, order), jnp.bfloat16)
        at = pl.multiple_of(off + k * LANES, PANEL)
        wide[side, pl.ds(at, PANEL), :] = v[RIGHT[k]]

    for i in range(PANEL):
        rows[i * SUBS:(i + 1) * SUBS, :] = jnp.sqrt(recip[i]) * y[i]
    whole = rows[pl.ds(tiles, PANEL, stride=SUBS), :]
    for s in range(tiles):
        span = slice(s * LANES, (s + 1) * LANES)
        column = lane + s * LANES
        part = rows[pl.ds(s, PANEL, stride=SUBS), :]
        inside = (column >= first) & (column < first + PANEL)
        f_ref[here, span] = jnp.where(column >= first + sub, jnp.where(inside, whole, part), 0.0)
        x_ref[here, span] = jnp.where(column <= first + sub, part, 0.0)


def factor_kernel(scale, *refs):
    chunk_refs, refs = refs[:SPREAD], refs[SPREAD:]
    new_ref, old_ref, f_ref, out_ref, *refs = refs
    packed, t_ref, x_ref, cols, rows, wide, narrow, x_pair, stack, *refs = refs
    tall, staged, in_sem, out_sem = refs
    tiles, order, _ = t_ref.shape
    new_count = new_ref.shape[1]
    load_new = pltpu.make_async_copy(new_ref, stack.at[:, pl.ds(0, new_count)], in_sem.at[0])
    load_old = pltpu.make_async_copy(
        old_ref, stack.at[:, pl.ds(new_count, order - new_count)], in_sem.at[1]
    )
    load_new.start()
    load_old.start()
    share = lax.axis_index("blk") % SPREAD
    height = packed.shape[0] // SPREAD
    for flip in range(SPREAD):
        at = pl.multiple_of((share ^ flip) * height, SUBS)
        packed[pl.ds(at, height), :] = chunk_refs[flip][...] * scale
    i = lax.broadcasted_iota(jnp.int32, (LANES, LANES), 0)
    j = lax.broadcasted_iota(jnp.int32, (LANES, LANES), 1)
    shared = packed[:LANES, :]
    right = packed[LANES:2 * LANES, :]
    upper = jnp.where(j >= i, shared, 0.0)
    lower = jnp.where(j < i, shared, 0.0)
    diagonal = packed[2 * LANES:2 * LANES + 1, :]
    t_ref[0, :LANES, :] = jnp.where(j >= i, shared, upper.T)
    t_ref[1, :LANES, :] = right
    t_ref[0, LANES:, :] = right.T
    corner = jnp.where(j < i, shared, lower.T)
    t_ref[1, LANES:, :] = jnp.where(i == j, diagonal, corner)
    wide[...] = jnp.zeros(wide.shape, wide.dtype)
    narrow[...] = jnp.zeros(narrow.shape, narrow.dtype)
    rows[...] = jnp.zeros(rows.shape, jnp.float32)

    @pl.loop(0, order // PANEL)
    def _(panel):
        factor_panel(panel, t_ref, f_ref, x_ref, cols, rows, wide, narrow)

    inverse = x_ref[...]
    high = inverse.astype(jnp.bfloat16)
    low = (inverse - high.astype(jnp.float32)).astype(jnp.bfloat16)
    x_pair[...] = jnp.concatenate([high, low], axis=1)
    load_new.wait()
    load_old.wait()
    _, planes, rows_y, rows_z = out_ref.shape
    steps = rows_y // 2
    count = order // steps

    def store(plane, step):
        some = pl.ds(step * count, count)
        return pltpu.make_async_copy(
            staged.at[plane, some], out_ref.at[some, plane], out_sem.at[plane, step]
        )

    for plane in range(planes + 1):
        @pl.loop(0, steps)
        def _(step):
            if plane < planes:
                block = stack[plane * steps + step]
                sums = jnp.dot(x_pair[:, :order], block, preferred_element_type=jnp.float32)
                sums = sums + jnp.dot(x_pair[:, order:], block, preferred_element_type=jnp.float32)
                for y in (0, 1):
                    part = sums[:, y * rows_z:(y + 1) * rows_z]
                    tall[plane % 2, pl.ds(2 * step + y, order, stride=rows_y), :] = part
            if plane > 0:
                at = pl.multiple_of(step * count * rows_y, count * rows_y)
                ready = tall[(plane - 1) % 2, pl.ds(at, count * rows_y), :].astype(jnp.bfloat16)
                staged[plane - 1, pl.ds(step * count, count)] = ready.reshape(count, rows_y, rows_z)
                store(plane - 1, step).start()

    for plane in range(planes):
        @pl.loop(0, steps)
        def _(step):
            store(plane, step).wait()


def factor_and_modes(chunks, s_new, s_old, shape, cell_total):
    order, planes, rows_y, rows_z = shape
    height = chunks[0].shape[0] * SPREAD
    vmem = pl.BlockSpec(memory_space=pltpu.VMEM)
    hbm = pl.BlockSpec(memory_space=pl.ANY)
    square = (order, order)
    return pl.pallas_call(
        functools.partial(factor_kernel, 1.0 / cell_total),
        out_shape=[
            jax.ShapeDtypeStruct(square, jnp.float32),
            jax.ShapeDtypeStruct(shape, jnp.bfloat16),
        ],
        in_specs=[vmem] * SPREAD + [hbm, hbm],
        out_specs=[vmem, hbm],
        scratch_shapes=[
            pltpu.VMEM((height, LANES), jnp.float32),
            pltpu.VMEM((order // LANES, order, LANES), jnp.float32),
            pltpu.VMEM(square, jnp.float32),
            pltpu.VMEM((PANEL, PANEL, LANES), jnp.float32),
            pltpu.VMEM((PANEL * SUBS, LANES), jnp.float32),
            pltpu.VMEM((2, len(LEFT) * LANES, order), jnp.bfloat16),
            pltpu.VMEM((LANES, order), jnp.bfloat16),
            pltpu.VMEM((order, 2 * order), jnp.bfloat16),
            pltpu.VMEM((planes * rows_y // 2, order, 2 * rows_z), jnp.bfloat16),
            pltpu.VMEM((2, order * rows_y, rows_z), jnp.float32),
            pltpu.VMEM((planes, order, rows_y, rows_z), jnp.bfloat16),
            pltpu.SemaphoreType.DMA((2,)),
            pltpu.SemaphoreType.DMA((planes, rows_y // 2)),
        ],
        compiler_params=pltpu.CompilerParams(vmem_limit_bytes=VMEM_BYTES),
        name="factor",
    )(*chunks, s_new, s_old)


def shards(snapshots, old_modes, mode_scales, plane_counts, links):
    new_count, planes, rows_y, rows_z = snapshots.shape
    order = new_count + old_modes.shape[0]
    peers = lax.axis_size("blk")
    up = [(i, (i + 1) % peers) for i in range(peers)]
    down = [(j, i) for i, j in up]
    first = lax.slice_in_dim(snapshots, 0, 1, axis=1)
    last = lax.dynamic_slice_in_dim(snapshots, plane_counts[0] - 1, 1, axis=1)
    after = lax.ppermute(first, "blk", down)
    before = lax.ppermute(last, "blk", up)
    s_old, old_gram = scaled_rows(old_modes, mode_scales, plane_counts)
    s_new, *chunks = filtered_rows(
        snapshots, before, after, plane_counts, links, s_old, old_gram
    )
    sums = sum_chunks(chunks, "blk")
    factor, modes = factor_and_modes(
        sums, s_new, s_old, (order, planes, rows_y, rows_z), peers * planes * rows_y * rows_z
    )
    return (modes, factor)


def solution(mesh):
    return jax.shard_map(
        shards,
        mesh=mesh,
        in_specs=(
            P(None, ("groups", "blk"), None, None),
            P(None, ("groups", "blk"), None, None),
            P("groups"),
            P(("groups", "blk")),
            P(("groups", "blk"), None),
        ),
        out_specs=(P(None, ("groups", "blk"), None, None), P("groups", None)),
        check_vma=False,
    )
```

```python
import functools

import jax
import jax.numpy as jnp
from jax import lax
from jax.experimental import pallas as pl
from jax.experimental.pallas import tpu as pltpu
from jax.sharding import PartitionSpec as P

PANEL = 16
HALF = 8
LANES = 128
SUBS = 8
SPREAD = 4
VMEM_BYTES = 40 * 1024 * 1024


def nt_dot(left_rows, right_rows):
    return lax.dot_general(
        left_rows, right_rows, (((1,), (1,)), ((), ())), preferred_element_type=jnp.float32
    )


def swap(x, axis, flip):
    peers = lax.axis_size(axis)
    return lax.ppermute(x, axis, [(i, i ^ flip) for i in range(peers)])


def relay(tall, s_ref, plane, rows_y):
    rows = s_ref.shape[1]
    for y in range(rows_y):
        part = tall[pl.ds(y, rows, stride=rows_y), :].astype(jnp.bfloat16)
        half = (y % 2) * LANES
        s_ref[(plane * rows_y + y) // 2, :, half:half + LANES] = part


def scale_kernel(scales_ref, count_ref, old_ref, s_ref, gram_ref, tall):
    rows, planes, rows_y, _ = old_ref.shape
    for plane in range(planes):
        alive = jnp.where(plane < count_ref[0], 1.0, 0.0)

        @pl.loop(0, rows, unroll=8)
        def _(row):
            weight = scales_ref[row]
            at = pl.multiple_of(row * rows_y, rows_y)
            tall[pl.ds(at, rows_y), :] = old_ref[row, plane].astype(jnp.float32) * weight * alive

        relay(tall, s_ref, plane, rows_y)
    gram_ref[...] = sum(nt_dot(s_ref[k], s_ref[k]) for k in range(s_ref.shape[0]))


def scaled_rows(old_modes, mode_scales, plane_counts):
    rows, planes, rows_y, rows_z = old_modes.shape
    cells = planes * rows_y * rows_z
    smem = pl.BlockSpec(memory_space=pltpu.SMEM)
    vmem = pl.BlockSpec(memory_space=pltpu.VMEM)
    return pl.pallas_call(
        scale_kernel,
        out_shape=[
            jax.ShapeDtypeStruct((planes * rows_y // 2, rows, 2 * rows_z), jnp.bfloat16),
            jax.ShapeDtypeStruct((rows, rows), jnp.float32),
        ],
        in_specs=[smem, smem, vmem],
        out_specs=[vmem, vmem],
        scratch_shapes=[pltpu.VMEM((rows * rows_y, rows_z), jnp.float32)],
        compiler_params=pltpu.CompilerParams(vmem_limit_bytes=VMEM_BYTES),
        cost_estimate=pl.CostEstimate(
            flops=2 * rows * rows * cells, bytes_accessed=8 * rows * cells, transcendentals=0
        ),
        name="scale_gram",
    )(mode_scales, plane_counts, old_modes)


def smooth(field, axis, place, length):
    lower = jnp.where(place == 0, 0.0, pltpu.roll(field, 1, axis=axis))
    upper = jnp.where(place == length - 1, 0.0, pltpu.roll(field, length - 1, axis=axis))
    return 0.25 * lower + 0.5 * field + 0.25 * upper


def packed_rows(order):
    chunk = -(-(order + SUBS) // (SPREAD * SUBS)) * SUBS
    return SPREAD * chunk


def filter_kernel(
    count_ref, links_ref, snap_ref, before_ref, after_ref, old_ref, oldgram_ref, s_ref, *rest
):
    chunk_refs, (tall, packed) = rest[:SPREAD], rest[SPREAD:]
    rows, planes, rows_y, rows_z = snap_ref.shape
    count = count_ref[0]
    join_low = links_ref[0, 0].astype(jnp.float32)
    join_high = links_ref[0, 1].astype(jnp.float32)
    place_y = lax.broadcasted_iota(jnp.int32, (rows_y, rows_z), 0)
    place_z = lax.broadcasted_iota(jnp.int32, (rows_y, rows_z), 1)
    for plane in range(planes):
        alive = jnp.where(plane < count, 1.0, 0.0)
        is_last = plane == count - 1

        @pl.loop(0, rows, unroll=8)
        def _(row):
            own = snap_ref[row, plane].astype(jnp.float32)
            if plane == 0:
                behind = before_ref[row, 0].astype(jnp.float32) * join_low
            else:
                behind = snap_ref[row, plane - 1].astype(jnp.float32)
            forward = after_ref[row, 0].astype(jnp.float32) * join_high
            if plane < planes - 1:
                forward = jnp.where(is_last, forward, snap_ref[row, plane + 1].astype(jnp.float32))
            field = 0.25 * behind + 0.5 * own + 0.25 * forward
            field = smooth(smooth(field, 0, place_y, rows_y), 1, place_z, rows_z) * alive
            at = pl.multiple_of(row * rows_y, rows_y)
            tall[pl.ds(at, rows_y), :] = field

        relay(tall, s_ref, plane, rows_y)
    pairs = range(s_ref.shape[0])
    new_new = sum(nt_dot(s_ref[k], s_ref[k]) for k in pairs)
    new_old = sum(nt_dot(s_ref[k], old_ref[k]) for k in pairs)
    split = LANES - rows
    old_old = oldgram_ref[...]
    top = jnp.concatenate([new_new, new_old[:, :split]], axis=1)
    hidden = jnp.zeros((split, rows), jnp.float32)
    middle = jnp.concatenate([hidden, old_old[:split, :split]], axis=1)
    upper_left = jnp.concatenate([top, middle], axis=0)
    upper_right = jnp.concatenate([new_old[:, split:], old_old[:split, split:]], axis=0)
    lower_right = old_old[split:, split:]
    i = lax.broadcasted_iota(jnp.int32, (LANES, LANES), 0)
    j = lax.broadcasted_iota(jnp.int32, (LANES, LANES), 1)
    packed[:LANES, :] = jnp.where(j >= i, upper_left, lower_right)
    packed[LANES:2 * LANES, :] = upper_right
    packed[2 * LANES:, :] = jnp.zeros((packed.shape[0] - 2 * LANES, LANES), jnp.float32)
    packed[2 * LANES:2 * LANES + 1, :] = jnp.sum(
        jnp.where(i == j, lower_right, 0.0), axis=0, keepdims=True
    )
    share = lax.axis_index("blk") % SPREAD
    height = packed.shape[0] // SPREAD
    for flip in range(SPREAD):
        at = pl.multiple_of((share ^ flip) * height, SUBS)
        chunk_refs[flip][...] = packed[pl.ds(at, height), :]


def filtered_rows(snapshots, before, after, plane_counts, links, s_old, old_gram):
    rows, planes, rows_y, rows_z = snapshots.shape
    cells = planes * rows_y * rows_z
    order = rows + s_old.shape[1]
    height = packed_rows(order)
    smem = pl.BlockSpec(memory_space=pltpu.SMEM)
    vmem = pl.BlockSpec(memory_space=pltpu.VMEM)
    chunk = jax.ShapeDtypeStruct((height // SPREAD, LANES), jnp.float32)
    return pl.pallas_call(
        filter_kernel,
        out_shape=[jax.ShapeDtypeStruct((planes * rows_y // 2, rows, 2 * rows_z), jnp.bfloat16)] + [chunk] * SPREAD,
        in_specs=[smem, smem] + [vmem] * 5,
        out_specs=[vmem] * (1 + SPREAD),
        scratch_shapes=[
            pltpu.VMEM((rows * rows_y, rows_z), jnp.float32),
            pltpu.VMEM((height, LANES), jnp.float32),
        ],
        compiler_params=pltpu.CompilerParams(vmem_limit_bytes=VMEM_BYTES),
        cost_estimate=pl.CostEstimate(
            flops=2 * rows * order * cells, bytes_accessed=2 * order * cells, transcendentals=0
        ),
        name="filter_gram",
    )(plane_counts, links, snapshots, before, after, s_old, old_gram)


def sum_chunks(chunks, axis):
    peers = lax.axis_size(axis)
    arrived = [chunks[0]] + [swap(chunks[d], axis, d) for d in range(1, SPREAD)]
    total = (arrived[0] + arrived[1]) + (arrived[2] + arrived[3])
    step = SPREAD
    while step < peers:
        if step * 4 <= peers:
            one, two, three = (swap(total, axis, d * step) for d in (1, 2, 3))
            total = (total + one) + (two + three)
            step *= 4
        else:
            total = total + swap(total, axis, step)
            step *= 2
    return [total] + [swap(total, axis, d) for d in range(1, SPREAD)]


def split_three(x):
    one = x.astype(jnp.bfloat16)
    rest = x - one.astype(jnp.float32)
    two = rest.astype(jnp.bfloat16)
    three = (rest - two.astype(jnp.float32)).astype(jnp.bfloat16)
    return one, two, three


LEFT = (0, 0, 0, 1, 1, 2)
RIGHT = (0, 1, 2, 0, 1, 0)


def eliminate_all(panel, low, t_ref, wide):
    tiles, order, _ = t_ref.shape
    first = panel * PANEL
    tile = jnp.maximum(panel, 0) // (LANES // PANEL)
    left = split_three(t_ref[tile, low:, :])
    left = jnp.concatenate([left[k] for k in LEFT], axis=1)
    update = jnp.dot(left, wide[lax.rem(panel + 2, 2)], preferred_element_type=jnp.float32)
    row = lax.broadcasted_iota(jnp.int32, (order - low, LANES), 0) + low
    lane = lax.broadcasted_iota(jnp.int32, (order - low, LANES), 1)
    below = row >= first + 2 * PANEL
    for s in range(tiles):
        column = lane + s * LANES
        mine = (column >= first) & (column < first + PANEL)
        held = t_ref[s, low:, :]
        fresh = jnp.where(mine, 0.0, held) - update[:, s * LANES:(s + 1) * LANES]
        t_ref[s, low:, :] = jnp.where(below, fresh, held)


def small_factor(entry, count):
    unit = [[None] * count for _ in range(count)]
    recip = []
    for k in range(count):
        recip.append(1.0 / entry[k][k])
        for i in range(k + 1, count):
            unit[i][k] = entry[i][k] * recip[k]
        for j in range(k + 1, count):
            for i in range(j, count):
                if i == j:
                    part = (entry[i][k] * entry[i][k]) * recip[k]
                else:
                    part = unit[i][k] * entry[j][k]
                entry[i][j] = entry[i][j] - part
    return unit, recip


def pivots(cols):
    def spread(j, i):
        return jnp.broadcast_to(cols[j, i:i + 1, :], (SUBS, LANES))

    upper, recip = small_factor([[spread(j, i) for j in range(i + 1)] for i in range(HALF)], HALF)
    below = [cols[j, HALF:, :] for j in range(HALF)]
    for k in range(HALF):
        for j in range(k + 1, HALF):
            below[j] = below[j] - below[k] * upper[j][k]
    corner = [cols[j, HALF:, :] for j in range(HALF, PANEL)]
    for k in range(HALF):
        cols[k, HALF:, :] = below[k] * recip[k]
    left = [[spread(k, HALF + i) for k in range(HALF)] for i in range(HALF)]
    for j in range(HALF):
        for k in range(HALF):
            corner[j] = corner[j] - below[k] * left[j][k]
        cols[HALF + j, HALF:, :] = corner[j]
    entry = [[spread(HALF + j, HALF + i) for j in range(i + 1)] for i in range(HALF)]
    lower, more = small_factor(entry, HALF)
    unit = [row + [None] * HALF for row in upper] + [left[i] + lower[i] for i in range(HALF)]
    return unit, recip + more


def factor_panel(panel, low, t_ref, f_ref, x_ref, cols, rows, wide, narrow):
    tiles, order, _ = t_ref.shape
    first = pl.multiple_of(panel * PANEL, PANEL)
    tile = panel // (LANES // PANEL)
    off = pl.multiple_of(first - tile * LANES, PANEL)
    here = pl.ds(first, PANEL)
    lane = lax.broadcasted_iota(jnp.int32, (PANEL, LANES), 1)
    sub = lax.broadcasted_iota(jnp.int32, (PANEL, LANES), 0)
    own = t_ref[tile, here, :]
    turn = lax.rem(LANES - off, LANES)
    turned = pltpu.roll(own, turn, axis=1)
    for j in range(PANEL):
        cols[j] = jnp.broadcast_to(turned[:, j:j + 1], (PANEL, LANES))
    for s in range(tiles):
        column = lane + s * LANES
        inside = (column >= first) & (column < first + PANEL)
        unit_rows = jnp.where(column - first == sub, 1.0, 0.0)
        rows[pl.ds(s, PANEL, stride=SUBS), :] = jnp.where(inside, unit_rows, t_ref[s, here, :])
    rows[pl.ds(tiles, PANEL, stride=SUBS), :] = own
    y = [rows[i * SUBS:(i + 1) * SUBS, :] for i in range(PANEL)]
    eliminate_all(panel - 1, low, t_ref, wide)
    after = jnp.minimum(first + PANEL, order - PANEL)
    after = pl.ds(pl.multiple_of(after, PANEL), PANEL)
    ahead = pltpu.roll(t_ref[tile, after, :], turn, axis=1)
    pieces = [jnp.where(lane < PANEL, piece.astype(jnp.float32), 0.0) for piece in split_three(ahead)]
    left = pieces[LEFT[0]]
    for k in range(1, len(LEFT)):
        left = left + pltpu.roll(pieces[LEFT[k]], k * PANEL, axis=1)
    left = left.astype(jnp.bfloat16)

    unit, recip = pivots(cols)
    for k in range(PANEL):
        for i in range(k + 1, PANEL):
            y[i] = y[i] - unit[i][k] * y[k]
    v = [recip[i] * y[i] for i in range(PANEL)]
    for j in reversed(range(PANEL)):
        for i in range(j):
            v[i] = v[i] - unit[j][i] * v[j]
    for i in range(PANEL):
        rows[i * SUBS:(i + 1) * SUBS, :] = v[i]
    v = jnp.concatenate([rows[pl.ds(s, PANEL, stride=SUBS), :] for s in range(tiles)], axis=1)
    v = split_three(v)
    for k in range(len(RIGHT)):
        narrow[k * PANEL:(k + 1) * PANEL, :] = v[RIGHT[k]]
    update = jnp.dot(left, narrow[...], preferred_element_type=jnp.float32)
    more = first + PANEL < order
    for s in range(tiles):
        column = lane + s * LANES
        mine = (column >= first) & (column < first + PANEL)
        held = t_ref[s, after, :]
        fresh = jnp.where(mine, 0.0, held) - update[:, s * LANES:(s + 1) * LANES]
        t_ref[s, after, :] = jnp.where(more, fresh, held)
    side = lax.rem(panel, 2)
    old_off = lax.rem(off + LANES - 2 * PANEL, LANES)
    for k in range(len(RIGHT)):
        old_at = pl.multiple_of(old_off + k * LANES, PANEL)
        wide[side, pl.ds(old_at, PANEL), :] = jnp.zeros((PANEL, order), jnp.bfloat16)
        at = pl.multiple_of(off + k * LANES, PANEL)
        wide[side, pl.ds(at, PANEL), :] = v[RIGHT[k]]

    for i in range(PANEL):
        rows[i * SUBS:(i + 1) * SUBS, :] = jnp.sqrt(recip[i]) * y[i]
    whole = rows[pl.ds(tiles, PANEL, stride=SUBS), :]
    for s in range(tiles):
        span = slice(s * LANES, (s + 1) * LANES)
        column = lane + s * LANES
        part = rows[pl.ds(s, PANEL, stride=SUBS), :]
        inside = (column >= first) & (column < first + PANEL)
        f_ref[here, span] = jnp.where(column >= first + sub, jnp.where(inside, whole, part), 0.0)
        x_ref[here, span] = jnp.where(column <= first + sub, part, 0.0)


def factor_kernel(scale, *refs):
    chunk_refs, refs = refs[:SPREAD], refs[SPREAD:]
    f_ref, x_pair, packed, t_ref, x_ref, cols, rows, wide, narrow = refs
    tiles, order, _ = t_ref.shape
    share = lax.axis_index("blk") % SPREAD
    height = packed.shape[0] // SPREAD
    for flip in range(SPREAD):
        at = pl.multiple_of((share ^ flip) * height, SUBS)
        packed[pl.ds(at, height), :] = chunk_refs[flip][...] * scale
    i = lax.broadcasted_iota(jnp.int32, (LANES, LANES), 0)
    j = lax.broadcasted_iota(jnp.int32, (LANES, LANES), 1)
    shared = packed[:LANES, :]
    right = packed[LANES:2 * LANES, :]
    upper = jnp.where(j >= i, shared, 0.0)
    lower = jnp.where(j < i, shared, 0.0)
    diagonal = packed[2 * LANES:2 * LANES + 1, :]
    t_ref[0, :LANES, :] = jnp.where(j >= i, shared, upper.T)
    t_ref[1, :LANES, :] = right
    t_ref[0, LANES:, :] = right.T
    corner = jnp.where(j < i, shared, lower.T)
    t_ref[1, LANES:, :] = jnp.where(i == j, diagonal, corner)
    wide[...] = jnp.zeros(wide.shape, wide.dtype)
    narrow[...] = jnp.zeros(narrow.shape, narrow.dtype)
    rows[...] = jnp.zeros(rows.shape, jnp.float32)

    per_tile = LANES // PANEL
    for low in range(0, order, LANES):
        @pl.loop(low // PANEL, low // PANEL + per_tile)
        def _(panel):
            factor_panel(panel, low, t_ref, f_ref, x_ref, cols, rows, wide, narrow)

    inverse = x_ref[...]
    high = inverse.astype(jnp.bfloat16)
    low = (inverse - high.astype(jnp.float32)).astype(jnp.bfloat16)
    x_pair[...] = jnp.concatenate([high, low], axis=1)


def modes_kernel(x_pair, new_ref, old_ref, out_ref, stack, tall, staged, in_sem, out_sem):
    order = stack.shape[1]
    new_count = new_ref.shape[1]
    load_new = pltpu.make_async_copy(new_ref, stack.at[:, pl.ds(0, new_count)], in_sem.at[0])
    load_old = pltpu.make_async_copy(
        old_ref, stack.at[:, pl.ds(new_count, order - new_count)], in_sem.at[1]
    )
    load_new.start()
    load_old.start()
    load_new.wait()
    load_old.wait()
    _, planes, rows_y, rows_z = out_ref.shape
    steps = rows_y // 2
    count = order // steps

    def store(plane, step):
        some = pl.ds(step * count, count)
        return pltpu.make_async_copy(
            staged.at[plane, some], out_ref.at[some, plane], out_sem.at[plane, step]
        )

    for plane in range(planes + 1):
        @pl.loop(0, steps)
        def _(step):
            if plane < planes:
                block = stack[plane * steps + step]
                sums = jnp.dot(x_pair[:, :order], block, preferred_element_type=jnp.float32)
                sums = sums + jnp.dot(x_pair[:, order:], block, preferred_element_type=jnp.float32)
                for y in (0, 1):
                    part = sums[:, y * rows_z:(y + 1) * rows_z]
                    tall[plane % 2, pl.ds(2 * step + y, order, stride=rows_y), :] = part
            if plane > 0:
                at = pl.multiple_of(step * count * rows_y, count * rows_y)
                ready = tall[(plane - 1) % 2, pl.ds(at, count * rows_y), :].astype(jnp.bfloat16)
                staged[plane - 1, pl.ds(step * count, count)] = ready.reshape(count, rows_y, rows_z)
                store(plane - 1, step).start()

    for plane in range(planes):
        @pl.loop(0, steps)
        def _(step):
            store(plane, step).wait()


def factor_and_inverse(chunks, order, cell_total):
    height = chunks[0].shape[0] * SPREAD
    square = (order, order)
    return pl.pallas_call(
        functools.partial(factor_kernel, 1.0 / cell_total),
        out_shape=[
            jax.ShapeDtypeStruct(square, jnp.float32),
            jax.ShapeDtypeStruct((order, 2 * order), jnp.bfloat16),
        ],
        scratch_shapes=[
            pltpu.VMEM((height, LANES), jnp.float32),
            pltpu.VMEM((order // LANES, order, LANES), jnp.float32),
            pltpu.VMEM(square, jnp.float32),
            pltpu.VMEM((PANEL, PANEL, LANES), jnp.float32),
            pltpu.VMEM((PANEL * SUBS, LANES), jnp.float32),
            pltpu.VMEM((2, len(LEFT) * LANES, order), jnp.bfloat16),
            pltpu.VMEM((LANES, order), jnp.bfloat16),
        ],
        compiler_params=pltpu.CompilerParams(vmem_limit_bytes=VMEM_BYTES),
        name="factor",
    )(*chunks)


def modes_product(x_pair, s_new, s_old, shape):
    order, planes, rows_y, rows_z = shape
    vmem = pl.BlockSpec(memory_space=pltpu.VMEM)
    hbm = pl.BlockSpec(memory_space=pl.ANY)
    return pl.pallas_call(
        modes_kernel,
        out_shape=jax.ShapeDtypeStruct(shape, jnp.bfloat16),
        in_specs=[vmem, hbm, hbm],
        out_specs=hbm,
        scratch_shapes=[
            pltpu.VMEM((planes * rows_y // 2, order, 2 * rows_z), jnp.bfloat16),
            pltpu.VMEM((2, order * rows_y, rows_z), jnp.float32),
            pltpu.VMEM((planes, order, rows_y, rows_z), jnp.bfloat16),
            pltpu.SemaphoreType.DMA((2,)),
            pltpu.SemaphoreType.DMA((planes, rows_y // 2)),
        ],
        compiler_params=pltpu.CompilerParams(vmem_limit_bytes=VMEM_BYTES),
        name="modes",
    )(x_pair, s_new, s_old)


def shards(snapshots, old_modes, mode_scales, plane_counts, links):
    new_count, planes, rows_y, rows_z = snapshots.shape
    order = new_count + old_modes.shape[0]
    peers = lax.axis_size("blk")
    up = [(i, (i + 1) % peers) for i in range(peers)]
    down = [(j, i) for i, j in up]
    first = lax.slice_in_dim(snapshots, 0, 1, axis=1)
    last = lax.dynamic_slice_in_dim(snapshots, plane_counts[0] - 1, 1, axis=1)
    after = lax.ppermute(first, "blk", down)
    before = lax.ppermute(last, "blk", up)
    s_old, old_gram = scaled_rows(old_modes, mode_scales, plane_counts)
    s_new, *chunks = filtered_rows(
        snapshots, before, after, plane_counts, links, s_old, old_gram
    )
    sums = sum_chunks(chunks, "blk")
    factor, x_pair = factor_and_inverse(sums, order, peers * planes * rows_y * rows_z)
    modes = modes_product(x_pair, s_new, s_old, (order, planes, rows_y, rows_z))
    return (modes, factor)


def solution(mesh):
    return jax.shard_map(
        shards,
        mesh=mesh,
        in_specs=(
            P(None, ("groups", "blk"), None, None),
            P(None, ("groups", "blk"), None, None),
            P("groups"),
            P(("groups", "blk")),
            P(("groups", "blk"), None),
        ),
        out_specs=(P(None, ("groups", "blk"), None, None), P("groups", None)),
        check_vma=False,
    )
```

```python
import functools

import jax
import jax.numpy as jnp
from jax import lax
from jax.experimental import pallas as pl
from jax.experimental.pallas import tpu as pltpu
from jax.sharding import PartitionSpec as P

PANEL = 16
HALF = 8
LANES = 128
SUBS = 8
SPREAD = 4
VMEM_BYTES = 40 * 1024 * 1024


def nt_dot(left_rows, right_rows):
    return lax.dot_general(
        left_rows, right_rows, (((1,), (1,)), ((), ())), preferred_element_type=jnp.float32
    )


def swap(x, axis, flip):
    peers = lax.axis_size(axis)
    return lax.ppermute(x, axis, [(i, i ^ flip) for i in range(peers)])


def turn_matrix(size, near):
    order = size * size
    row = lax.broadcasted_iota(jnp.int32, (order, order), 0)
    col = lax.broadcasted_iota(jnp.int32, (order, order), 1)
    same = row % size == col // size
    step = row // size - col % size
    weight = jnp.where(step == 0, 0.5 if near else 1.0, 0.0)
    if near:
        weight = jnp.where((step == 1) | (step == -1), near, weight)
    return jnp.where(same, weight, 0.0).astype(jnp.bfloat16)


def place(turned, s_ref, rows_y, at):
    for plane in range(turned.shape[1] // LANES):
        for y in range(rows_y):
            part = turned[y * rows_y:(y + 1) * rows_y, plane * LANES:(plane + 1) * LANES]
            half = (y % 2) * LANES
            s_ref[(plane * rows_y + y) // 2, at, half:half + LANES] = part


def scale_kernel(count_ref, scales_ref, old_ref, s_ref, gram_ref):
    rows, planes, rows_y, rows_z = old_ref.shape
    turn = turn_matrix(rows_y, 0.0)
    plane = lax.broadcasted_iota(jnp.int32, (rows_y, planes * rows_z), 1) // rows_z
    alive = jnp.where(plane < count_ref[0], 1.0, 0.0)

    @pl.loop(0, rows // rows_y)
    def _(group):
        at = pl.ds(pl.multiple_of(group * rows_y, rows_y), rows_y)
        block = old_ref[at]
        block = jnp.concatenate(
            [block[:, p].reshape(rows_y * rows_y, rows_z) for p in range(planes)], axis=1
        )
        turned = jnp.dot(turn, block, preferred_element_type=jnp.float32)
        weight = scales_ref[at, :] * alive
        turned = turned.reshape(rows_y, rows_y, planes * rows_z) * weight[None]
        turned = turned.reshape(rows_y * rows_y, planes * rows_z).astype(jnp.bfloat16)
        place(turned, s_ref, rows_y, at)

    gram_ref[...] = sum(nt_dot(s_ref[k], s_ref[k]) for k in range(s_ref.shape[0]))


def scaled_rows(old_modes, mode_scales, plane_counts):
    rows, planes, rows_y, rows_z = old_modes.shape
    cells = planes * rows_y * rows_z
    smem = pl.BlockSpec(memory_space=pltpu.SMEM)
    vmem = pl.BlockSpec(memory_space=pltpu.VMEM)
    return pl.pallas_call(
        scale_kernel,
        out_shape=[
            jax.ShapeDtypeStruct((planes * rows_y // 2, rows, 2 * rows_z), jnp.bfloat16),
            jax.ShapeDtypeStruct((rows, rows), jnp.float32),
        ],
        in_specs=[smem, vmem, vmem],
        out_specs=[vmem, vmem],
        compiler_params=pltpu.CompilerParams(vmem_limit_bytes=VMEM_BYTES),
        cost_estimate=pl.CostEstimate(
            flops=2 * rows * rows * cells, bytes_accessed=8 * rows * cells, transcendentals=0
        ),
        name="scale_gram",
    )(plane_counts, mode_scales.reshape(rows, 1), old_modes)


def packed_rows(order):
    chunk = -(-(order + SUBS) // (SPREAD * SUBS)) * SUBS
    return SPREAD * chunk


def filter_kernel(
    count_ref, links_ref, snap_ref, before_ref, after_ref, old_ref, oldgram_ref, s_ref, *rest
):
    chunk_refs, packed = rest[:SPREAD], rest[SPREAD]
    rows, planes, rows_y, rows_z = snap_ref.shape
    count = count_ref[0]
    join_low = links_ref[0, 0].astype(jnp.float32)
    join_high = links_ref[0, 1].astype(jnp.float32)
    z_from = lax.broadcasted_iota(jnp.int32, (rows_z, rows_z), 0)
    z_to = lax.broadcasted_iota(jnp.int32, (rows_z, rows_z), 1)
    gap = jnp.abs(z_from - z_to)
    smooth_z = jnp.where(gap == 0, 0.5, jnp.where(gap == 1, 0.25, 0.0))
    nothing = jnp.zeros((rows_z, rows_z), jnp.bfloat16)
    blocks = [[nothing] * planes for _ in range(planes + 2)]
    for p in range(planes):
        alive = jnp.where(p < count, 1.0, 0.0)
        is_last = jnp.where(p == count - 1, 1.0, 0.0)
        behind = alive * join_low if p == 0 else alive
        blocks[p][p] = (smooth_z * (0.25 * behind)).astype(jnp.bfloat16)
        blocks[p + 1][p] = (smooth_z * (0.5 * alive)).astype(jnp.bfloat16)
        if p < planes - 1:
            inner = 0.25 * alive * (1.0 - is_last)
            blocks[p + 2][p] = (smooth_z * inner).astype(jnp.bfloat16)
            blocks[planes + 1][p] = (smooth_z * (0.25 * is_last * join_high)).astype(jnp.bfloat16)
        else:
            blocks[planes + 1][p] = (smooth_z * (0.25 * alive * join_high)).astype(jnp.bfloat16)
    weights = jnp.concatenate([jnp.concatenate(line, axis=1) for line in blocks], axis=0)
    turn = turn_matrix(rows_y, 0.25)

    @pl.loop(0, rows // rows_y)
    def _(group):
        at = pl.ds(pl.multiple_of(group * rows_y, rows_y), rows_y)
        snap = snap_ref[at]
        sources = [before_ref[at][:, 0]] + [snap[:, p] for p in range(planes)] + [after_ref[at][:, 0]]
        sources = [x.reshape(rows_y * rows_y, rows_z) for x in sources]
        field = jnp.dot(
            jnp.concatenate(sources, axis=1), weights, preferred_element_type=jnp.float32
        )
        high = field.astype(jnp.bfloat16)
        low = (field - high.astype(jnp.float32)).astype(jnp.bfloat16)
        turned = jnp.dot(turn, high, preferred_element_type=jnp.float32)
        turned = turned + jnp.dot(turn, low, preferred_element_type=jnp.float32)
        place(turned.astype(jnp.bfloat16), s_ref, rows_y, at)

    pairs = range(s_ref.shape[0])
    new_new = sum(nt_dot(s_ref[k], s_ref[k]) for k in pairs)
    new_old = sum(nt_dot(s_ref[k], old_ref[k]) for k in pairs)
    split = LANES - rows
    old_old = oldgram_ref[...]
    top = jnp.concatenate([new_new, new_old[:, :split]], axis=1)
    hidden = jnp.zeros((split, rows), jnp.float32)
    middle = jnp.concatenate([hidden, old_old[:split, :split]], axis=1)
    upper_left = jnp.concatenate([top, middle], axis=0)
    upper_right = jnp.concatenate([new_old[:, split:], old_old[:split, split:]], axis=0)
    lower_right = old_old[split:, split:]
    i = lax.broadcasted_iota(jnp.int32, (LANES, LANES), 0)
    j = lax.broadcasted_iota(jnp.int32, (LANES, LANES), 1)
    packed[:LANES, :] = jnp.where(j >= i, upper_left, lower_right)
    packed[LANES:2 * LANES, :] = upper_right
    packed[2 * LANES:, :] = jnp.zeros((packed.shape[0] - 2 * LANES, LANES), jnp.float32)
    packed[2 * LANES:2 * LANES + 1, :] = jnp.sum(
        jnp.where(i == j, lower_right, 0.0), axis=0, keepdims=True
    )
    share = lax.axis_index("blk") % SPREAD
    height = packed.shape[0] // SPREAD
    for flip in range(SPREAD):
        at = pl.multiple_of((share ^ flip) * height, SUBS)
        chunk_refs[flip][...] = packed[pl.ds(at, height), :]


def filtered_rows(snapshots, before, after, plane_counts, links, s_old, old_gram):
    rows, planes, rows_y, rows_z = snapshots.shape
    cells = planes * rows_y * rows_z
    order = rows + s_old.shape[1]
    height = packed_rows(order)
    smem = pl.BlockSpec(memory_space=pltpu.SMEM)
    vmem = pl.BlockSpec(memory_space=pltpu.VMEM)
    chunk = jax.ShapeDtypeStruct((height // SPREAD, LANES), jnp.float32)
    return pl.pallas_call(
        filter_kernel,
        out_shape=[jax.ShapeDtypeStruct((planes * rows_y // 2, rows, 2 * rows_z), jnp.bfloat16)] + [chunk] * SPREAD,
        in_specs=[smem, smem] + [vmem] * 5,
        out_specs=[vmem] * (1 + SPREAD),
        scratch_shapes=[pltpu.VMEM((height, LANES), jnp.float32)],
        compiler_params=pltpu.CompilerParams(vmem_limit_bytes=VMEM_BYTES),
        cost_estimate=pl.CostEstimate(
            flops=2 * rows * order * cells, bytes_accessed=2 * order * cells, transcendentals=0
        ),
        name="filter_gram",
    )(plane_counts, links, snapshots, before, after, s_old, old_gram)


def sum_chunks(chunks, axis):
    peers = lax.axis_size(axis)
    arrived = [chunks[0]] + [swap(chunks[d], axis, d) for d in range(1, SPREAD)]
    total = (arrived[0] + arrived[1]) + (arrived[2] + arrived[3])
    step = SPREAD
    while step < peers:
        if step * 4 <= peers:
            one, two, three = (swap(total, axis, d * step) for d in (1, 2, 3))
            total = (total + one) + (two + three)
            step *= 4
        else:
            total = total + swap(total, axis, step)
            step *= 2
    return [total] + [swap(total, axis, d) for d in range(1, SPREAD)]


def split_three(x):
    one = x.astype(jnp.bfloat16)
    rest = x - one.astype(jnp.float32)
    two = rest.astype(jnp.bfloat16)
    three = (rest - two.astype(jnp.float32)).astype(jnp.bfloat16)
    return one, two, three


LEFT = (0, 0, 0, 1, 1, 2)
RIGHT = (0, 1, 2, 0, 1, 0)


def eliminate_all(panel, low, t_ref, wide):
    tiles, order, _ = t_ref.shape
    first = panel * PANEL
    tile = jnp.maximum(panel, 0) // (LANES // PANEL)
    left = split_three(t_ref[tile, low:, :])
    left = jnp.concatenate([left[k] for k in LEFT], axis=1)
    update = jnp.dot(left, wide[lax.rem(panel + 2, 2)], preferred_element_type=jnp.float32)
    row = lax.broadcasted_iota(jnp.int32, (order - low, LANES), 0) + low
    lane = lax.broadcasted_iota(jnp.int32, (order - low, LANES), 1)
    below = row >= first + 2 * PANEL
    for s in range(tiles):
        column = lane + s * LANES
        mine = (column >= first) & (column < first + PANEL)
        held = t_ref[s, low:, :]
        fresh = jnp.where(mine, 0.0, held) - update[:, s * LANES:(s + 1) * LANES]
        t_ref[s, low:, :] = jnp.where(below, fresh, held)


def small_factor(entry, count):
    unit = [[None] * count for _ in range(count)]
    recip = []
    for k in range(count):
        recip.append(1.0 / entry[k][k])
        for i in range(k + 1, count):
            unit[i][k] = entry[i][k] * recip[k]
        for j in range(k + 1, count):
            for i in range(j, count):
                if i == j:
                    part = (entry[i][k] * entry[i][k]) * recip[k]
                else:
                    part = unit[i][k] * entry[j][k]
                entry[i][j] = entry[i][j] - part
    return unit, recip


def pivots(cols):
    def spread(j, i):
        return jnp.broadcast_to(cols[j, i:i + 1, :], (SUBS, LANES))

    upper, recip = small_factor([[spread(j, i) for j in range(i + 1)] for i in range(HALF)], HALF)
    below = [cols[j, HALF:, :] for j in range(HALF)]
    for k in range(HALF):
        for j in range(k + 1, HALF):
            below[j] = below[j] - below[k] * upper[j][k]
    corner = [cols[j, HALF:, :] for j in range(HALF, PANEL)]
    for k in range(HALF):
        cols[k, HALF:, :] = below[k] * recip[k]
    left = [[spread(k, HALF + i) for k in range(HALF)] for i in range(HALF)]
    for j in range(HALF):
        for k in range(HALF):
            corner[j] = corner[j] - below[k] * left[j][k]
        cols[HALF + j, HALF:, :] = corner[j]
    entry = [[spread(HALF + j, HALF + i) for j in range(i + 1)] for i in range(HALF)]
    lower, more = small_factor(entry, HALF)
    unit = [row + [None] * HALF for row in upper] + [left[i] + lower[i] for i in range(HALF)]
    return unit, recip + more


def factor_panel(panel, low, t_ref, f_ref, x_ref, cols, rows, wide, narrow):
    tiles, order, _ = t_ref.shape
    first = pl.multiple_of(panel * PANEL, PANEL)
    tile = panel // (LANES // PANEL)
    off = pl.multiple_of(first - tile * LANES, PANEL)
    here = pl.ds(first, PANEL)
    lane = lax.broadcasted_iota(jnp.int32, (PANEL, LANES), 1)
    sub = lax.broadcasted_iota(jnp.int32, (PANEL, LANES), 0)
    own = t_ref[tile, here, :]
    turn = lax.rem(LANES - off, LANES)
    turned = pltpu.roll(own, turn, axis=1)
    for j in range(PANEL):
        cols[j] = jnp.broadcast_to(turned[:, j:j + 1], (PANEL, LANES))
    for s in range(tiles):
        column = lane + s * LANES
        inside = (column >= first) & (column < first + PANEL)
        unit_rows = jnp.where(column - first == sub, 1.0, 0.0)
        rows[pl.ds(s, PANEL, stride=SUBS), :] = jnp.where(inside, unit_rows, t_ref[s, here, :])
    rows[pl.ds(tiles, PANEL, stride=SUBS), :] = own
    y = [rows[i * SUBS:(i + 1) * SUBS, :] for i in range(PANEL)]
    eliminate_all(panel - 1, low, t_ref, wide)
    after = jnp.minimum(first + PANEL, order - PANEL)
    after = pl.ds(pl.multiple_of(after, PANEL), PANEL)
    ahead = pltpu.roll(t_ref[tile, after, :], turn, axis=1)
    pieces = [jnp.where(lane < PANEL, piece.astype(jnp.float32), 0.0) for piece in split_three(ahead)]
    left = pieces[LEFT[0]]
    for k in range(1, len(LEFT)):
        left = left + pltpu.roll(pieces[LEFT[k]], k * PANEL, axis=1)
    left = left.astype(jnp.bfloat16)

    unit, recip = pivots(cols)
    for k in range(PANEL):
        for i in range(k + 1, PANEL):
            y[i] = y[i] - unit[i][k] * y[k]
    v = [recip[i] * y[i] for i in range(PANEL)]
    for j in reversed(range(PANEL)):
        for i in range(j):
            v[i] = v[i] - unit[j][i] * v[j]
    for i in range(PANEL):
        rows[i * SUBS:(i + 1) * SUBS, :] = v[i]
    v = jnp.concatenate([rows[pl.ds(s, PANEL, stride=SUBS), :] for s in range(tiles)], axis=1)
    v = split_three(v)
    for k in range(len(RIGHT)):
        narrow[k * PANEL:(k + 1) * PANEL, :] = v[RIGHT[k]]
    update = jnp.dot(left, narrow[...], preferred_element_type=jnp.float32)
    more = first + PANEL < order
    for s in range(tiles):
        column = lane + s * LANES
        mine = (column >= first) & (column < first + PANEL)
        held = t_ref[s, after, :]
        fresh = jnp.where(mine, 0.0, held) - update[:, s * LANES:(s + 1) * LANES]
        t_ref[s, after, :] = jnp.where(more, fresh, held)
    side = lax.rem(panel, 2)
    old_off = lax.rem(off + LANES - 2 * PANEL, LANES)
    for k in range(len(RIGHT)):
        old_at = pl.multiple_of(old_off + k * LANES, PANEL)
        wide[side, pl.ds(old_at, PANEL), :] = jnp.zeros((PANEL, order), jnp.bfloat16)
        at = pl.multiple_of(off + k * LANES, PANEL)
        wide[side, pl.ds(at, PANEL), :] = v[RIGHT[k]]

    for i in range(PANEL):
        rows[i * SUBS:(i + 1) * SUBS, :] = jnp.sqrt(recip[i]) * y[i]
    whole = rows[pl.ds(tiles, PANEL, stride=SUBS), :]
    for s in range(tiles):
        span = slice(s * LANES, (s + 1) * LANES)
        column = lane + s * LANES
        part = rows[pl.ds(s, PANEL, stride=SUBS), :]
        inside = (column >= first) & (column < first + PANEL)
        f_ref[here, span] = jnp.where(column >= first + sub, jnp.where(inside, whole, part), 0.0)
        x_ref[here, span] = jnp.where(column <= first + sub, part, 0.0)


def factor_kernel(scale, *refs):
    chunk_refs, refs = refs[:SPREAD], refs[SPREAD:]
    new_ref, old_ref, f_ref, out_ref, packed, t_ref, x_ref, cols, rows, *refs = refs
    wide, narrow, x_pair, stack, mixed, staged, in_sem, out_sem = refs
    tiles, order, _ = t_ref.shape
    new_count = new_ref.shape[1]
    load_new = pltpu.make_async_copy(new_ref, stack.at[:, pl.ds(0, new_count)], in_sem.at[0])
    load_old = pltpu.make_async_copy(
        old_ref, stack.at[:, pl.ds(new_count, order - new_count)], in_sem.at[1]
    )
    load_new.start()
    load_old.start()
    share = lax.axis_index("blk") % SPREAD
    height = packed.shape[0] // SPREAD
    for flip in range(SPREAD):
        at = pl.multiple_of((share ^ flip) * height, SUBS)
        packed[pl.ds(at, height), :] = chunk_refs[flip][...] * scale
    i = lax.broadcasted_iota(jnp.int32, (LANES, LANES), 0)
    j = lax.broadcasted_iota(jnp.int32, (LANES, LANES), 1)
    shared = packed[:LANES, :]
    right = packed[LANES:2 * LANES, :]
    upper = jnp.where(j >= i, shared, 0.0)
    lower = jnp.where(j < i, shared, 0.0)
    diagonal = packed[2 * LANES:2 * LANES + 1, :]
    t_ref[0, :LANES, :] = jnp.where(j >= i, shared, upper.T)
    t_ref[1, :LANES, :] = right
    t_ref[0, LANES:, :] = right.T
    corner = jnp.where(j < i, shared, lower.T)
    t_ref[1, LANES:, :] = jnp.where(i == j, diagonal, corner)
    wide[...] = jnp.zeros(wide.shape, wide.dtype)
    narrow[...] = jnp.zeros(narrow.shape, narrow.dtype)
    rows[...] = jnp.zeros(rows.shape, jnp.float32)

    per_tile = LANES // PANEL
    for low in range(0, order, LANES):
        @pl.loop(low // PANEL, low // PANEL + per_tile)
        def _(panel):
            factor_panel(panel, low, t_ref, f_ref, x_ref, cols, rows, wide, narrow)

    inverse = x_ref[...]
    high = inverse.astype(jnp.bfloat16)
    low = (inverse - high.astype(jnp.float32)).astype(jnp.bfloat16)
    x_pair[0] = high
    x_pair[1] = low
    load_new.wait()
    load_old.wait()
    _, planes, rows_y, rows_z = out_ref.shape
    steps = rows_y // 2
    for plane in range(planes):
        @pl.loop(0, steps, unroll=2)
        def _(step):
            block = stack[plane * steps + step]
            sums = jnp.dot(x_pair[0], block, preferred_element_type=jnp.float32)
            sums = sums + jnp.dot(x_pair[1], block, preferred_element_type=jnp.float32)
            sums = sums.astype(jnp.bfloat16).reshape(order // rows_y, rows_y, 2 * rows_z)
            for half in (0, 1):
                at = pl.multiple_of((2 * step + half) * rows_y, rows_y)
                mixed[:, pl.ds(at, rows_y), plane * rows_z:(plane + 1) * rows_z] = sums[
                    :, :, half * rows_z:(half + 1) * rows_z
                ]

    turn = turn_matrix(rows_y, 0.0)

    def store(group):
        some = pl.ds(pl.multiple_of(group * rows_y, rows_y), rows_y)
        return pltpu.make_async_copy(staged.at[some], out_ref.at[some], out_sem.at[group])

    @pl.loop(0, order // rows_y, unroll=2)
    def _(group):
        turned = jnp.dot(turn, mixed[group], preferred_element_type=jnp.float32)
        turned = turned.astype(jnp.bfloat16)
        some = pl.ds(pl.multiple_of(group * rows_y, rows_y), rows_y)
        for plane in range(planes):
            part = turned[:, plane * rows_z:(plane + 1) * rows_z]
            staged[some, plane] = part.reshape(rows_y, rows_y, rows_z)
        store(group).start()

    @pl.loop(0, order // rows_y)
    def _(group):
        store(group).wait()


def factor_and_modes(chunks, s_new, s_old, shape, cell_total):
    order, planes, rows_y, rows_z = shape
    height = chunks[0].shape[0] * SPREAD
    vmem = pl.BlockSpec(memory_space=pltpu.VMEM)
    hbm = pl.BlockSpec(memory_space=pl.ANY)
    square = (order, order)
    pairs = planes * rows_y // 2
    return pl.pallas_call(
        functools.partial(factor_kernel, 1.0 / cell_total),
        out_shape=[
            jax.ShapeDtypeStruct(square, jnp.float32),
            jax.ShapeDtypeStruct(shape, jnp.bfloat16),
        ],
        in_specs=[vmem] * SPREAD + [hbm, hbm],
        out_specs=[vmem, hbm],
        scratch_shapes=[
            pltpu.VMEM((height, LANES), jnp.float32),
            pltpu.VMEM((order // LANES, order, LANES), jnp.float32),
            pltpu.VMEM(square, jnp.float32),
            pltpu.VMEM((PANEL, PANEL, LANES), jnp.float32),
            pltpu.VMEM((PANEL * SUBS, LANES), jnp.float32),
            pltpu.VMEM((2, len(LEFT) * LANES, order), jnp.bfloat16),
            pltpu.VMEM((LANES, order), jnp.bfloat16),
            pltpu.VMEM((2, order, order), jnp.bfloat16),
            pltpu.VMEM((pairs, order, 2 * rows_z), jnp.bfloat16),
            pltpu.VMEM((order // rows_y, rows_y * rows_y, planes * rows_z), jnp.bfloat16),
            pltpu.VMEM(shape, jnp.bfloat16),
            pltpu.SemaphoreType.DMA((2,)),
            pltpu.SemaphoreType.DMA((order // rows_y,)),
        ],
        compiler_params=pltpu.CompilerParams(vmem_limit_bytes=VMEM_BYTES),
        name="factor",
    )(*chunks, s_new, s_old)


def shards(snapshots, old_modes, mode_scales, plane_counts, links):
    new_count, planes, rows_y, rows_z = snapshots.shape
    order = new_count + old_modes.shape[0]
    peers = lax.axis_size("blk")
    up = [(i, (i + 1) % peers) for i in range(peers)]
    down = [(j, i) for i, j in up]
    first = lax.slice_in_dim(snapshots, 0, 1, axis=1)
    last = lax.dynamic_slice_in_dim(snapshots, plane_counts[0] - 1, 1, axis=1)
    after = lax.ppermute(first, "blk", down)
    before = lax.ppermute(last, "blk", up)
    s_old, old_gram = scaled_rows(old_modes, mode_scales, plane_counts)
    s_new, *chunks = filtered_rows(
        snapshots, before, after, plane_counts, links, s_old, old_gram
    )
    sums = sum_chunks(chunks, "blk")
    factor, modes = factor_and_modes(
        sums, s_new, s_old, (order, planes, rows_y, rows_z), peers * planes * rows_y * rows_z
    )
    return (modes, factor)


def solution(mesh):
    return jax.shard_map(
        shards,
        mesh=mesh,
        in_specs=(
            P(None, ("groups", "blk"), None, None),
            P(None, ("groups", "blk"), None, None),
            P("groups"),
            P(("groups", "blk")),
            P(("groups", "blk"), None),
        ),
        out_specs=(P(None, ("groups", "blk"), None, None), P("groups", None)),
        check_vma=False,
    )
```

```python
import functools

import jax
import jax.numpy as jnp
from jax import lax
from jax.experimental import pallas as pl
from jax.experimental.pallas import tpu as pltpu
from jax.sharding import PartitionSpec as P

PANEL = 16
HALF = 8
GROUP = 64
LANES = 128
SUBS = 8
SPREAD = 4
VMEM_BYTES = 40 * 1024 * 1024


def nt_dot(left_rows, right_rows):
    return lax.dot_general(
        left_rows, right_rows, (((1,), (1,)), ((), ())), preferred_element_type=jnp.float32
    )


def swap(x, axis, flip):
    peers = lax.axis_size(axis)
    return lax.ppermute(x, axis, [(i, i ^ flip) for i in range(peers)])


def turn_matrix(size, near):
    order = size * size
    row = lax.broadcasted_iota(jnp.int32, (order, order), 0)
    col = lax.broadcasted_iota(jnp.int32, (order, order), 1)
    same = row % size == col // size
    step = row // size - col % size
    weight = jnp.where(step == 0, 0.5 if near else 1.0, 0.0)
    if near:
        weight = jnp.where((step == 1) | (step == -1), near, weight)
    return jnp.where(same, weight, 0.0).astype(jnp.bfloat16)


def place(turned, s_ref, rows_y, at):
    for plane in range(turned.shape[1] // LANES):
        for y in range(rows_y):
            part = turned[y * rows_y:(y + 1) * rows_y, plane * LANES:(plane + 1) * LANES]
            half = (y % 2) * LANES
            s_ref[(plane * rows_y + y) // 2, at, half:half + LANES] = part


def scale_kernel(count_ref, scales_ref, old_ref, s_ref, gram_ref):
    rows, planes, rows_y, rows_z = old_ref.shape
    turn = turn_matrix(rows_y, 0.0)
    plane = lax.broadcasted_iota(jnp.int32, (rows_y, planes * rows_z), 1) // rows_z
    alive = jnp.where(plane < count_ref[0], 1.0, 0.0)

    for group in range(rows // rows_y):
        at = slice(group * rows_y, (group + 1) * rows_y)
        block = old_ref[at]
        block = jnp.concatenate(
            [block[:, p].reshape(rows_y * rows_y, rows_z) for p in range(planes)], axis=1
        )
        turned = jnp.dot(turn, block, preferred_element_type=jnp.float32)
        weight = scales_ref[at, :] * alive
        turned = turned.reshape(rows_y, rows_y, planes * rows_z) * weight[None]
        turned = turned.reshape(rows_y * rows_y, planes * rows_z).astype(jnp.bfloat16)
        place(turned, s_ref, rows_y, at)

    gram_ref[...] = sum(nt_dot(s_ref[k], s_ref[k]) for k in range(s_ref.shape[0]))


def scaled_rows(old_modes, mode_scales, plane_counts):
    rows, planes, rows_y, rows_z = old_modes.shape
    cells = planes * rows_y * rows_z
    smem = pl.BlockSpec(memory_space=pltpu.SMEM)
    vmem = pl.BlockSpec(memory_space=pltpu.VMEM)
    return pl.pallas_call(
        scale_kernel,
        out_shape=[
            jax.ShapeDtypeStruct((planes * rows_y // 2, rows, 2 * rows_z), jnp.bfloat16),
            jax.ShapeDtypeStruct((rows, rows), jnp.float32),
        ],
        in_specs=[smem, vmem, vmem],
        out_specs=[vmem, vmem],
        compiler_params=pltpu.CompilerParams(vmem_limit_bytes=VMEM_BYTES),
        cost_estimate=pl.CostEstimate(
            flops=2 * rows * rows * cells, bytes_accessed=8 * rows * cells, transcendentals=0
        ),
        name="scale_gram",
    )(plane_counts, mode_scales.reshape(rows, 1), old_modes)


def packed_rows(order):
    chunk = -(-(order + SUBS) // (SPREAD * SUBS)) * SUBS
    return SPREAD * chunk


def filter_kernel(
    count_ref, links_ref, snap_ref, after_ref, before_ref, old_ref, oldgram_ref, s_ref, *rest
):
    keep_ref, give_ref, packed = rest
    rows, planes, rows_y, rows_z = snap_ref.shape
    count = count_ref[0]
    join_low = links_ref[0, 0].astype(jnp.float32)
    join_high = links_ref[0, 1].astype(jnp.float32)
    z_from = lax.broadcasted_iota(jnp.int32, (rows_z, rows_z), 0)
    z_to = lax.broadcasted_iota(jnp.int32, (rows_z, rows_z), 1)
    gap = jnp.abs(z_from - z_to)
    smooth_z = jnp.where(gap == 0, 0.5, jnp.where(gap == 1, 0.25, 0.0))
    nothing = jnp.zeros((rows_z, rows_z), jnp.bfloat16)
    blocks = [[nothing] * planes for _ in range(planes + 2)]
    for p in range(planes):
        alive = jnp.where(p < count, 1.0, 0.0)
        is_last = jnp.where(p == count - 1, 1.0, 0.0)
        behind = alive * join_low if p == 0 else alive
        blocks[p][p] = (smooth_z * (0.25 * behind)).astype(jnp.bfloat16)
        blocks[p + 1][p] = (smooth_z * (0.5 * alive)).astype(jnp.bfloat16)
        if p < planes - 1:
            inner = 0.25 * alive * (1.0 - is_last)
            blocks[p + 2][p] = (smooth_z * inner).astype(jnp.bfloat16)
            blocks[planes + 1][p] = (smooth_z * (0.25 * is_last * join_high)).astype(jnp.bfloat16)
        else:
            blocks[planes + 1][p] = (smooth_z * (0.25 * alive * join_high)).astype(jnp.bfloat16)
    weights = jnp.concatenate([jnp.concatenate(line, axis=1) for line in blocks], axis=0)
    turn = turn_matrix(rows_y, 0.25)

    for group in range(rows // rows_y):
        at = slice(group * rows_y, (group + 1) * rows_y)
        snap = snap_ref[at]
        sources = [before_ref[at][:, 0]] + [snap[:, p] for p in range(planes)] + [after_ref[at][:, 0]]
        sources = [x.reshape(rows_y * rows_y, rows_z) for x in sources]
        field = jnp.dot(
            jnp.concatenate(sources, axis=1), weights, preferred_element_type=jnp.float32
        )
        high = field.astype(jnp.bfloat16)
        low = (field - high.astype(jnp.float32)).astype(jnp.bfloat16)
        turned = jnp.dot(turn, high, preferred_element_type=jnp.float32)
        turned = turned + jnp.dot(turn, low, preferred_element_type=jnp.float32)
        place(turned.astype(jnp.bfloat16), s_ref, rows_y, at)

    pairs = range(s_ref.shape[0])
    new_new = sum(nt_dot(s_ref[k], s_ref[k]) for k in pairs)
    new_old = sum(nt_dot(s_ref[k], old_ref[k]) for k in pairs)
    split = LANES - rows
    old_old = oldgram_ref[...]
    top = jnp.concatenate([new_new, new_old[:, :split]], axis=1)
    hidden = jnp.zeros((split, rows), jnp.float32)
    middle = jnp.concatenate([hidden, old_old[:split, :split]], axis=1)
    upper_left = jnp.concatenate([top, middle], axis=0)
    upper_right = jnp.concatenate([new_old[:, split:], old_old[:split, split:]], axis=0)
    lower_right = old_old[split:, split:]
    i = lax.broadcasted_iota(jnp.int32, (LANES, LANES), 0)
    j = lax.broadcasted_iota(jnp.int32, (LANES, LANES), 1)
    packed[:LANES, :] = jnp.where(j >= i, upper_left, lower_right)
    packed[LANES:2 * LANES, :] = upper_right
    packed[2 * LANES:, :] = jnp.zeros((packed.shape[0] - 2 * LANES, LANES), jnp.float32)
    packed[2 * LANES:2 * LANES + 1, :] = jnp.sum(
        jnp.where(i == j, lower_right, 0.0), axis=0, keepdims=True
    )
    share = lax.axis_index("blk") % SPREAD
    height = packed.shape[0] // SPREAD
    for flip in range(SPREAD):
        at = pl.multiple_of((share ^ flip) * height, SUBS)
        side = give_ref if flip % 2 else keep_ref
        part = flip // 2 * height
        side[part:part + height, :] = packed[pl.ds(at, height), :]


def filtered_rows(snapshots, before, after, plane_counts, links, s_old, old_gram):
    rows, planes, rows_y, rows_z = snapshots.shape
    cells = planes * rows_y * rows_z
    order = rows + s_old.shape[1]
    height = packed_rows(order)
    smem = pl.BlockSpec(memory_space=pltpu.SMEM)
    vmem = pl.BlockSpec(memory_space=pltpu.VMEM)
    half = jax.ShapeDtypeStruct((height // 2, LANES), jnp.float32)
    return pl.pallas_call(
        filter_kernel,
        out_shape=[jax.ShapeDtypeStruct((planes * rows_y // 2, rows, 2 * rows_z), jnp.bfloat16)] + [half] * 2,
        in_specs=[smem, smem] + [vmem] * 5,
        out_specs=[vmem] * 3,
        scratch_shapes=[pltpu.VMEM((height, LANES), jnp.float32)],
        compiler_params=pltpu.CompilerParams(vmem_limit_bytes=VMEM_BYTES),
        cost_estimate=pl.CostEstimate(
            flops=2 * rows * order * cells, bytes_accessed=2 * order * cells, transcendentals=0
        ),
        name="filter_gram",
    )(plane_counts, links, snapshots, after, before, s_old, old_gram)


def sum_shares(keep, give, axis):
    peers = lax.axis_size(axis)
    height = keep.shape[0] // 2
    both = keep + swap(give, axis, 1)
    total = both[:height] + swap(both[height:], axis, 2)
    step = SPREAD
    while step < peers:
        total = total + swap(total, axis, step)
        step *= 2
    both = jnp.concatenate([total, swap(total, axis, 2)], axis=0)
    return both, swap(both, axis, 1)


def split_three(x):
    one = x.astype(jnp.bfloat16)
    rest = x - one.astype(jnp.float32)
    two = rest.astype(jnp.bfloat16)
    three = (rest - two.astype(jnp.float32)).astype(jnp.bfloat16)
    return one, two, three


LEFT = (0, 0, 0, 1, 1, 2)
RIGHT = (0, 1, 2, 0, 1, 0)


def eliminate_all(panel, low, t_ref, wide):
    tiles, order, _ = t_ref.shape
    first = panel * PANEL
    tile = jnp.maximum(panel, 0) // (LANES // PANEL)
    left = split_three(t_ref[tile, low:, :])
    left = jnp.concatenate([left[k] for k in LEFT], axis=1)
    update = jnp.dot(left, wide[lax.rem(panel + 2, 2)], preferred_element_type=jnp.float32)
    row = lax.broadcasted_iota(jnp.int32, (order - low, LANES), 0) + low
    lane = lax.broadcasted_iota(jnp.int32, (order - low, LANES), 1)
    below = row >= first + 2 * PANEL
    for s in range(tiles):
        column = lane + s * LANES
        mine = (column >= first) & (column < first + PANEL)
        held = t_ref[s, low:, :]
        fresh = jnp.where(mine, 0.0, held) - update[:, s * LANES:(s + 1) * LANES]
        t_ref[s, low:, :] = jnp.where(below, fresh, held)


def small_factor(entry, count):
    unit = [[None] * count for _ in range(count)]
    recip = []
    for k in range(count):
        recip.append(1.0 / entry[k][k])
        for i in range(k + 1, count):
            unit[i][k] = entry[i][k] * recip[k]
        for j in range(k + 1, count):
            for i in range(j, count):
                if i == j:
                    part = (entry[i][k] * entry[i][k]) * recip[k]
                else:
                    part = unit[i][k] * entry[j][k]
                entry[i][j] = entry[i][j] - part
    return unit, recip


def pivots(cols):
    def spread(j, i):
        return jnp.broadcast_to(cols[j, i:i + 1, :], (SUBS, LANES))

    upper, recip = small_factor([[spread(j, i) for j in range(i + 1)] for i in range(HALF)], HALF)
    below = [cols[j, HALF:, :] for j in range(HALF)]
    for k in range(HALF):
        for j in range(k + 1, HALF):
            below[j] = below[j] - below[k] * upper[j][k]
    corner = [cols[j, HALF:, :] for j in range(HALF, PANEL)]
    for k in range(HALF):
        cols[k, HALF:, :] = below[k] * recip[k]
    left = [[spread(k, HALF + i) for k in range(HALF)] for i in range(HALF)]
    for j in range(HALF):
        for k in range(HALF):
            corner[j] = corner[j] - below[k] * left[j][k]
        cols[HALF + j, HALF:, :] = corner[j]
    entry = [[spread(HALF + j, HALF + i) for j in range(i + 1)] for i in range(HALF)]
    lower, more = small_factor(entry, HALF)
    unit = [row + [None] * HALF for row in upper] + [left[i] + lower[i] for i in range(HALF)]
    return unit, recip + more


def factor_panel(panel, low, t_ref, f_ref, x_ref, cols, rows, wide, narrow):
    tiles, order, _ = t_ref.shape
    first = pl.multiple_of(panel * PANEL, PANEL)
    tile = panel // (LANES // PANEL)
    off = pl.multiple_of(first - tile * LANES, PANEL)
    here = pl.ds(first, PANEL)
    lane = lax.broadcasted_iota(jnp.int32, (PANEL, LANES), 1)
    sub = lax.broadcasted_iota(jnp.int32, (PANEL, LANES), 0)
    own = t_ref[tile, here, :]
    turn = lax.rem(LANES - off, LANES)
    turned = pltpu.roll(own, turn, axis=1)
    for j in range(PANEL):
        cols[j] = jnp.broadcast_to(turned[:, j:j + 1], (PANEL, LANES))
    for s in range(tiles):
        column = lane + s * LANES
        inside = (column >= first) & (column < first + PANEL)
        unit_rows = jnp.where(column - first == sub, 1.0, 0.0)
        rows[pl.ds(s, PANEL, stride=SUBS), :] = jnp.where(inside, unit_rows, t_ref[s, here, :])
    rows[pl.ds(tiles, PANEL, stride=SUBS), :] = own
    y = [rows[i * SUBS:(i + 1) * SUBS, :] for i in range(PANEL)]
    eliminate_all(panel - 1, low, t_ref, wide)
    after = jnp.minimum(first + PANEL, order - PANEL)
    after = pl.ds(pl.multiple_of(after, PANEL), PANEL)
    ahead = pltpu.roll(t_ref[tile, after, :], turn, axis=1)
    pieces = [jnp.where(lane < PANEL, piece.astype(jnp.float32), 0.0) for piece in split_three(ahead)]
    left = pieces[LEFT[0]]
    for k in range(1, len(LEFT)):
        left = left + pltpu.roll(pieces[LEFT[k]], k * PANEL, axis=1)
    left = left.astype(jnp.bfloat16)

    unit, recip = pivots(cols)
    for k in range(PANEL):
        for i in range(k + 1, PANEL):
            y[i] = y[i] - unit[i][k] * y[k]
    v = [recip[i] * y[i] for i in range(PANEL)]
    for j in reversed(range(PANEL)):
        for i in range(j):
            v[i] = v[i] - unit[j][i] * v[j]
    for i in range(PANEL):
        rows[i * SUBS:(i + 1) * SUBS, :] = v[i]
    v = jnp.concatenate([rows[pl.ds(s, PANEL, stride=SUBS), :] for s in range(tiles)], axis=1)
    v = split_three(v)
    for k in range(len(RIGHT)):
        narrow[k * PANEL:(k + 1) * PANEL, :] = v[RIGHT[k]]
    update = jnp.dot(left, narrow[...], preferred_element_type=jnp.float32)
    more = first + PANEL < order
    for s in range(tiles):
        column = lane + s * LANES
        mine = (column >= first) & (column < first + PANEL)
        held = t_ref[s, after, :]
        fresh = jnp.where(mine, 0.0, held) - update[:, s * LANES:(s + 1) * LANES]
        t_ref[s, after, :] = jnp.where(more, fresh, held)
    side = lax.rem(panel, 2)
    old_off = lax.rem(off + LANES - 2 * PANEL, LANES)
    for k in range(len(RIGHT)):
        old_at = pl.multiple_of(old_off + k * LANES, PANEL)
        wide[side, pl.ds(old_at, PANEL), :] = jnp.zeros((PANEL, order), jnp.bfloat16)
        at = pl.multiple_of(off + k * LANES, PANEL)
        wide[side, pl.ds(at, PANEL), :] = v[RIGHT[k]]

    for i in range(PANEL):
        rows[i * SUBS:(i + 1) * SUBS, :] = jnp.sqrt(recip[i]) * y[i]
    whole = rows[pl.ds(tiles, PANEL, stride=SUBS), :]
    for s in range(tiles):
        span = slice(s * LANES, (s + 1) * LANES)
        column = lane + s * LANES
        part = rows[pl.ds(s, PANEL, stride=SUBS), :]
        inside = (column >= first) & (column < first + PANEL)
        f_ref[here, span] = jnp.where(column >= first + sub, jnp.where(inside, whole, part), 0.0)
        x_ref[here, span] = jnp.where(column <= first + sub, part, 0.0)


def factor_kernel(scale, *refs):
    sum_refs, refs = refs[:2], refs[2:]
    new_ref, old_ref, f_ref, out_ref, packed, t_ref, x_ref, cols, rows, *refs = refs
    wide, narrow, x_pair, stack, mixed, staged, in_sem, out_sem = refs
    tiles, order, _ = t_ref.shape
    _, planes, rows_y, rows_z = out_ref.shape
    new_count = new_ref.shape[1]
    load_new = pltpu.make_async_copy(new_ref, stack.at[:, pl.ds(0, new_count)], in_sem.at[0])
    load_old = pltpu.make_async_copy(
        old_ref, stack.at[:, pl.ds(new_count, order - new_count)], in_sem.at[1]
    )
    load_new.start()
    load_old.start()
    share = lax.axis_index("blk") % SPREAD
    height = packed.shape[0] // SPREAD
    for flip in range(SPREAD):
        at = pl.multiple_of((share ^ flip) * height, SUBS)
        part = flip // 2 * height
        packed[pl.ds(at, height), :] = sum_refs[flip % 2][part:part + height, :] * scale
    i = lax.broadcasted_iota(jnp.int32, (LANES, LANES), 0)
    j = lax.broadcasted_iota(jnp.int32, (LANES, LANES), 1)
    shared = packed[:LANES, :]
    right = packed[LANES:2 * LANES, :]
    upper = jnp.where(j >= i, shared, 0.0)
    lower = jnp.where(j < i, shared, 0.0)
    diagonal = packed[2 * LANES:2 * LANES + 1, :]
    t_ref[0, :LANES, :] = jnp.where(j >= i, shared, upper.T)
    t_ref[1, :LANES, :] = right
    t_ref[0, LANES:, :] = right.T
    corner = jnp.where(j < i, shared, lower.T)
    t_ref[1, LANES:, :] = jnp.where(i == j, diagonal, corner)
    wide[...] = jnp.zeros(wide.shape, wide.dtype)
    narrow[...] = jnp.zeros(narrow.shape, narrow.dtype)
    rows[...] = jnp.zeros(rows.shape, jnp.float32)

    turn = turn_matrix(rows_y, 0.0)
    steps = rows_y // 2
    per_group = GROUP // PANEL
    pairs = planes * steps
    per_panel = pairs // per_group

    def split_rows(group):
        rows_here = x_ref[group * GROUP:(group + 1) * GROUP, :]
        high = rows_here.astype(jnp.bfloat16)
        x_pair[:GROUP, :] = high
        x_pair[GROUP:, :] = (rows_here - high.astype(jnp.float32)).astype(jnp.bfloat16)

    def multiply(group, pair):
        depth = (group + 1) * GROUP
        sums = jnp.dot(
            x_pair[:, :depth], stack[pair, :depth, :], preferred_element_type=jnp.float32
        )
        sums = (sums[:GROUP] + sums[GROUP:]).astype(jnp.bfloat16)
        sums = sums.reshape(GROUP // rows_y, rows_y, 2 * rows_z)
        some = slice(group * GROUP // rows_y, (group + 1) * GROUP // rows_y)
        for half in (0, 1):
            y = 2 * (pair % steps) + half
            at = pl.ds(pl.multiple_of(y * rows_y, rows_y), rows_y)
            mixed[pair // steps, some, at, :] = sums[:, :, half * rows_z:(half + 1) * rows_z]

    def store(some):
        at = pl.ds(pl.multiple_of(some * rows_y, rows_y), rows_y)
        return pltpu.make_async_copy(staged.at[at], out_ref.at[at], out_sem.at[some])

    def finish(some):
        block = jnp.concatenate([mixed[plane, some] for plane in range(planes)], axis=1)
        turned = jnp.dot(turn, block, preferred_element_type=jnp.float32).astype(jnp.bfloat16)
        at = pl.ds(pl.multiple_of(some * rows_y, rows_y), rows_y)
        for plane in range(planes):
            part = turned[:, plane * rows_z:(plane + 1) * rows_z]
            staged[at, plane] = part.reshape(rows_y, rows_y, rows_z)
        store(some).start()

    groups = order // GROUP
    blocks = GROUP // rows_y
    for group in range(groups):
        if group == 1:
            load_new.wait()
            load_old.wait()
        if group > 0:
            split_rows(group - 1)

        @pl.loop(0, per_group)
        def _(step):
            panel = group * per_group + step
            factor_panel(panel, group * GROUP, t_ref, f_ref, x_ref, cols, rows, wide, narrow)
            if group > 0:
                for k in range(per_panel):
                    multiply(group - 1, step * per_panel + k)
            if group > 1:
                finish((group - 2) * blocks + step)

    split_rows(groups - 1)
    for k in range(blocks):
        finish((groups - 2) * blocks + k)
    for pair in range(pairs):
        multiply(groups - 1, pair)
    for k in range(blocks):
        finish((groups - 1) * blocks + k)

    @pl.loop(0, order // rows_y)
    def _(some):
        store(some).wait()


def factor_and_modes(sums, s_new, s_old, shape, cell_total):
    order, planes, rows_y, rows_z = shape
    height = sums[0].shape[0] * 2
    vmem = pl.BlockSpec(memory_space=pltpu.VMEM)
    hbm = pl.BlockSpec(memory_space=pl.ANY)
    square = (order, order)
    pairs = planes * rows_y // 2
    return pl.pallas_call(
        functools.partial(factor_kernel, 1.0 / cell_total),
        out_shape=[
            jax.ShapeDtypeStruct(square, jnp.float32),
            jax.ShapeDtypeStruct(shape, jnp.bfloat16),
        ],
        in_specs=[vmem] * 2 + [hbm, hbm],
        out_specs=[vmem, hbm],
        scratch_shapes=[
            pltpu.VMEM((height, LANES), jnp.float32),
            pltpu.VMEM((order // LANES, order, LANES), jnp.float32),
            pltpu.VMEM(square, jnp.float32),
            pltpu.VMEM((PANEL, PANEL, LANES), jnp.float32),
            pltpu.VMEM((PANEL * SUBS, LANES), jnp.float32),
            pltpu.VMEM((2, len(LEFT) * LANES, order), jnp.bfloat16),
            pltpu.VMEM((LANES, order), jnp.bfloat16),
            pltpu.VMEM((2 * GROUP, order), jnp.bfloat16),
            pltpu.VMEM((pairs, order, 2 * rows_z), jnp.bfloat16),
            pltpu.VMEM((planes, order // rows_y, rows_y * rows_y, rows_z), jnp.bfloat16),
            pltpu.VMEM(shape, jnp.bfloat16),
            pltpu.SemaphoreType.DMA((2,)),
            pltpu.SemaphoreType.DMA((order // rows_y,)),
        ],
        compiler_params=pltpu.CompilerParams(vmem_limit_bytes=VMEM_BYTES),
        name="factor",
    )(*sums, s_new, s_old)


def shards(snapshots, old_modes, mode_scales, plane_counts, links):
    new_count, planes, rows_y, rows_z = snapshots.shape
    order = new_count + old_modes.shape[0]
    peers = lax.axis_size("blk")
    up = [(i, (i + 1) % peers) for i in range(peers)]
    down = [(j, i) for i, j in up]
    first = lax.slice_in_dim(snapshots, 0, 1, axis=1)
    last = lax.dynamic_slice_in_dim(snapshots, plane_counts[0] - 1, 1, axis=1)
    before = lax.ppermute(last, "blk", up)
    after = lax.ppermute(first, "blk", down)
    s_old, old_gram = scaled_rows(old_modes, mode_scales, plane_counts)
    s_new, keep, give = filtered_rows(
        snapshots, before, after, plane_counts, links, s_old, old_gram
    )
    sums = sum_shares(keep, give, "blk")
    factor, modes = factor_and_modes(
        sums, s_new, s_old, (order, planes, rows_y, rows_z), peers * planes * rows_y * rows_z
    )
    return (modes, factor)


def solution(mesh):
    return jax.shard_map(
        shards,
        mesh=mesh,
        in_specs=(
            P(None, ("groups", "blk"), None, None),
            P(None, ("groups", "blk"), None, None),
            P("groups"),
            P(("groups", "blk")),
            P(("groups", "blk"), None),
        ),
        out_specs=(P(None, ("groups", "blk"), None, None), P("groups", None)),
        check_vma=False,
    )
```

```python
import functools

import jax
import jax.numpy as jnp
from jax import lax
from jax.experimental import pallas as pl
from jax.experimental.pallas import tpu as pltpu
from jax.sharding import PartitionSpec as P

PANEL = 16
HALF = 8
GROUP = 64
LANES = 128
SUBS = 8
SPREAD = 4
VMEM_BYTES = 40 * 1024 * 1024


def nt_dot(left_rows, right_rows):
    return lax.dot_general(
        left_rows, right_rows, (((1,), (1,)), ((), ())), preferred_element_type=jnp.float32
    )


def swap(x, axis, flip):
    peers = lax.axis_size(axis)
    return lax.ppermute(x, axis, [(i, i ^ flip) for i in range(peers)])


def turn_matrix(size, near):
    order = size * size
    row = lax.broadcasted_iota(jnp.int32, (order, order), 0)
    col = lax.broadcasted_iota(jnp.int32, (order, order), 1)
    same = row % size == col // size
    step = row // size - col % size
    weight = jnp.where(step == 0, 0.5 if near else 1.0, 0.0)
    if near:
        weight = jnp.where((step == 1) | (step == -1), near, weight)
    return jnp.where(same, weight, 0.0).astype(jnp.bfloat16)


def place(turned, s_ref, rows_y, at):
    for plane in range(turned.shape[1] // LANES):
        for y in range(rows_y):
            part = turned[y * rows_y:(y + 1) * rows_y, plane * LANES:(plane + 1) * LANES]
            half = (y % 2) * LANES
            s_ref[(plane * rows_y + y) // 2, at, half:half + LANES] = part


def scale_kernel(count_ref, scales_ref, old_ref, s_ref, gram_ref):
    rows, planes, rows_y, rows_z = old_ref.shape
    turn = turn_matrix(rows_y, 0.0)
    plane = lax.broadcasted_iota(jnp.int32, (rows_y, planes * rows_z), 1) // rows_z
    alive = jnp.where(plane < count_ref[0], 1.0, 0.0)

    for group in range(rows // rows_y):
        at = slice(group * rows_y, (group + 1) * rows_y)
        block = old_ref[at]
        block = jnp.concatenate(
            [block[:, p].reshape(rows_y * rows_y, rows_z) for p in range(planes)], axis=1
        )
        turned = jnp.dot(turn, block, preferred_element_type=jnp.float32)
        weight = scales_ref[at, :] * alive
        turned = turned.reshape(rows_y, rows_y, planes * rows_z) * weight[None]
        turned = turned.reshape(rows_y * rows_y, planes * rows_z).astype(jnp.bfloat16)
        place(turned, s_ref, rows_y, at)

    gram_ref[...] = sum(nt_dot(s_ref[k], s_ref[k]) for k in range(s_ref.shape[0]))


def scaled_rows(old_modes, mode_scales, plane_counts):
    rows, planes, rows_y, rows_z = old_modes.shape
    cells = planes * rows_y * rows_z
    smem = pl.BlockSpec(memory_space=pltpu.SMEM)
    vmem = pl.BlockSpec(memory_space=pltpu.VMEM)
    return pl.pallas_call(
        scale_kernel,
        out_shape=[
            jax.ShapeDtypeStruct((planes * rows_y // 2, rows, 2 * rows_z), jnp.bfloat16),
            jax.ShapeDtypeStruct((rows, rows), jnp.float32),
        ],
        in_specs=[smem, vmem, vmem],
        out_specs=[vmem, vmem],
        compiler_params=pltpu.CompilerParams(vmem_limit_bytes=VMEM_BYTES),
        cost_estimate=pl.CostEstimate(
            flops=2 * rows * rows * cells, bytes_accessed=8 * rows * cells, transcendentals=0
        ),
        name="scale_gram",
    )(plane_counts, mode_scales.reshape(rows, 1), old_modes)


def packed_rows(order):
    chunk = -(-(order + SUBS) // (SPREAD * SUBS)) * SUBS
    return SPREAD * chunk


def filter_kernel(
    count_ref, links_ref, snap_ref, after_ref, before_ref, old_ref, oldgram_ref, s_ref, *rest
):
    chunk_refs, packed = rest[:SPREAD], rest[SPREAD]
    rows, planes, rows_y, rows_z = snap_ref.shape
    count = count_ref[0]
    join_low = links_ref[0, 0].astype(jnp.float32)
    join_high = links_ref[0, 1].astype(jnp.float32)
    z_from = lax.broadcasted_iota(jnp.int32, (rows_z, rows_z), 0)
    z_to = lax.broadcasted_iota(jnp.int32, (rows_z, rows_z), 1)
    gap = jnp.abs(z_from - z_to)
    smooth_z = jnp.where(gap == 0, 0.5, jnp.where(gap == 1, 0.25, 0.0))
    nothing = jnp.zeros((rows_z, rows_z), jnp.bfloat16)
    blocks = [[nothing] * planes for _ in range(planes + 2)]
    for p in range(planes):
        alive = jnp.where(p < count, 1.0, 0.0)
        is_last = jnp.where(p == count - 1, 1.0, 0.0)
        behind = alive * join_low if p == 0 else alive
        blocks[p][p] = (smooth_z * (0.25 * behind)).astype(jnp.bfloat16)
        blocks[p + 1][p] = (smooth_z * (0.5 * alive)).astype(jnp.bfloat16)
        if p < planes - 1:
            inner = 0.25 * alive * (1.0 - is_last)
            blocks[p + 2][p] = (smooth_z * inner).astype(jnp.bfloat16)
            blocks[planes + 1][p] = (smooth_z * (0.25 * is_last * join_high)).astype(jnp.bfloat16)
        else:
            blocks[planes + 1][p] = (smooth_z * (0.25 * alive * join_high)).astype(jnp.bfloat16)
    weights = jnp.concatenate([jnp.concatenate(line, axis=1) for line in blocks], axis=0)
    turn = turn_matrix(rows_y, 0.25)

    for group in range(rows // rows_y):
        at = slice(group * rows_y, (group + 1) * rows_y)
        snap = snap_ref[at]
        sources = [before_ref[at][:, 0]] + [snap[:, p] for p in range(planes)] + [after_ref[at][:, 0]]
        sources = [x.reshape(rows_y * rows_y, rows_z) for x in sources]
        field = jnp.dot(
            jnp.concatenate(sources, axis=1), weights, preferred_element_type=jnp.float32
        )
        high = field.astype(jnp.bfloat16)
        low = (field - high.astype(jnp.float32)).astype(jnp.bfloat16)
        turned = jnp.dot(turn, high, preferred_element_type=jnp.float32)
        turned = turned + jnp.dot(turn, low, preferred_element_type=jnp.float32)
        place(turned.astype(jnp.bfloat16), s_ref, rows_y, at)

    pairs = range(s_ref.shape[0])
    new_new = sum(nt_dot(s_ref[k], s_ref[k]) for k in pairs)
    new_old = sum(nt_dot(s_ref[k], old_ref[k]) for k in pairs)
    split = LANES - rows
    old_old = oldgram_ref[...]
    top = jnp.concatenate([new_new, new_old[:, :split]], axis=1)
    hidden = jnp.zeros((split, rows), jnp.float32)
    middle = jnp.concatenate([hidden, old_old[:split, :split]], axis=1)
    upper_left = jnp.concatenate([top, middle], axis=0)
    upper_right = jnp.concatenate([new_old[:, split:], old_old[:split, split:]], axis=0)
    lower_right = old_old[split:, split:]
    i = lax.broadcasted_iota(jnp.int32, (LANES, LANES), 0)
    j = lax.broadcasted_iota(jnp.int32, (LANES, LANES), 1)
    packed[:LANES, :] = jnp.where(j >= i, upper_left, lower_right)
    packed[LANES:2 * LANES, :] = upper_right
    packed[2 * LANES:, :] = jnp.zeros((packed.shape[0] - 2 * LANES, LANES), jnp.float32)
    packed[2 * LANES:2 * LANES + 1, :] = jnp.sum(
        jnp.where(i == j, lower_right, 0.0), axis=0, keepdims=True
    )
    share = lax.axis_index("blk") % SPREAD
    height = packed.shape[0] // SPREAD
    for flip in range(SPREAD):
        at = pl.multiple_of((share ^ flip) * height, SUBS)
        chunk_refs[flip][...] = packed[pl.ds(at, height), :]


def filtered_rows(snapshots, before, after, plane_counts, links, s_old, old_gram):
    rows, planes, rows_y, rows_z = snapshots.shape
    cells = planes * rows_y * rows_z
    order = rows + s_old.shape[1]
    height = packed_rows(order)
    smem = pl.BlockSpec(memory_space=pltpu.SMEM)
    vmem = pl.BlockSpec(memory_space=pltpu.VMEM)
    chunk = jax.ShapeDtypeStruct((height // SPREAD, LANES), jnp.float32)
    return pl.pallas_call(
        filter_kernel,
        out_shape=[jax.ShapeDtypeStruct((planes * rows_y // 2, rows, 2 * rows_z), jnp.bfloat16)] + [chunk] * SPREAD,
        in_specs=[smem, smem] + [vmem] * 5,
        out_specs=[vmem] * (1 + SPREAD),
        scratch_shapes=[pltpu.VMEM((height, LANES), jnp.float32)],
        compiler_params=pltpu.CompilerParams(vmem_limit_bytes=VMEM_BYTES),
        cost_estimate=pl.CostEstimate(
            flops=2 * rows * order * cells, bytes_accessed=2 * order * cells, transcendentals=0
        ),
        name="filter_gram",
    )(plane_counts, links, snapshots, after, before, s_old, old_gram)


def sum_chunks(chunks, axis):
    peers = lax.axis_size(axis)
    arrived = [chunks[0]] + [swap(chunks[d], axis, d) for d in range(1, SPREAD)]
    total = (arrived[0] + arrived[1]) + (arrived[2] + arrived[3])
    step = SPREAD
    while step < peers:
        if step * 4 <= peers:
            one, two, three = (swap(total, axis, d * step) for d in (1, 2, 3))
            total = (total + one) + (two + three)
            step *= 4
        else:
            total = total + swap(total, axis, step)
            step *= 2
    return [total] + [swap(total, axis, d) for d in range(1, SPREAD)]


def split_three(x):
    one = x.astype(jnp.bfloat16)
    rest = x - one.astype(jnp.float32)
    two = rest.astype(jnp.bfloat16)
    three = (rest - two.astype(jnp.float32)).astype(jnp.bfloat16)
    return one, two, three


LEFT = (0, 0, 0, 1, 1, 2)
RIGHT = (0, 1, 2, 0, 1, 0)


def small_factor(entry, count):
    unit = [[None] * count for _ in range(count)]
    recip = []
    for k in range(count):
        recip.append(1.0 / entry[k][k])
        for i in range(k + 1, count):
            unit[i][k] = entry[i][k] * recip[k]
        for j in range(k + 1, count):
            for i in range(j, count):
                if i == j:
                    part = (entry[i][k] * entry[i][k]) * recip[k]
                else:
                    part = unit[i][k] * entry[j][k]
                entry[i][j] = entry[i][j] - part
    return unit, recip


def pivots(cols):
    def spread(j, i):
        return jnp.broadcast_to(cols[j, i:i + 1, :], (SUBS, LANES))

    upper, recip = small_factor([[spread(j, i) for j in range(i + 1)] for i in range(HALF)], HALF)
    below = [cols[j, HALF:, :] for j in range(HALF)]
    for k in range(HALF):
        for j in range(k + 1, HALF):
            below[j] = below[j] - below[k] * upper[j][k]
    corner = [cols[j, HALF:, :] for j in range(HALF, PANEL)]
    for k in range(HALF):
        cols[k, HALF:, :] = below[k] * recip[k]
    left = [[spread(k, HALF + i) for k in range(HALF)] for i in range(HALF)]
    for j in range(HALF):
        for k in range(HALF):
            corner[j] = corner[j] - below[k] * left[j][k]
        cols[HALF + j, HALF:, :] = corner[j]
    entry = [[spread(HALF + j, HALF + i) for j in range(i + 1)] for i in range(HALF)]
    lower, more = small_factor(entry, HALF)
    unit = [row + [None] * HALF for row in upper] + [left[i] + lower[i] for i in range(HALF)]
    return unit, recip + more


def left_pieces(panel, t_ref, low, high):
    off = panel * PANEL % LANES
    block = t_ref[panel * PANEL // LANES, low:high, :]
    lane = lax.broadcasted_iota(jnp.int32, block.shape, 1)
    block = jnp.where((lane >= off) & (lane < off + PANEL), block, 0.0)
    pieces = [piece.astype(jnp.float32) for piece in split_three(block)]
    left = pieces[LEFT[0]]
    for k in range(1, len(LEFT)):
        left = left + pltpu.roll(pieces[LEFT[k]], k * PANEL, axis=1)
    return left.astype(jnp.bfloat16)


def right_pieces(panel, v):
    pieces = split_three(v)
    empty = jnp.zeros(v.shape, jnp.bfloat16)
    slots = [empty] * (LANES // PANEL)
    for k in range(len(RIGHT)):
        slots[(panel + k) % len(slots)] = pieces[RIGHT[k]]
    return jnp.concatenate(slots, axis=0)


def subtract(panel, t_ref, low, high, left, right):
    update = jnp.dot(left, right, preferred_element_type=jnp.float32)
    off = panel * PANEL % LANES
    for s in range(t_ref.shape[0]):
        held = t_ref[s, low:high, :]
        if s == panel * PANEL // LANES:
            lane = lax.broadcasted_iota(jnp.int32, held.shape, 1)
            held = jnp.where((lane >= off) & (lane < off + PANEL), 0.0, held)
        t_ref[s, low:high, :] = held - update[:, s * LANES:(s + 1) * LANES]


def factor_panel(panel, t_ref, f_ref, x_ref, cols, rows, late):
    tiles, order, _ = t_ref.shape
    first = panel * PANEL
    end = first + PANEL
    tile, off = first // LANES, first % LANES
    rows_in, rows_v, rows_w = (rows.at[panel % 2, k] for k in range(3))
    cols = cols.at[panel % 2]
    lane = lax.broadcasted_iota(jnp.int32, (PANEL, LANES), 1)
    sub = lax.broadcasted_iota(jnp.int32, (PANEL, LANES), 0)
    inside = (lane >= off) & (lane < off + PANEL)
    own = t_ref[tile, first:end, :]
    for j in range(PANEL):
        cols[j] = jnp.broadcast_to(own[:, off + j:off + j + 1], (PANEL, LANES))
    for s in range(tiles):
        block = t_ref[s, first:end, :]
        if s == tile:
            block = jnp.where(inside, jnp.where(lane - off == sub, 1.0, 0.0), block)
        rows_in[pl.ds(s, PANEL, stride=SUBS), :] = block
    rows_in[pl.ds(tiles, PANEL, stride=SUBS), :] = own
    y = [rows_in[i * SUBS:(i + 1) * SUBS, :] for i in range(PANEL)]
    late()
    near = min(end + PANEL, order)
    if end < order:
        left_near = left_pieces(panel, t_ref, end, near)
    if near < order:
        left_far = left_pieces(panel, t_ref, near, order)

    unit, recip = pivots(cols)
    for k in range(PANEL):
        for i in range(k + 1, PANEL):
            y[i] = y[i] - unit[i][k] * y[k]
    v = [recip[i] * y[i] for i in range(PANEL)]
    for j in reversed(range(PANEL)):
        for i in range(j):
            v[i] = v[i] - unit[j][i] * v[j]
    if end < order:
        for i in range(PANEL):
            rows_v[i * SUBS:(i + 1) * SUBS, :] = v[i]
        right = jnp.concatenate(
            [rows_v[pl.ds(s, PANEL, stride=SUBS), :] for s in range(tiles)], axis=1
        )
        right = right_pieces(panel, right)
        subtract(panel, t_ref, end, near, left_near, right)

    def rest():
        if near < order:
            subtract(panel, t_ref, near, order, left_far, right)

    def outputs():
        for i in range(PANEL):
            rows_w[i * SUBS:(i + 1) * SUBS, :] = jnp.sqrt(recip[i]) * y[i]
        zero = jnp.zeros((PANEL, LANES), jnp.float32)
        for s in range(tiles):
            span = slice(s * LANES, (s + 1) * LANES)
            part = rows_w[pl.ds(s, PANEL, stride=SUBS), :]
            if s == tile:
                whole = rows_w[pl.ds(tiles, PANEL, stride=SUBS), :]
                upper = jnp.where(inside, whole, part)
                f_ref[first:end, span] = jnp.where(lane >= off + sub, upper, 0.0)
                x_ref[first:end, span] = jnp.where(lane <= off + sub, part, 0.0)
            else:
                f_ref[first:end, span] = part if s > tile else zero
                x_ref[first:end, span] = part if s < tile else zero

    return rest, outputs


def factor_kernel(scale, *refs):
    sum_refs, refs = refs[:SPREAD], refs[SPREAD:]
    new_ref, old_ref, f_ref, out_ref, packed, t_ref, x_ref, cols, rows, *refs = refs
    x_pair, stack, mixed, staged, in_sem, out_sem = refs
    tiles, order, _ = t_ref.shape
    _, planes, rows_y, rows_z = out_ref.shape
    new_count = new_ref.shape[1]
    load_new = pltpu.make_async_copy(new_ref, stack.at[:, pl.ds(0, new_count)], in_sem.at[0])
    load_old = pltpu.make_async_copy(
        old_ref, stack.at[:, pl.ds(new_count, order - new_count)], in_sem.at[1]
    )
    load_new.start()
    load_old.start()
    share = lax.axis_index("blk") % SPREAD
    height = packed.shape[0] // SPREAD
    for flip in range(SPREAD):
        at = pl.multiple_of((share ^ flip) * height, SUBS)
        packed[pl.ds(at, height), :] = sum_refs[flip][...] * scale
    i = lax.broadcasted_iota(jnp.int32, (LANES, LANES), 0)
    j = lax.broadcasted_iota(jnp.int32, (LANES, LANES), 1)
    shared = packed[:LANES, :]
    right = packed[LANES:2 * LANES, :]
    upper = jnp.where(j >= i, shared, 0.0)
    lower = jnp.where(j < i, shared, 0.0)
    diagonal = packed[2 * LANES:2 * LANES + 1, :]
    t_ref[0, :LANES, :] = jnp.where(j >= i, shared, upper.T)
    t_ref[1, :LANES, :] = right
    t_ref[0, LANES:, :] = right.T
    corner = jnp.where(j < i, shared, lower.T)
    t_ref[1, LANES:, :] = jnp.where(i == j, diagonal, corner)
    rows[...] = jnp.zeros(rows.shape, jnp.float32)

    turn = turn_matrix(rows_y, 0.0)
    steps = rows_y // 2
    per_group = GROUP // PANEL
    pairs = planes * steps
    per_panel = pairs // per_group

    def split_rows(group):
        rows_here = x_ref[group * GROUP:(group + 1) * GROUP, :]
        high = rows_here.astype(jnp.bfloat16)
        x_pair[group % 2, :GROUP, :] = high
        x_pair[group % 2, GROUP:, :] = (rows_here - high.astype(jnp.float32)).astype(jnp.bfloat16)

    def multiply(group, pair):
        depth = (group + 1) * GROUP
        sums = jnp.dot(
            x_pair[group % 2, :, :depth], stack[pair, :depth, :], preferred_element_type=jnp.float32
        )
        sums = (sums[:GROUP] + sums[GROUP:]).astype(jnp.bfloat16)
        sums = sums.reshape(GROUP // rows_y, rows_y, 2 * rows_z)
        some = slice(group * GROUP // rows_y, (group + 1) * GROUP // rows_y)
        for half in (0, 1):
            y = 2 * (pair % steps) + half
            at = slice(y * rows_y, (y + 1) * rows_y)
            mixed[pair // steps, some, at, :] = sums[:, :, half * rows_z:(half + 1) * rows_z]

    def store(some):
        at = pl.ds(some * rows_y, rows_y)
        return pltpu.make_async_copy(staged.at[at], out_ref.at[at], out_sem.at[some])

    def finish(some):
        block = jnp.concatenate([mixed[plane, some] for plane in range(planes)], axis=1)
        turned = jnp.dot(turn, block, preferred_element_type=jnp.float32).astype(jnp.bfloat16)
        for plane in range(planes):
            part = turned[:, plane * rows_z:(plane + 1) * rows_z]
            staged[some * rows_y:(some + 1) * rows_y, plane] = part.reshape(rows_y, rows_y, rows_z)
        store(some).start()

    groups = order // GROUP
    blocks = GROUP // rows_y

    def nothing():
        pass

    late, outputs = nothing, nothing
    for group in range(groups):
        if group == 1:
            load_new.wait()
            load_old.wait()
        for step in range(per_group):
            panel = group * per_group + step
            before = outputs
            late, outputs = factor_panel(panel, t_ref, f_ref, x_ref, cols, rows, late)
            before()
            if group > 0:
                if step == 0:
                    split_rows(group - 1)
                for k in range(per_panel):
                    multiply(group - 1, step * per_panel + k)
            if group > 1:
                finish((group - 2) * blocks + step)
    outputs()
    split_rows(groups - 1)
    for k in range(blocks):
        finish((groups - 2) * blocks + k)
    for pair in range(pairs):
        multiply(groups - 1, pair)
    for k in range(blocks):
        finish((groups - 1) * blocks + k)

    for some in range(order // rows_y):
        store(some).wait()


def factor_and_modes(sums, s_new, s_old, shape, cell_total):
    order, planes, rows_y, rows_z = shape
    height = sums[0].shape[0] * SPREAD
    vmem = pl.BlockSpec(memory_space=pltpu.VMEM)
    hbm = pl.BlockSpec(memory_space=pl.ANY)
    square = (order, order)
    pairs = planes * rows_y // 2
    return pl.pallas_call(
        functools.partial(factor_kernel, 1.0 / cell_total),
        out_shape=[
            jax.ShapeDtypeStruct(square, jnp.float32),
            jax.ShapeDtypeStruct(shape, jnp.bfloat16),
        ],
        in_specs=[vmem] * SPREAD + [hbm, hbm],
        out_specs=[vmem, hbm],
        scratch_shapes=[
            pltpu.VMEM((height, LANES), jnp.float32),
            pltpu.VMEM((order // LANES, order, LANES), jnp.float32),
            pltpu.VMEM(square, jnp.float32),
            pltpu.VMEM((2, PANEL, PANEL, LANES), jnp.float32),
            pltpu.VMEM((2, 3, PANEL * SUBS, LANES), jnp.float32),
            pltpu.VMEM((2, 2 * GROUP, order), jnp.bfloat16),
            pltpu.VMEM((pairs, order, 2 * rows_z), jnp.bfloat16),
            pltpu.VMEM((planes, order // rows_y, rows_y * rows_y, rows_z), jnp.bfloat16),
            pltpu.VMEM(shape, jnp.bfloat16),
            pltpu.SemaphoreType.DMA((2,)),
            pltpu.SemaphoreType.DMA((order // rows_y,)),
        ],
        compiler_params=pltpu.CompilerParams(vmem_limit_bytes=VMEM_BYTES),
        name="factor",
    )(*sums, s_new, s_old)


def shards(snapshots, old_modes, mode_scales, plane_counts, links):
    new_count, planes, rows_y, rows_z = snapshots.shape
    order = new_count + old_modes.shape[0]
    peers = lax.axis_size("blk")
    up = [(i, (i + 1) % peers) for i in range(peers)]
    down = [(j, i) for i, j in up]
    first = lax.slice_in_dim(snapshots, 0, 1, axis=1)
    last = lax.dynamic_slice_in_dim(snapshots, plane_counts[0] - 1, 1, axis=1)
    before = lax.ppermute(last, "blk", up)
    after = lax.ppermute(first, "blk", down)
    s_old, old_gram = scaled_rows(old_modes, mode_scales, plane_counts)
    s_new, *chunks = filtered_rows(
        snapshots, before, after, plane_counts, links, s_old, old_gram
    )
    sums = sum_chunks(chunks, "blk")
    factor, modes = factor_and_modes(
        sums, s_new, s_old, (order, planes, rows_y, rows_z), peers * planes * rows_y * rows_z
    )
    return (modes, factor)


def solution(mesh):
    return jax.shard_map(
        shards,
        mesh=mesh,
        in_specs=(
            P(None, ("groups", "blk"), None, None),
            P(None, ("groups", "blk"), None, None),
            P("groups"),
            P(("groups", "blk")),
            P(("groups", "blk"), None),
        ),
        out_specs=(P(None, ("groups", "blk"), None, None), P("groups", None)),
        check_vma=False,
    )
```

```python
import functools

import jax
import jax.numpy as jnp
from jax import lax
from jax.experimental import pallas as pl
from jax.experimental.pallas import tpu as pltpu
from jax.sharding import PartitionSpec as P

PANEL = 16
HALF = 8
GROUP = 64
LANES = 128
SUBS = 8
SPREAD = 4
VMEM_BYTES = 40 * 1024 * 1024


def nt_dot(left_rows, right_rows):
    return lax.dot_general(
        left_rows, right_rows, (((1,), (1,)), ((), ())), preferred_element_type=jnp.float32
    )


def swap(x, axis, flip):
    peers = lax.axis_size(axis)
    return lax.ppermute(x, axis, [(i, i ^ flip) for i in range(peers)])


def turn_matrix(size, near):
    order = size * size
    row = lax.broadcasted_iota(jnp.int32, (order, order), 0)
    col = lax.broadcasted_iota(jnp.int32, (order, order), 1)
    same = row % size == col // size
    step = row // size - col % size
    weight = jnp.where(step == 0, 0.5 if near else 1.0, 0.0)
    if near:
        weight = jnp.where((step == 1) | (step == -1), near, weight)
    return jnp.where(same, weight, 0.0).astype(jnp.bfloat16)


def place(turned, s_ref, rows_y, at):
    for plane in range(turned.shape[1] // LANES):
        for y in range(rows_y):
            part = turned[y * rows_y:(y + 1) * rows_y, plane * LANES:(plane + 1) * LANES]
            half = (y % 2) * LANES
            s_ref[(plane * rows_y + y) // 2, at, half:half + LANES] = part


def edge_kernel(count_ref, snap_ref, first_ref, last_ref):
    rows, planes, rows_y, rows_z = snap_ref.shape
    count = count_ref[0]
    for row in range(rows):
        first_ref[row, 0] = snap_ref[row, 0]
        last = snap_ref[row, 0]
        for p in range(1, planes):
            last = jnp.where(count > p, snap_ref[row, p], last)
        last_ref[row, 0] = last


def edge_planes(snapshots, plane_counts):
    rows, _, rows_y, rows_z = snapshots.shape
    smem = pl.BlockSpec(memory_space=pltpu.SMEM)
    vmem = pl.BlockSpec(memory_space=pltpu.VMEM)
    plane = jax.ShapeDtypeStruct((rows, 1, rows_y, rows_z), jnp.bfloat16)
    return pl.pallas_call(
        edge_kernel,
        out_shape=[plane, plane],
        in_specs=[smem, vmem],
        out_specs=[vmem, vmem],
        compiler_params=pltpu.CompilerParams(vmem_limit_bytes=VMEM_BYTES),
        name="edges",
    )(plane_counts, snapshots)


def plane_weights(table_ref, planes, rows_z):
    count = table_ref[0]
    join_low = table_ref[1].astype(jnp.float32)
    join_high = table_ref[2].astype(jnp.float32)
    z_from = lax.broadcasted_iota(jnp.int32, (rows_z, rows_z), 0)
    z_to = lax.broadcasted_iota(jnp.int32, (rows_z, rows_z), 1)
    gap = jnp.abs(z_from - z_to)
    smooth_z = jnp.where(gap == 0, 0.5, jnp.where(gap == 1, 0.25, 0.0))
    inner = [[0.0] * planes for _ in range(planes)]
    outer = [[0.0] * planes for _ in range(2)]
    for p in range(planes):
        alive = jnp.where(p < count, 1.0, 0.0)
        is_last = jnp.where(p == count - 1, 1.0, 0.0)
        inner[p][p] = 0.5 * alive
        if p > 0:
            inner[p - 1][p] = 0.25 * alive
        else:
            outer[0][p] = 0.25 * alive * join_low
        if p < planes - 1:
            inner[p + 1][p] = 0.25 * alive * (1.0 - is_last)
        outer[1][p] = 0.25 * is_last * join_high

    def matrix(weights):
        lines = [[(smooth_z * w).astype(jnp.bfloat16) for w in line] for line in weights]
        return jnp.concatenate([jnp.concatenate(line, axis=1) for line in lines], axis=0)

    return matrix(inner), matrix(outer)


def smoothed(planes_by_lane, weights, turn):
    field = jnp.dot(planes_by_lane, weights, preferred_element_type=jnp.float32)
    high = field.astype(jnp.bfloat16)
    low = (field - high.astype(jnp.float32)).astype(jnp.bfloat16)
    turned = jnp.dot(turn, high, preferred_element_type=jnp.float32)
    return turned + jnp.dot(turn, low, preferred_element_type=jnp.float32)


def scale_kernel(
    table_ref, scales_ref, old_ref, snap_ref,
    s_ref, gram_ref, inner_ref, outer_ref, turn_ref,
):
    rows, planes, rows_y, rows_z = old_ref.shape
    turn = turn_matrix(rows_y, 0.0)
    plane = lax.broadcasted_iota(jnp.int32, (rows_y, planes * rows_z), 1) // rows_z
    alive = jnp.where(plane < table_ref[0], 1.0, 0.0)
    scales = []
    for low in range(0, rows, LANES):
        some = scales_ref[:, low:min(low + LANES, rows)]
        scales.append(jnp.broadcast_to(some, (LANES, some.shape[1])).T)
    scales = jnp.concatenate(scales, axis=0)
    scales = jnp.concatenate([scales] * planes, axis=1)

    for group in range(rows // rows_y):
        at = slice(group * rows_y, (group + 1) * rows_y)
        block = old_ref[at]
        block = jnp.concatenate(
            [block[:, p].reshape(rows_y * rows_y, rows_z) for p in range(planes)], axis=1
        )
        turned = jnp.dot(turn, block, preferred_element_type=jnp.float32)
        weight = scales[at] * alive
        turned = turned.reshape(rows_y, rows_y, planes * rows_z) * weight[None]
        turned = turned.reshape(rows_y * rows_y, planes * rows_z).astype(jnp.bfloat16)
        place(turned, s_ref, rows_y, at)

    gram_ref[...] = sum(nt_dot(s_ref[k], s_ref[k]) for k in range(s_ref.shape[0]))

    inner, outer = plane_weights(table_ref, planes, rows_z)
    turn = turn_matrix(rows_y, 0.25)
    outer_ref[...] = outer
    turn_ref[...] = turn
    for group in range(snap_ref.shape[0] // rows_y):
        snap = snap_ref[group * rows_y:(group + 1) * rows_y]
        sources = [snap[:, p].reshape(rows_y * rows_y, rows_z) for p in range(planes)]
        inner_ref[group] = smoothed(jnp.concatenate(sources, axis=1), inner, turn)


def prepared_rows(old_modes, snapshots, mode_scales, plane_counts, links):
    rows, planes, rows_y, rows_z = old_modes.shape
    table = jnp.concatenate([plane_counts, links.reshape(-1)])
    cells = planes * rows_y * rows_z
    groups = snapshots.shape[0] // rows_y
    square = rows_y * rows_y
    smem = pl.BlockSpec(memory_space=pltpu.SMEM)
    vmem = pl.BlockSpec(memory_space=pltpu.VMEM)
    return pl.pallas_call(
        scale_kernel,
        out_shape=[
            jax.ShapeDtypeStruct((planes * rows_y // 2, rows, 2 * rows_z), jnp.bfloat16),
            jax.ShapeDtypeStruct((rows, rows), jnp.float32),
            jax.ShapeDtypeStruct((groups, square, planes * rows_z), jnp.float32),
            jax.ShapeDtypeStruct((2 * rows_z, planes * rows_z), jnp.bfloat16),
            jax.ShapeDtypeStruct((square, square), jnp.bfloat16),
        ],
        in_specs=[smem, vmem, vmem, vmem],
        out_specs=[vmem] * 5,
        compiler_params=pltpu.CompilerParams(vmem_limit_bytes=VMEM_BYTES),
        cost_estimate=pl.CostEstimate(
            flops=2 * rows * rows * cells, bytes_accessed=8 * rows * cells, transcendentals=0
        ),
        name="prepare",
    )(table, mode_scales.reshape(1, rows), old_modes, snapshots)


def packed_rows(order):
    chunk = -(-(order + SUBS) // (SPREAD * SUBS)) * SUBS
    return SPREAD * chunk


def filter_kernel(
    before_ref, after_ref, inner_ref, outer_ref, turn_ref, old_ref, oldgram_ref, s_ref, *rest
):
    chunk_refs, packed = rest[:SPREAD], rest[SPREAD]
    rows, _, rows_y, rows_z = before_ref.shape
    for group in range(rows // rows_y):
        at = slice(group * rows_y, (group + 1) * rows_y)
        sources = [x[at][:, 0].reshape(rows_y * rows_y, rows_z) for x in (before_ref, after_ref)]
        halo = smoothed(jnp.concatenate(sources, axis=1), outer_ref[...], turn_ref[...])
        place((inner_ref[group] + halo).astype(jnp.bfloat16), s_ref, rows_y, at)

    pairs = range(s_ref.shape[0])
    new_new = sum(nt_dot(s_ref[k], s_ref[k]) for k in pairs)
    new_old = sum(nt_dot(s_ref[k], old_ref[k]) for k in pairs)
    split = LANES - rows
    old_old = oldgram_ref[...]
    top = jnp.concatenate([new_new, new_old[:, :split]], axis=1)
    hidden = jnp.zeros((split, rows), jnp.float32)
    middle = jnp.concatenate([hidden, old_old[:split, :split]], axis=1)
    upper_left = jnp.concatenate([top, middle], axis=0)
    upper_right = jnp.concatenate([new_old[:, split:], old_old[:split, split:]], axis=0)
    lower_right = old_old[split:, split:]
    i = lax.broadcasted_iota(jnp.int32, (LANES, LANES), 0)
    j = lax.broadcasted_iota(jnp.int32, (LANES, LANES), 1)
    packed[:LANES, :] = jnp.where(j >= i, upper_left, lower_right)
    packed[LANES:2 * LANES, :] = upper_right
    packed[2 * LANES:, :] = jnp.zeros((packed.shape[0] - 2 * LANES, LANES), jnp.float32)
    packed[2 * LANES:2 * LANES + 1, :] = jnp.sum(
        jnp.where(i == j, lower_right, 0.0), axis=0, keepdims=True
    )
    share = lax.axis_index("blk") % SPREAD
    height = packed.shape[0] // SPREAD
    for flip in range(SPREAD):
        at = pl.multiple_of((share ^ flip) * height, SUBS)
        chunk_refs[flip][...] = packed[pl.ds(at, height), :]


def filtered_rows(before, after, inner, outer, turn, s_old, old_gram):
    rows = before.shape[0]
    pairs, old_rows, lanes = s_old.shape
    order = rows + old_rows
    height = packed_rows(order)
    vmem = pl.BlockSpec(memory_space=pltpu.VMEM)
    chunk = jax.ShapeDtypeStruct((height // SPREAD, LANES), jnp.float32)
    return pl.pallas_call(
        filter_kernel,
        out_shape=[jax.ShapeDtypeStruct((pairs, rows, lanes), jnp.bfloat16)] + [chunk] * SPREAD,
        in_specs=[vmem] * 7,
        out_specs=[vmem] * (1 + SPREAD),
        scratch_shapes=[pltpu.VMEM((height, LANES), jnp.float32)],
        compiler_params=pltpu.CompilerParams(vmem_limit_bytes=VMEM_BYTES),
        cost_estimate=pl.CostEstimate(
            flops=2 * rows * order * pairs * lanes,
            bytes_accessed=2 * order * pairs * lanes,
            transcendentals=0,
        ),
        name="filter_gram",
    )(before, after, inner, outer, turn, s_old, old_gram)


def sum_chunks(chunks, axis):
    peers = lax.axis_size(axis)
    arrived = [chunks[0]] + [swap(chunks[d], axis, d) for d in range(1, SPREAD)]
    total = (arrived[0] + arrived[1]) + (arrived[2] + arrived[3])
    step = SPREAD
    while step < peers:
        if step * 4 <= peers:
            one, two, three = (swap(total, axis, d * step) for d in (1, 2, 3))
            total = (total + one) + (two + three)
            step *= 4
        else:
            total = total + swap(total, axis, step)
            step *= 2
    return [total] + [swap(total, axis, d) for d in range(1, SPREAD)]


def split_three(x):
    one = x.astype(jnp.bfloat16)
    rest = x - one.astype(jnp.float32)
    two = rest.astype(jnp.bfloat16)
    three = (rest - two.astype(jnp.float32)).astype(jnp.bfloat16)
    return one, two, three


LEFT = (0, 0, 0, 1, 1, 2)
RIGHT = (0, 1, 2, 0, 1, 0)


def small_factor(entry, count):
    unit = [[None] * count for _ in range(count)]
    recip = []
    for k in range(count):
        recip.append(1.0 / entry[k][k])
        for i in range(k + 1, count):
            unit[i][k] = entry[i][k] * recip[k]
        for j in range(k + 1, count):
            for i in range(j, count):
                if i == j:
                    part = (entry[i][k] * entry[i][k]) * recip[k]
                else:
                    part = unit[i][k] * entry[j][k]
                entry[i][j] = entry[i][j] - part
    return unit, recip


def pivots(cols):
    def spread(j, i):
        return jnp.broadcast_to(cols[j, i:i + 1, :], (SUBS, LANES))

    upper, recip = small_factor([[spread(j, i) for j in range(i + 1)] for i in range(HALF)], HALF)
    below = [cols[j, HALF:, :] for j in range(HALF)]
    for k in range(HALF):
        for j in range(k + 1, HALF):
            below[j] = below[j] - below[k] * upper[j][k]
    corner = [cols[j, HALF:, :] for j in range(HALF, PANEL)]
    for k in range(HALF):
        cols[k, HALF:, :] = below[k] * recip[k]
    left = [[spread(k, HALF + i) for k in range(HALF)] for i in range(HALF)]
    for j in range(HALF):
        for k in range(HALF):
            corner[j] = corner[j] - below[k] * left[j][k]
        cols[HALF + j, HALF:, :] = corner[j]
    entry = [[spread(HALF + j, HALF + i) for j in range(i + 1)] for i in range(HALF)]
    lower, more = small_factor(entry, HALF)
    unit = [row + [None] * HALF for row in upper] + [left[i] + lower[i] for i in range(HALF)]
    return unit, recip + more


def left_pieces(panel, t_ref, low, high):
    off = panel * PANEL % LANES
    block = t_ref[panel * PANEL // LANES, low:high, :]
    lane = lax.broadcasted_iota(jnp.int32, block.shape, 1)
    block = jnp.where((lane >= off) & (lane < off + PANEL), block, 0.0)
    pieces = [piece.astype(jnp.float32) for piece in split_three(block)]
    left = pieces[LEFT[0]]
    for k in range(1, len(LEFT)):
        left = left + pltpu.roll(pieces[LEFT[k]], k * PANEL, axis=1)
    return left.astype(jnp.bfloat16)


def right_pieces(panel, v):
    pieces = split_three(v)
    empty = jnp.zeros(v.shape, jnp.bfloat16)
    slots = [empty] * (LANES // PANEL)
    for k in range(len(RIGHT)):
        slots[(panel + k) % len(slots)] = pieces[RIGHT[k]]
    return jnp.concatenate(slots, axis=0)


def subtract(panel, t_ref, low, high, left, right):
    update = jnp.dot(left, right, preferred_element_type=jnp.float32)
    off = panel * PANEL % LANES
    for s in range(t_ref.shape[0]):
        held = t_ref[s, low:high, :]
        if s == panel * PANEL // LANES:
            lane = lax.broadcasted_iota(jnp.int32, held.shape, 1)
            held = jnp.where((lane >= off) & (lane < off + PANEL), 0.0, held)
        t_ref[s, low:high, :] = held - update[:, s * LANES:(s + 1) * LANES]


def factor_panel(panel, t_ref, f_ref, x_ref, cols, rows, late):
    tiles, order, _ = t_ref.shape
    first = panel * PANEL
    end = first + PANEL
    tile, off = first // LANES, first % LANES
    rows_in, rows_v, rows_w = (rows.at[panel % 2, k] for k in range(3))
    cols = cols.at[panel % 2]
    lane = lax.broadcasted_iota(jnp.int32, (PANEL, LANES), 1)
    sub = lax.broadcasted_iota(jnp.int32, (PANEL, LANES), 0)
    inside = (lane >= off) & (lane < off + PANEL)
    own = t_ref[tile, first:end, :]
    for j in range(PANEL):
        cols[j] = jnp.broadcast_to(own[:, off + j:off + j + 1], (PANEL, LANES))
    for s in range(tiles):
        block = t_ref[s, first:end, :]
        if s == tile:
            block = jnp.where(inside, jnp.where(lane - off == sub, 1.0, 0.0), block)
        rows_in[pl.ds(s, PANEL, stride=SUBS), :] = block
    rows_in[pl.ds(tiles, PANEL, stride=SUBS), :] = own
    y = [rows_in[i * SUBS:(i + 1) * SUBS, :] for i in range(PANEL)]
    late()
    near = min(end + PANEL, order)
    if end < order:
        left_near = left_pieces(panel, t_ref, end, near)
    if near < order:
        left_far = left_pieces(panel, t_ref, near, order)

    unit, recip = pivots(cols)
    for k in range(PANEL):
        for i in range(k + 1, PANEL):
            y[i] = y[i] - unit[i][k] * y[k]
    v = [recip[i] * y[i] for i in range(PANEL)]
    for j in reversed(range(PANEL)):
        for i in range(j):
            v[i] = v[i] - unit[j][i] * v[j]
    if end < order:
        for i in range(PANEL):
            rows_v[i * SUBS:(i + 1) * SUBS, :] = v[i]
        right = jnp.concatenate(
            [rows_v[pl.ds(s, PANEL, stride=SUBS), :] for s in range(tiles)], axis=1
        )
        right = right_pieces(panel, right)
        subtract(panel, t_ref, end, near, left_near, right)

    def rest():
        if near < order:
            subtract(panel, t_ref, near, order, left_far, right)

    def outputs():
        for i in range(PANEL):
            rows_w[i * SUBS:(i + 1) * SUBS, :] = jnp.sqrt(recip[i]) * y[i]
        zero = jnp.zeros((PANEL, LANES), jnp.float32)
        for s in range(tiles):
            span = slice(s * LANES, (s + 1) * LANES)
            part = rows_w[pl.ds(s, PANEL, stride=SUBS), :]
            if s == tile:
                whole = rows_w[pl.ds(tiles, PANEL, stride=SUBS), :]
                upper = jnp.where(inside, whole, part)
                f_ref[first:end, span] = jnp.where(lane >= off + sub, upper, 0.0)
                x_ref[first:end, span] = jnp.where(lane <= off + sub, part, 0.0)
            else:
                f_ref[first:end, span] = part if s > tile else zero
                x_ref[first:end, span] = part if s < tile else zero

    return rest, outputs


def factor_kernel(scale, *refs):
    sum_refs, refs = refs[:SPREAD], refs[SPREAD:]
    new_ref, old_ref, f_ref, out_ref, packed, t_ref, x_ref, cols, rows, *refs = refs
    x_pair, stack, mixed, staged, in_sem, out_sem = refs
    tiles, order, _ = t_ref.shape
    _, planes, rows_y, rows_z = out_ref.shape
    new_count = new_ref.shape[1]
    load_new = pltpu.make_async_copy(new_ref, stack.at[:, pl.ds(0, new_count)], in_sem.at[0])
    load_old = pltpu.make_async_copy(
        old_ref, stack.at[:, pl.ds(new_count, order - new_count)], in_sem.at[1]
    )
    load_new.start()
    load_old.start()
    share = lax.axis_index("blk") % SPREAD
    height = packed.shape[0] // SPREAD
    for flip in range(SPREAD):
        at = pl.multiple_of((share ^ flip) * height, SUBS)
        packed[pl.ds(at, height), :] = sum_refs[flip][...] * scale
    i = lax.broadcasted_iota(jnp.int32, (LANES, LANES), 0)
    j = lax.broadcasted_iota(jnp.int32, (LANES, LANES), 1)
    shared = packed[:LANES, :]
    right = packed[LANES:2 * LANES, :]
    upper = jnp.where(j >= i, shared, 0.0)
    lower = jnp.where(j < i, shared, 0.0)
    diagonal = packed[2 * LANES:2 * LANES + 1, :]
    t_ref[0, :LANES, :] = jnp.where(j >= i, shared, upper.T)
    t_ref[1, :LANES, :] = right
    t_ref[0, LANES:, :] = right.T
    corner = jnp.where(j < i, shared, lower.T)
    t_ref[1, LANES:, :] = jnp.where(i == j, diagonal, corner)
    rows[...] = jnp.zeros(rows.shape, jnp.float32)

    turn = turn_matrix(rows_y, 0.0)
    steps = rows_y // 2
    per_group = GROUP // PANEL
    pairs = planes * steps
    per_panel = pairs // per_group

    def split_rows(group):
        rows_here = x_ref[group * GROUP:(group + 1) * GROUP, :]
        high = rows_here.astype(jnp.bfloat16)
        x_pair[group % 2, :GROUP, :] = high
        x_pair[group % 2, GROUP:, :] = (rows_here - high.astype(jnp.float32)).astype(jnp.bfloat16)

    def multiply(group, pair):
        depth = (group + 1) * GROUP
        sums = jnp.dot(
            x_pair[group % 2, :, :depth], stack[pair, :depth, :], preferred_element_type=jnp.float32
        )
        sums = (sums[:GROUP] + sums[GROUP:]).astype(jnp.bfloat16)
        sums = sums.reshape(GROUP // rows_y, rows_y, 2 * rows_z)
        some = slice(group * GROUP // rows_y, (group + 1) * GROUP // rows_y)
        for half in (0, 1):
            y = 2 * (pair % steps) + half
            at = slice(y * rows_y, (y + 1) * rows_y)
            mixed[pair // steps, some, at, :] = sums[:, :, half * rows_z:(half + 1) * rows_z]

    def store(some):
        at = pl.ds(some * rows_y, rows_y)
        return pltpu.make_async_copy(staged.at[at], out_ref.at[at], out_sem.at[some])

    def finish(some):
        block = jnp.concatenate([mixed[plane, some] for plane in range(planes)], axis=1)
        turned = jnp.dot(turn, block, preferred_element_type=jnp.float32).astype(jnp.bfloat16)
        for plane in range(planes):
            part = turned[:, plane * rows_z:(plane + 1) * rows_z]
            staged[some * rows_y:(some + 1) * rows_y, plane] = part.reshape(rows_y, rows_y, rows_z)
        store(some).start()

    groups = order // GROUP
    blocks = GROUP // rows_y

    def nothing():
        pass

    late, outputs = nothing, nothing
    for group in range(groups):
        if group == 1:
            load_new.wait()
            load_old.wait()
        for step in range(per_group):
            panel = group * per_group + step
            before = outputs
            late, outputs = factor_panel(panel, t_ref, f_ref, x_ref, cols, rows, late)
            before()
            if group > 0:
                if step == 0:
                    split_rows(group - 1)
                for k in range(per_panel):
                    multiply(group - 1, step * per_panel + k)
            if group > 1:
                finish((group - 2) * blocks + step)
    outputs()
    split_rows(groups - 1)
    for k in range(blocks):
        finish((groups - 2) * blocks + k)
    for pair in range(pairs):
        multiply(groups - 1, pair)
    for k in range(blocks):
        finish((groups - 1) * blocks + k)

    for some in range(order // rows_y):
        store(some).wait()


def factor_and_modes(sums, s_new, s_old, shape, cell_total):
    order, planes, rows_y, rows_z = shape
    height = sums[0].shape[0] * SPREAD
    vmem = pl.BlockSpec(memory_space=pltpu.VMEM)
    hbm = pl.BlockSpec(memory_space=pl.ANY)
    square = (order, order)
    pairs = planes * rows_y // 2
    return pl.pallas_call(
        functools.partial(factor_kernel, 1.0 / cell_total),
        out_shape=[
            jax.ShapeDtypeStruct(square, jnp.float32),
            jax.ShapeDtypeStruct(shape, jnp.bfloat16),
        ],
        in_specs=[vmem] * SPREAD + [hbm, hbm],
        out_specs=[vmem, hbm],
        scratch_shapes=[
            pltpu.VMEM((height, LANES), jnp.float32),
            pltpu.VMEM((order // LANES, order, LANES), jnp.float32),
            pltpu.VMEM(square, jnp.float32),
            pltpu.VMEM((2, PANEL, PANEL, LANES), jnp.float32),
            pltpu.VMEM((2, 3, PANEL * SUBS, LANES), jnp.float32),
            pltpu.VMEM((2, 2 * GROUP, order), jnp.bfloat16),
            pltpu.VMEM((pairs, order, 2 * rows_z), jnp.bfloat16),
            pltpu.VMEM((planes, order // rows_y, rows_y * rows_y, rows_z), jnp.bfloat16),
            pltpu.VMEM(shape, jnp.bfloat16),
            pltpu.SemaphoreType.DMA((2,)),
            pltpu.SemaphoreType.DMA((order // rows_y,)),
        ],
        compiler_params=pltpu.CompilerParams(vmem_limit_bytes=VMEM_BYTES),
        name="factor",
    )(*sums, s_new, s_old)


def shards(snapshots, old_modes, mode_scales, plane_counts, links):
    new_count, planes, rows_y, rows_z = snapshots.shape
    order = new_count + old_modes.shape[0]
    peers = lax.axis_size("blk")
    up = [(i, (i + 1) % peers) for i in range(peers)]
    down = [(j, i) for i, j in up]
    first, last = edge_planes(snapshots, plane_counts)
    before = lax.ppermute(last, "blk", up)
    after = lax.ppermute(first, "blk", down)
    s_old, old_gram, inner, outer, turn = prepared_rows(
        old_modes, snapshots, mode_scales, plane_counts, links
    )
    s_new, *chunks = filtered_rows(before, after, inner, outer, turn, s_old, old_gram)
    sums = sum_chunks(chunks, "blk")
    factor, modes = factor_and_modes(
        sums, s_new, s_old, (order, planes, rows_y, rows_z), peers * planes * rows_y * rows_z
    )
    return (modes, factor)


def solution(mesh):
    return jax.shard_map(
        shards,
        mesh=mesh,
        in_specs=(
            P(None, ("groups", "blk"), None, None),
            P(None, ("groups", "blk"), None, None),
            P("groups"),
            P(("groups", "blk")),
            P(("groups", "blk"), None),
        ),
        out_specs=(P(None, ("groups", "blk"), None, None), P("groups", None)),
        check_vma=False,
    )
```

```python
import functools

import jax
import jax.numpy as jnp
from jax import lax
from jax.experimental import pallas as pl
from jax.experimental.pallas import tpu as pltpu
from jax.sharding import PartitionSpec as P

PANEL = 32
BLOCK = 8
GROUPS = (64, 64, 64, 32, 32)
LANES = 128
SUBS = 8
SPREAD = 4
VMEM_BYTES = 40 * 1024 * 1024


def nt_dot(left_rows, right_rows):
    return lax.dot_general(
        left_rows, right_rows, (((1,), (1,)), ((), ())), preferred_element_type=jnp.float32
    )


def swap(x, axis, flip):
    peers = lax.axis_size(axis)
    return lax.ppermute(x, axis, [(i, i ^ flip) for i in range(peers)])


def turn_matrix(size, near):
    order = size * size
    row = lax.broadcasted_iota(jnp.int32, (order, order), 0)
    col = lax.broadcasted_iota(jnp.int32, (order, order), 1)
    same = row % size == col // size
    step = row // size - col % size
    weight = jnp.where(step == 0, 0.5 if near else 1.0, 0.0)
    if near:
        weight = jnp.where((step == 1) | (step == -1), near, weight)
    return jnp.where(same, weight, 0.0).astype(jnp.bfloat16)


def place(turned, s_ref, rows_y, at):
    for plane in range(turned.shape[1] // LANES):
        for y in range(rows_y):
            part = turned[y * rows_y:(y + 1) * rows_y, plane * LANES:(plane + 1) * LANES]
            half = (y % 2) * LANES
            s_ref[(plane * rows_y + y) // 2, at, half:half + LANES] = part


def edge_kernel(count_ref, snap_ref, first_ref, last_ref):
    rows, planes, rows_y, rows_z = snap_ref.shape
    count = count_ref[0]
    for row in range(rows):
        first_ref[row, 0] = snap_ref[row, 0]
        last = snap_ref[row, 0]
        for p in range(1, planes):
            last = jnp.where(count > p, snap_ref[row, p], last)
        last_ref[row, 0] = last


def edge_planes(snapshots, plane_counts):
    rows, _, rows_y, rows_z = snapshots.shape
    smem = pl.BlockSpec(memory_space=pltpu.SMEM)
    vmem = pl.BlockSpec(memory_space=pltpu.VMEM)
    plane = jax.ShapeDtypeStruct((rows, 1, rows_y, rows_z), jnp.bfloat16)
    return pl.pallas_call(
        edge_kernel,
        out_shape=[plane, plane],
        in_specs=[smem, vmem],
        out_specs=[vmem, vmem],
        compiler_params=pltpu.CompilerParams(vmem_limit_bytes=VMEM_BYTES),
        name="edges",
    )(plane_counts, snapshots)


def plane_weights(table_ref, planes, rows_z):
    count = table_ref[0]
    join_low = table_ref[1].astype(jnp.float32)
    join_high = table_ref[2].astype(jnp.float32)
    z_from = lax.broadcasted_iota(jnp.int32, (rows_z, rows_z), 0)
    z_to = lax.broadcasted_iota(jnp.int32, (rows_z, rows_z), 1)
    gap = jnp.abs(z_from - z_to)
    smooth_z = jnp.where(gap == 0, 0.5, jnp.where(gap == 1, 0.25, 0.0))
    inner = [[0.0] * planes for _ in range(planes)]
    outer = [[0.0] * planes for _ in range(2)]
    for p in range(planes):
        alive = jnp.where(p < count, 1.0, 0.0)
        is_last = jnp.where(p == count - 1, 1.0, 0.0)
        inner[p][p] = 0.5 * alive
        if p > 0:
            inner[p - 1][p] = 0.25 * alive
        else:
            outer[0][p] = 0.25 * alive * join_low
        if p < planes - 1:
            inner[p + 1][p] = 0.25 * alive * (1.0 - is_last)
        outer[1][p] = 0.25 * is_last * join_high

    def matrix(weights):
        lines = [[(smooth_z * w).astype(jnp.bfloat16) for w in line] for line in weights]
        return jnp.concatenate([jnp.concatenate(line, axis=1) for line in lines], axis=0)

    return matrix(inner), matrix(outer)


def smoothed(planes_by_lane, weights, turn):
    field = jnp.dot(planes_by_lane, weights, preferred_element_type=jnp.float32)
    high = field.astype(jnp.bfloat16)
    low = (field - high.astype(jnp.float32)).astype(jnp.bfloat16)
    turned = jnp.dot(turn, high, preferred_element_type=jnp.float32)
    return turned + jnp.dot(turn, low, preferred_element_type=jnp.float32)


def scale_kernel(
    table_ref, scales_ref, old_ref, snap_ref,
    s_ref, gram_ref, inner_ref, outer_ref, turn_ref,
):
    rows, planes, rows_y, rows_z = old_ref.shape
    turn = turn_matrix(rows_y, 0.0)
    plane = lax.broadcasted_iota(jnp.int32, (rows_y, planes * rows_z), 1) // rows_z
    alive = jnp.where(plane < table_ref[0], 1.0, 0.0)
    scales = []
    for low in range(0, rows, LANES):
        some = scales_ref[:, low:min(low + LANES, rows)]
        scales.append(jnp.broadcast_to(some, (LANES, some.shape[1])).T)
    scales = jnp.concatenate(scales, axis=0)
    scales = jnp.concatenate([scales] * planes, axis=1)

    for group in range(rows // rows_y):
        at = slice(group * rows_y, (group + 1) * rows_y)
        block = old_ref[at]
        block = jnp.concatenate(
            [block[:, p].reshape(rows_y * rows_y, rows_z) for p in range(planes)], axis=1
        )
        turned = jnp.dot(turn, block, preferred_element_type=jnp.float32)
        weight = scales[at] * alive
        turned = turned.reshape(rows_y, rows_y, planes * rows_z) * weight[None]
        turned = turned.reshape(rows_y * rows_y, planes * rows_z).astype(jnp.bfloat16)
        place(turned, s_ref, rows_y, at)

    gram_ref[...] = sum(nt_dot(s_ref[k], s_ref[k]) for k in range(s_ref.shape[0]))

    inner, outer = plane_weights(table_ref, planes, rows_z)
    turn = turn_matrix(rows_y, 0.25)
    outer_ref[...] = outer
    turn_ref[...] = turn
    for group in range(snap_ref.shape[0] // rows_y):
        snap = snap_ref[group * rows_y:(group + 1) * rows_y]
        sources = [snap[:, p].reshape(rows_y * rows_y, rows_z) for p in range(planes)]
        inner_ref[group] = smoothed(jnp.concatenate(sources, axis=1), inner, turn)


def prepared_rows(old_modes, snapshots, mode_scales, plane_counts, links):
    rows, planes, rows_y, rows_z = old_modes.shape
    table = jnp.concatenate([plane_counts, links.reshape(-1)])
    cells = planes * rows_y * rows_z
    groups = snapshots.shape[0] // rows_y
    square = rows_y * rows_y
    smem = pl.BlockSpec(memory_space=pltpu.SMEM)
    vmem = pl.BlockSpec(memory_space=pltpu.VMEM)
    return pl.pallas_call(
        scale_kernel,
        out_shape=[
            jax.ShapeDtypeStruct((planes * rows_y // 2, rows, 2 * rows_z), jnp.bfloat16),
            jax.ShapeDtypeStruct((rows, rows), jnp.float32),
            jax.ShapeDtypeStruct((groups, square, planes * rows_z), jnp.float32),
            jax.ShapeDtypeStruct((2 * rows_z, planes * rows_z), jnp.bfloat16),
            jax.ShapeDtypeStruct((square, square), jnp.bfloat16),
        ],
        in_specs=[smem, vmem, vmem, vmem],
        out_specs=[vmem] * 5,
        compiler_params=pltpu.CompilerParams(vmem_limit_bytes=VMEM_BYTES),
        cost_estimate=pl.CostEstimate(
            flops=2 * rows * rows * cells, bytes_accessed=8 * rows * cells, transcendentals=0
        ),
        name="prepare",
    )(table, mode_scales.reshape(1, rows), old_modes, snapshots)


def packed_rows(order):
    chunk = -(-(order + SUBS) // (SPREAD * SUBS)) * SUBS
    return SPREAD * chunk


def filter_kernel(
    before_ref, after_ref, inner_ref, outer_ref, turn_ref, old_ref, oldgram_ref, s_ref, *rest
):
    chunk_refs, packed = rest[SPREAD - 1::-1], rest[SPREAD]
    rows, _, rows_y, rows_z = before_ref.shape
    for group in range(rows // rows_y):
        at = slice(group * rows_y, (group + 1) * rows_y)
        sources = [x[at][:, 0].reshape(rows_y * rows_y, rows_z) for x in (before_ref, after_ref)]
        halo = smoothed(jnp.concatenate(sources, axis=1), outer_ref[...], turn_ref[...])
        place((inner_ref[group] + halo).astype(jnp.bfloat16), s_ref, rows_y, at)

    pairs = range(s_ref.shape[0])
    new_new = sum(nt_dot(s_ref[k], s_ref[k]) for k in pairs)
    new_old = sum(nt_dot(s_ref[k], old_ref[k]) for k in pairs)
    split = LANES - rows
    old_old = oldgram_ref[...]
    top = jnp.concatenate([new_new, new_old[:, :split]], axis=1)
    hidden = jnp.zeros((split, rows), jnp.float32)
    middle = jnp.concatenate([hidden, old_old[:split, :split]], axis=1)
    upper_left = jnp.concatenate([top, middle], axis=0)
    upper_right = jnp.concatenate([new_old[:, split:], old_old[:split, split:]], axis=0)
    lower_right = old_old[split:, split:]
    i = lax.broadcasted_iota(jnp.int32, (LANES, LANES), 0)
    j = lax.broadcasted_iota(jnp.int32, (LANES, LANES), 1)
    packed[:LANES, :] = jnp.where(j >= i, upper_left, lower_right)
    packed[LANES:2 * LANES, :] = upper_right
    packed[2 * LANES:, :] = jnp.zeros((packed.shape[0] - 2 * LANES, LANES), jnp.float32)
    packed[2 * LANES:2 * LANES + 1, :] = jnp.sum(
        jnp.where(i == j, lower_right, 0.0), axis=0, keepdims=True
    )
    share = lax.axis_index("blk") % SPREAD
    height = packed.shape[0] // SPREAD
    for flip in range(SPREAD):
        at = pl.multiple_of((share ^ flip) * height, SUBS)
        chunk_refs[flip][...] = packed[pl.ds(at, height), :]


def filtered_rows(before, after, inner, outer, turn, s_old, old_gram):
    rows = before.shape[0]
    pairs, old_rows, lanes = s_old.shape
    order = rows + old_rows
    height = packed_rows(order)
    vmem = pl.BlockSpec(memory_space=pltpu.VMEM)
    chunk = jax.ShapeDtypeStruct((height // SPREAD, LANES), jnp.float32)
    return pl.pallas_call(
        filter_kernel,
        out_shape=[jax.ShapeDtypeStruct((pairs, rows, lanes), jnp.bfloat16)] + [chunk] * SPREAD,
        in_specs=[vmem] * 7,
        out_specs=[vmem] * (1 + SPREAD),
        scratch_shapes=[pltpu.VMEM((height, LANES), jnp.float32)],
        compiler_params=pltpu.CompilerParams(vmem_limit_bytes=VMEM_BYTES),
        cost_estimate=pl.CostEstimate(
            flops=2 * rows * order * pairs * lanes,
            bytes_accessed=2 * order * pairs * lanes,
            transcendentals=0,
        ),
        name="filter_gram",
    )(before, after, inner, outer, turn, s_old, old_gram)


def sum_chunks(chunks, axis):
    peers = lax.axis_size(axis)
    arrived = [chunks[0]] + [swap(chunks[d], axis, d) for d in range(1, SPREAD)]
    total = (arrived[0] + arrived[1]) + (arrived[2] + arrived[3])
    step = SPREAD
    while step < peers:
        if step * 4 <= peers:
            one, two, three = (swap(total, axis, d * step) for d in (1, 2, 3))
            total = (total + one) + (two + three)
            step *= 4
        else:
            total = total + swap(total, axis, step)
            step *= 2
    return [total] + [swap(total, axis, d) for d in range(1, SPREAD)]


def split_three(x):
    one = x.astype(jnp.bfloat16)
    rest = x - one.astype(jnp.float32)
    two = rest.astype(jnp.bfloat16)
    three = (rest - two.astype(jnp.float32)).astype(jnp.bfloat16)
    return one, two, three


LEFT = (0, 0, 0, 1, 1, 2)
RIGHT = (0, 1, 2, 0, 1, 0)


def small_factor(entry, count):
    unit = [[None] * count for _ in range(count)]
    recip = []
    for k in range(count):
        recip.append(1.0 / entry[k][k])
        for i in range(k + 1, count):
            unit[i][k] = entry[i][k] * recip[k]
        for j in range(k + 1, count):
            for i in range(j, count):
                if i == j:
                    part = (entry[i][k] * entry[i][k]) * recip[k]
                else:
                    part = unit[i][k] * entry[j][k]
                entry[i][j] = entry[i][j] - part
    return unit, recip


def pivots(cols):
    def spread(j, i):
        return jnp.broadcast_to(cols[j, i:i + 1, :], (SUBS, LANES))

    unit = [[] for _ in range(PANEL)]
    recip = []
    open_cols = [cols[j, j // BLOCK * BLOCK:, :] for j in range(PANEL)]
    for first in range(0, PANEL, BLOCK):
        end = first + BLOCK
        if first:
            for j in range(first, end):
                cols[j, first:, :] = open_cols[j]
        entry = [[spread(first + j, first + i) for j in range(i + 1)] for i in range(BLOCK)]
        upper, some = small_factor(entry, BLOCK)
        recip += some
        for i in range(BLOCK):
            unit[first + i] += upper[i]
        if end == PANEL:
            break
        below = [open_cols[j][BLOCK:] for j in range(first, end)]
        count = PANEL - end
        for k in range(BLOCK):
            for j in range(k + 1, BLOCK):
                below[j] = below[j] - below[k] * jnp.tile(upper[j][k], (count // SUBS, 1))
        for k in range(BLOCK):
            cols[first + k, end:, :] = below[k] * jnp.tile(some[k], (count // SUBS, 1))
        for i in range(end, PANEL):
            unit[i] += [spread(first + k, i) for k in range(BLOCK)]
        for j in range(end, PANEL):
            skip = j // BLOCK * BLOCK - end
            height = (count - skip) // SUBS
            for k in range(BLOCK):
                part = below[k][skip:] * jnp.tile(unit[j][first + k], (height, 1))
                open_cols[j] = open_cols[j] - part
    return unit, recip


def left_pieces(panel, t_ref, low, high):
    off = panel * PANEL % LANES
    block = t_ref[panel * PANEL // LANES, low:high, :]
    lane = lax.broadcasted_iota(jnp.int32, block.shape, 1)
    block = jnp.where((lane >= off) & (lane < off + PANEL), block, 0.0)
    pieces = [piece.astype(jnp.float32) for piece in split_three(block)]
    slots = LANES // PANEL
    left = []
    for k in range(len(LEFT)):
        piece = pieces[LEFT[k]]
        if k % slots:
            left[-1] = left[-1] + pltpu.roll(piece, k % slots * PANEL, axis=1)
        else:
            left.append(piece)
    return jnp.concatenate(left, axis=1).astype(jnp.bfloat16)


def right_pieces(panel, v):
    pieces = split_three(v)
    empty = jnp.zeros(v.shape, jnp.bfloat16)
    slots = LANES // PANEL
    right = [empty] * (-(-len(RIGHT) // slots) * slots)
    for k in range(len(RIGHT)):
        right[k // slots * slots + (panel + k) % slots] = pieces[RIGHT[k]]
    return jnp.concatenate(right, axis=0)


def subtract(panel, t_ref, low, high, left, right):
    update = jnp.dot(left, right, preferred_element_type=jnp.float32)
    off = panel * PANEL % LANES
    for s in range(t_ref.shape[0]):
        held = t_ref[s, low:high, :]
        if s == panel * PANEL // LANES:
            lane = lax.broadcasted_iota(jnp.int32, held.shape, 1)
            held = jnp.where((lane >= off) & (lane < off + PANEL), 0.0, held)
        t_ref[s, low:high, :] = held - update[:, s * LANES:(s + 1) * LANES]


def factor_panel(panel, t_ref, f_ref, x_ref, cols, rows, late):
    tiles, order, _ = t_ref.shape
    first = panel * PANEL
    end = first + PANEL
    tile, off = first // LANES, first % LANES
    rows_in, rows_v, rows_w = (rows.at[panel % 2, k] for k in range(3))
    cols = cols.at[panel % 2]
    lane = lax.broadcasted_iota(jnp.int32, (PANEL, LANES), 1)
    sub = lax.broadcasted_iota(jnp.int32, (PANEL, LANES), 0)
    inside = (lane >= off) & (lane < off + PANEL)
    own = t_ref[tile, first:end, :]
    for j in range(PANEL):
        cols[j] = jnp.broadcast_to(own[:, off + j:off + j + 1], (PANEL, LANES))
    for s in range(tiles):
        block = t_ref[s, first:end, :]
        if s == tile:
            block = jnp.where(inside, jnp.where(lane - off == sub, 1.0, 0.0), block)
        rows_in[pl.ds(s, PANEL, stride=SUBS), :] = block
    rows_in[pl.ds(tiles, PANEL, stride=SUBS), :] = own
    y = [rows_in[i * SUBS:(i + 1) * SUBS, :] for i in range(PANEL)]
    late()
    near = min(end + PANEL, order)
    if end < order:
        left_near = left_pieces(panel, t_ref, end, near)
    if near < order:
        left_far = left_pieces(panel, t_ref, near, order)

    unit, recip = pivots(cols)
    for k in range(PANEL):
        for i in range(k + 1, PANEL):
            y[i] = y[i] - unit[i][k] * y[k]
    v = [recip[i] * y[i] for i in range(PANEL)]
    for j in reversed(range(PANEL)):
        for i in range(j):
            v[i] = v[i] - unit[j][i] * v[j]
    if end < order:
        for i in range(PANEL):
            rows_v[i * SUBS:(i + 1) * SUBS, :] = v[i]
        right = jnp.concatenate(
            [rows_v[pl.ds(s, PANEL, stride=SUBS), :] for s in range(tiles)], axis=1
        )
        right = right_pieces(panel, right)
        subtract(panel, t_ref, end, near, left_near, right)

    def rest():
        if near < order:
            subtract(panel, t_ref, near, order, left_far, right)

    def outputs():
        for i in range(PANEL):
            rows_w[i * SUBS:(i + 1) * SUBS, :] = jnp.sqrt(recip[i]) * y[i]
        zero = jnp.zeros((PANEL, LANES), jnp.float32)
        for s in range(tiles):
            span = slice(s * LANES, (s + 1) * LANES)
            part = rows_w[pl.ds(s, PANEL, stride=SUBS), :]
            if s == tile:
                whole = rows_w[pl.ds(tiles, PANEL, stride=SUBS), :]
                upper = jnp.where(inside, whole, part)
                f_ref[first:end, span] = jnp.where(lane >= off + sub, upper, 0.0)
                x_ref[first:end, span] = jnp.where(lane <= off + sub, part, 0.0)
            else:
                f_ref[first:end, span] = part if s > tile else zero
                x_ref[first:end, span] = part if s < tile else zero

    return rest, outputs


def factor_kernel(scale, *refs):
    sum_refs, refs = refs[:SPREAD], refs[SPREAD:]
    new_ref, old_ref, f_ref, out_ref, packed, t_ref, x_ref, cols, rows, *refs = refs
    x_pair, stack, mixed, staged, in_sem, out_sem = refs
    tiles, order, _ = t_ref.shape
    _, planes, rows_y, rows_z = out_ref.shape
    new_count = new_ref.shape[1]
    load_new = pltpu.make_async_copy(new_ref, stack.at[:, pl.ds(0, new_count)], in_sem.at[0])
    load_old = pltpu.make_async_copy(
        old_ref, stack.at[:, pl.ds(new_count, order - new_count)], in_sem.at[1]
    )
    load_new.start()
    load_old.start()
    share = lax.axis_index("blk") % SPREAD
    height = packed.shape[0] // SPREAD
    for flip in range(SPREAD):
        at = pl.multiple_of((share ^ flip) * height, SUBS)
        packed[pl.ds(at, height), :] = sum_refs[flip][...] * scale
    i = lax.broadcasted_iota(jnp.int32, (LANES, LANES), 0)
    j = lax.broadcasted_iota(jnp.int32, (LANES, LANES), 1)
    shared = packed[:LANES, :]
    right = packed[LANES:2 * LANES, :]
    upper = jnp.where(j >= i, shared, 0.0)
    lower = jnp.where(j < i, shared, 0.0)
    diagonal = packed[2 * LANES:2 * LANES + 1, :]
    t_ref[0, :LANES, :] = jnp.where(j >= i, shared, upper.T)
    t_ref[1, :LANES, :] = right
    t_ref[0, LANES:, :] = right.T
    corner = jnp.where(j < i, shared, lower.T)
    t_ref[1, LANES:, :] = jnp.where(i == j, diagonal, corner)
    rows[...] = jnp.zeros(rows.shape, jnp.float32)

    turn = turn_matrix(rows_y, 0.0)
    steps = rows_y // 2
    pairs = planes * steps
    starts = [sum(GROUPS[:k]) for k in range(len(GROUPS))]

    def split_rows(group):
        size = GROUPS[group]
        rows_here = x_ref[starts[group]:starts[group] + size, :]
        high = rows_here.astype(jnp.bfloat16)
        x_pair[group, :size, :] = high
        x_pair[group, size:2 * size, :] = (rows_here - high.astype(jnp.float32)).astype(jnp.bfloat16)

    def multiply(group, pair):
        size = GROUPS[group]
        depth = starts[group] + size
        sums = jnp.dot(
            x_pair[group, :2 * size, :depth],
            stack[pair, :depth, :],
            preferred_element_type=jnp.float32,
        )
        sums = (sums[:size] + sums[size:]).astype(jnp.bfloat16)
        sums = sums.reshape(size // rows_y, rows_y, 2 * rows_z)
        some = slice(starts[group] // rows_y, depth // rows_y)
        for half in (0, 1):
            y = 2 * (pair % steps) + half
            at = slice(y * rows_y, (y + 1) * rows_y)
            mixed[pair // steps, some, at, :] = sums[:, :, half * rows_z:(half + 1) * rows_z]

    def store(some):
        at = pl.ds(some * rows_y, rows_y)
        return pltpu.make_async_copy(staged.at[at], out_ref.at[at], out_sem.at[some])

    def finish(some):
        block = jnp.concatenate([mixed[plane, some] for plane in range(planes)], axis=1)
        turned = jnp.dot(turn, block, preferred_element_type=jnp.float32).astype(jnp.bfloat16)
        for plane in range(planes):
            part = turned[:, plane * rows_z:(plane + 1) * rows_z]
            staged[some * rows_y:(some + 1) * rows_y, plane] = part.reshape(rows_y, rows_y, rows_z)
        store(some).start()

    def nothing():
        pass

    late, outputs = nothing, nothing
    for group in range(len(GROUPS)):
        if group == 1:
            load_new.wait()
            load_old.wait()
        panels = GROUPS[group] // PANEL
        for step in range(panels):
            panel = starts[group] // PANEL + step
            before = outputs
            late, outputs = factor_panel(panel, t_ref, f_ref, x_ref, cols, rows, late)
            before()
            if group > 0:
                if step == 0:
                    split_rows(group - 1)
                for pair in range(step * pairs // panels, (step + 1) * pairs // panels):
                    multiply(group - 1, pair)
            if group > 1 and step == 0:
                for some in range(starts[group - 2] // rows_y, starts[group - 1] // rows_y):
                    finish(some)
    outputs()
    last = len(GROUPS) - 1
    split_rows(last)
    for some in range(starts[last - 1] // rows_y, starts[last] // rows_y):
        finish(some)
    for pair in range(pairs):
        multiply(last, pair)
    for some in range(starts[last] // rows_y, order // rows_y):
        finish(some)

    for some in range(order // rows_y):
        store(some).wait()


def factor_and_modes(sums, s_new, s_old, shape, cell_total):
    order, planes, rows_y, rows_z = shape
    height = sums[0].shape[0] * SPREAD
    vmem = pl.BlockSpec(memory_space=pltpu.VMEM)
    hbm = pl.BlockSpec(memory_space=pl.ANY)
    square = (order, order)
    pairs = planes * rows_y // 2
    return pl.pallas_call(
        functools.partial(factor_kernel, 1.0 / cell_total),
        out_shape=[
            jax.ShapeDtypeStruct(square, jnp.float32),
            jax.ShapeDtypeStruct(shape, jnp.bfloat16),
        ],
        in_specs=[vmem] * SPREAD + [hbm, hbm],
        out_specs=[vmem, hbm],
        scratch_shapes=[
            pltpu.VMEM((height, LANES), jnp.float32),
            pltpu.VMEM((order // LANES, order, LANES), jnp.float32),
            pltpu.VMEM(square, jnp.float32),
            pltpu.VMEM((2, PANEL, PANEL, LANES), jnp.float32),
            pltpu.VMEM((2, 3, PANEL * SUBS, LANES), jnp.float32),
            pltpu.VMEM((len(GROUPS), 2 * max(GROUPS), order), jnp.bfloat16),
            pltpu.VMEM((pairs, order, 2 * rows_z), jnp.bfloat16),
            pltpu.VMEM((planes, order // rows_y, rows_y * rows_y, rows_z), jnp.bfloat16),
            pltpu.VMEM(shape, jnp.bfloat16),
            pltpu.SemaphoreType.DMA((2,)),
            pltpu.SemaphoreType.DMA((order // rows_y,)),
        ],
        compiler_params=pltpu.CompilerParams(vmem_limit_bytes=VMEM_BYTES),
        name="factor",
    )(*sums, s_new, s_old)


def shards(snapshots, old_modes, mode_scales, plane_counts, links):
    new_count, planes, rows_y, rows_z = snapshots.shape
    order = new_count + old_modes.shape[0]
    peers = lax.axis_size("blk")
    up = [(i, (i + 1) % peers) for i in range(peers)]
    down = [(j, i) for i, j in up]
    first, last = edge_planes(snapshots, plane_counts)
    before = lax.ppermute(last, "blk", up)
    after = lax.ppermute(first, "blk", down)
    s_old, old_gram, inner, outer, turn = prepared_rows(
        old_modes, snapshots, mode_scales, plane_counts, links
    )
    s_new, *chunks = filtered_rows(before, after, inner, outer, turn, s_old, old_gram)
    chunks = chunks[::-1]
    sums = sum_chunks(chunks, "blk")
    factor, modes = factor_and_modes(
        sums, s_new, s_old, (order, planes, rows_y, rows_z), peers * planes * rows_y * rows_z
    )
    return (modes, factor)


def solution(mesh):
    return jax.shard_map(
        shards,
        mesh=mesh,
        in_specs=(
            P(None, ("groups", "blk"), None, None),
            P(None, ("groups", "blk"), None, None),
            P("groups"),
            P(("groups", "blk")),
            P(("groups", "blk"), None),
        ),
        out_specs=(P(None, ("groups", "blk"), None, None), P("groups", None)),
        check_vma=False,
    )
```

```python
import functools

import jax
import jax.numpy as jnp
from jax import lax
from jax.experimental import pallas as pl
from jax.experimental.pallas import tpu as pltpu
from jax.sharding import PartitionSpec as P

PANEL = 16
HALF = 8
GROUPS = (64, 64, 64, 32, 32)
LANES = 128
SUBS = 8
SPREAD = 4
VMEM_BYTES = 40 * 1024 * 1024


def nt_dot(left_rows, right_rows):
    return lax.dot_general(
        left_rows, right_rows, (((1,), (1,)), ((), ())), preferred_element_type=jnp.float32
    )


def swap(x, axis, flip):
    peers = lax.axis_size(axis)
    return lax.ppermute(x, axis, [(i, i ^ flip) for i in range(peers)])


def turn_matrix(size, near):
    order = size * size
    row = lax.broadcasted_iota(jnp.int32, (order, order), 0)
    col = lax.broadcasted_iota(jnp.int32, (order, order), 1)
    same = row % size == col // size
    step = row // size - col % size
    weight = jnp.where(step == 0, 0.5 if near else 1.0, 0.0)
    if near:
        weight = jnp.where((step == 1) | (step == -1), near, weight)
    return jnp.where(same, weight, 0.0).astype(jnp.bfloat16)


def place(turned, s_ref, rows_y, at):
    for plane in range(turned.shape[1] // LANES):
        for y in range(rows_y):
            part = turned[y * rows_y:(y + 1) * rows_y, plane * LANES:(plane + 1) * LANES]
            half = (y % 2) * LANES
            s_ref[(plane * rows_y + y) // 2, at, half:half + LANES] = part


def edge_kernel(count_ref, snap_ref, first_ref, last_ref):
    rows, planes, rows_y, rows_z = snap_ref.shape
    count = count_ref[0]
    for row in range(rows):
        first_ref[row, 0] = snap_ref[row, 0]
        last = snap_ref[row, 0]
        for p in range(1, planes):
            last = jnp.where(count > p, snap_ref[row, p], last)
        last_ref[row, 0] = last


def edge_planes(snapshots, plane_counts):
    rows, _, rows_y, rows_z = snapshots.shape
    smem = pl.BlockSpec(memory_space=pltpu.SMEM)
    vmem = pl.BlockSpec(memory_space=pltpu.VMEM)
    plane = jax.ShapeDtypeStruct((rows, 1, rows_y, rows_z), jnp.bfloat16)
    return pl.pallas_call(
        edge_kernel,
        out_shape=[plane, plane],
        in_specs=[smem, vmem],
        out_specs=[vmem, vmem],
        compiler_params=pltpu.CompilerParams(vmem_limit_bytes=VMEM_BYTES),
        name="edges",
    )(plane_counts, snapshots)


def plane_weights(table_ref, planes, rows_z):
    count = table_ref[0]
    join_low = table_ref[1].astype(jnp.float32)
    join_high = table_ref[2].astype(jnp.float32)
    z_from = lax.broadcasted_iota(jnp.int32, (rows_z, rows_z), 0)
    z_to = lax.broadcasted_iota(jnp.int32, (rows_z, rows_z), 1)
    gap = jnp.abs(z_from - z_to)
    smooth_z = jnp.where(gap == 0, 0.5, jnp.where(gap == 1, 0.25, 0.0))
    inner = [[0.0] * planes for _ in range(planes)]
    outer = [[0.0] * planes for _ in range(2)]
    for p in range(planes):
        alive = jnp.where(p < count, 1.0, 0.0)
        is_last = jnp.where(p == count - 1, 1.0, 0.0)
        inner[p][p] = 0.5 * alive
        if p > 0:
            inner[p - 1][p] = 0.25 * alive
        else:
            outer[0][p] = 0.25 * alive * join_low
        if p < planes - 1:
            inner[p + 1][p] = 0.25 * alive * (1.0 - is_last)
        outer[1][p] = 0.25 * is_last * join_high

    def matrix(weights):
        lines = [[(smooth_z * w).astype(jnp.bfloat16) for w in line] for line in weights]
        return jnp.concatenate([jnp.concatenate(line, axis=1) for line in lines], axis=0)

    return matrix(inner), matrix(outer)


def smoothed(planes_by_lane, weights, turn):
    field = jnp.dot(planes_by_lane, weights, preferred_element_type=jnp.float32)
    high = field.astype(jnp.bfloat16)
    low = (field - high.astype(jnp.float32)).astype(jnp.bfloat16)
    turned = jnp.dot(turn, high, preferred_element_type=jnp.float32)
    return turned + jnp.dot(turn, low, preferred_element_type=jnp.float32)


def scale_kernel(
    table_ref, scales_ref, old_ref, snap_ref,
    s_ref, gram_ref, inner_ref, outer_ref, turn_ref,
):
    rows, planes, rows_y, rows_z = old_ref.shape
    turn = turn_matrix(rows_y, 0.0)
    plane = lax.broadcasted_iota(jnp.int32, (rows_y, planes * rows_z), 1) // rows_z
    alive = jnp.where(plane < table_ref[0], 1.0, 0.0)
    scales = []
    for low in range(0, rows, LANES):
        some = scales_ref[:, low:min(low + LANES, rows)]
        scales.append(jnp.broadcast_to(some, (LANES, some.shape[1])).T)
    scales = jnp.concatenate(scales, axis=0)
    scales = jnp.concatenate([scales] * planes, axis=1)

    for group in range(rows // rows_y):
        at = slice(group * rows_y, (group + 1) * rows_y)
        block = old_ref[at]
        block = jnp.concatenate(
            [block[:, p].reshape(rows_y * rows_y, rows_z) for p in range(planes)], axis=1
        )
        turned = jnp.dot(turn, block, preferred_element_type=jnp.float32)
        weight = scales[at] * alive
        turned = turned.reshape(rows_y, rows_y, planes * rows_z) * weight[None]
        turned = turned.reshape(rows_y * rows_y, planes * rows_z).astype(jnp.bfloat16)
        place(turned, s_ref, rows_y, at)

    gram_ref[...] = sum(nt_dot(s_ref[k], s_ref[k]) for k in range(s_ref.shape[0]))

    inner, outer = plane_weights(table_ref, planes, rows_z)
    turn = turn_matrix(rows_y, 0.25)
    outer_ref[...] = outer
    turn_ref[...] = turn
    for group in range(snap_ref.shape[0] // rows_y):
        snap = snap_ref[group * rows_y:(group + 1) * rows_y]
        sources = [snap[:, p].reshape(rows_y * rows_y, rows_z) for p in range(planes)]
        inner_ref[group] = smoothed(jnp.concatenate(sources, axis=1), inner, turn)


def prepared_rows(old_modes, snapshots, mode_scales, plane_counts, links):
    rows, planes, rows_y, rows_z = old_modes.shape
    table = jnp.concatenate([plane_counts, links.reshape(-1)])
    cells = planes * rows_y * rows_z
    groups = snapshots.shape[0] // rows_y
    square = rows_y * rows_y
    smem = pl.BlockSpec(memory_space=pltpu.SMEM)
    vmem = pl.BlockSpec(memory_space=pltpu.VMEM)
    return pl.pallas_call(
        scale_kernel,
        out_shape=[
            jax.ShapeDtypeStruct((planes * rows_y // 2, rows, 2 * rows_z), jnp.bfloat16),
            jax.ShapeDtypeStruct((rows, rows), jnp.float32),
            jax.ShapeDtypeStruct((groups, square, planes * rows_z), jnp.float32),
            jax.ShapeDtypeStruct((2 * rows_z, planes * rows_z), jnp.bfloat16),
            jax.ShapeDtypeStruct((square, square), jnp.bfloat16),
        ],
        in_specs=[smem, vmem, vmem, vmem],
        out_specs=[vmem] * 5,
        compiler_params=pltpu.CompilerParams(vmem_limit_bytes=VMEM_BYTES),
        cost_estimate=pl.CostEstimate(
            flops=2 * rows * rows * cells, bytes_accessed=8 * rows * cells, transcendentals=0
        ),
        name="prepare",
    )(table, mode_scales.reshape(1, rows), old_modes, snapshots)


def packed_rows(order):
    chunk = -(-(order + SUBS) // (SPREAD * SUBS)) * SUBS
    return SPREAD * chunk


def filter_kernel(
    before_ref, after_ref, inner_ref, outer_ref, turn_ref, old_ref, oldgram_ref, s_ref, *rest
):
    chunk_refs, packed = rest[:SPREAD], rest[SPREAD]
    rows, _, rows_y, rows_z = before_ref.shape
    for group in range(rows // rows_y):
        at = slice(group * rows_y, (group + 1) * rows_y)
        sources = [x[at][:, 0].reshape(rows_y * rows_y, rows_z) for x in (before_ref, after_ref)]
        halo = smoothed(jnp.concatenate(sources, axis=1), outer_ref[...], turn_ref[...])
        place((inner_ref[group] + halo).astype(jnp.bfloat16), s_ref, rows_y, at)

    pairs = range(s_ref.shape[0])
    new_new = sum(nt_dot(s_ref[k], s_ref[k]) for k in pairs)
    new_old = sum(nt_dot(s_ref[k], old_ref[k]) for k in pairs)
    split = LANES - rows
    old_old = oldgram_ref[...]
    top = jnp.concatenate([new_new, new_old[:, :split]], axis=1)
    hidden = jnp.zeros((split, rows), jnp.float32)
    middle = jnp.concatenate([hidden, old_old[:split, :split]], axis=1)
    upper_left = jnp.concatenate([top, middle], axis=0)
    upper_right = jnp.concatenate([new_old[:, split:], old_old[:split, split:]], axis=0)
    lower_right = old_old[split:, split:]
    i = lax.broadcasted_iota(jnp.int32, (LANES, LANES), 0)
    j = lax.broadcasted_iota(jnp.int32, (LANES, LANES), 1)
    packed[:LANES, :] = jnp.where(j >= i, upper_left, lower_right)
    packed[LANES:2 * LANES, :] = upper_right
    packed[2 * LANES:, :] = jnp.zeros((packed.shape[0] - 2 * LANES, LANES), jnp.float32)
    packed[2 * LANES:2 * LANES + 1, :] = jnp.sum(
        jnp.where(i == j, lower_right, 0.0), axis=0, keepdims=True
    )
    share = lax.axis_index("blk") % SPREAD
    height = packed.shape[0] // SPREAD
    for flip in range(SPREAD):
        at = pl.multiple_of((share ^ flip) * height, SUBS)
        chunk_refs[flip][...] = packed[pl.ds(at, height), :]


def filtered_rows(before, after, inner, outer, turn, s_old, old_gram):
    rows = before.shape[0]
    pairs, old_rows, lanes = s_old.shape
    order = rows + old_rows
    height = packed_rows(order)
    vmem = pl.BlockSpec(memory_space=pltpu.VMEM)
    chunk = jax.ShapeDtypeStruct((height // SPREAD, LANES), jnp.float32)
    return pl.pallas_call(
        filter_kernel,
        out_shape=[jax.ShapeDtypeStruct((pairs, rows, lanes), jnp.bfloat16)] + [chunk] * SPREAD,
        in_specs=[vmem] * 7,
        out_specs=[vmem] * (1 + SPREAD),
        scratch_shapes=[pltpu.VMEM((height, LANES), jnp.float32)],
        compiler_params=pltpu.CompilerParams(vmem_limit_bytes=VMEM_BYTES),
        cost_estimate=pl.CostEstimate(
            flops=2 * rows * order * pairs * lanes,
            bytes_accessed=2 * order * pairs * lanes,
            transcendentals=0,
        ),
        name="filter_gram",
    )(before, after, inner, outer, turn, s_old, old_gram)


def sum_chunks(chunks, axis):
    peers = lax.axis_size(axis)
    arrived = [chunks[0]] + [swap(chunks[d], axis, d) for d in range(1, SPREAD)]
    total = (arrived[0] + arrived[1]) + (arrived[2] + arrived[3])
    step = SPREAD
    while step < peers:
        if step * 4 <= peers:
            one, two, three = (swap(total, axis, d * step) for d in (1, 2, 3))
            total = (total + one) + (two + three)
            step *= 4
        else:
            total = total + swap(total, axis, step)
            step *= 2
    return [total] + [swap(total, axis, d) for d in range(1, SPREAD)]


def split_three(x):
    one = x.astype(jnp.bfloat16)
    rest = x - one.astype(jnp.float32)
    two = rest.astype(jnp.bfloat16)
    three = (rest - two.astype(jnp.float32)).astype(jnp.bfloat16)
    return one, two, three


LEFT = (0, 0, 0, 1, 1, 2)
RIGHT = (0, 1, 2, 0, 1, 0)


def small_factor(entry, count):
    unit = [[None] * count for _ in range(count)]
    recip = []
    for k in range(count):
        recip.append(1.0 / entry[k][k])
        for i in range(k + 1, count):
            unit[i][k] = entry[i][k] * recip[k]
        for j in range(k + 1, count):
            for i in range(j, count):
                if i == j:
                    part = (entry[i][k] * entry[i][k]) * recip[k]
                else:
                    part = unit[i][k] * entry[j][k]
                entry[i][j] = entry[i][j] - part
    return unit, recip


def pivots(cols):
    def spread(j, i):
        return jnp.broadcast_to(cols[j, i:i + 1, :], (SUBS, LANES))

    upper, recip = small_factor([[spread(j, i) for j in range(i + 1)] for i in range(HALF)], HALF)
    below = [cols[j, HALF:, :] for j in range(HALF)]
    for k in range(HALF):
        for j in range(k + 1, HALF):
            below[j] = below[j] - below[k] * upper[j][k]
    corner = [cols[j, HALF:, :] for j in range(HALF, PANEL)]
    for k in range(HALF):
        cols[k, HALF:, :] = below[k] * recip[k]
    left = [[spread(k, HALF + i) for k in range(HALF)] for i in range(HALF)]
    for j in range(HALF):
        for k in range(HALF):
            corner[j] = corner[j] - below[k] * left[j][k]
        cols[HALF + j, HALF:, :] = corner[j]
    entry = [[spread(HALF + j, HALF + i) for j in range(i + 1)] for i in range(HALF)]
    lower, more = small_factor(entry, HALF)
    unit = [row + [None] * HALF for row in upper] + [left[i] + lower[i] for i in range(HALF)]
    return unit, recip + more


def left_pieces(panel, t_ref, low, high):
    off = panel * PANEL % LANES
    block = t_ref[panel * PANEL // LANES, low:high, :]
    lane = lax.broadcasted_iota(jnp.int32, block.shape, 1)
    block = jnp.where((lane >= off) & (lane < off + PANEL), block, 0.0)
    pieces = [piece.astype(jnp.float32) for piece in split_three(block)]
    left = pieces[LEFT[0]]
    for k in range(1, len(LEFT)):
        left = left + pltpu.roll(pieces[LEFT[k]], k * PANEL, axis=1)
    return left.astype(jnp.bfloat16)


def right_pieces(panel, v):
    pieces = split_three(v)
    empty = jnp.zeros(v.shape, jnp.bfloat16)
    slots = [empty] * (LANES // PANEL)
    for k in range(len(RIGHT)):
        slots[(panel + k) % len(slots)] = pieces[RIGHT[k]]
    return jnp.concatenate(slots, axis=0)


def subtract(panel, t_ref, low, high, left, right):
    update = jnp.dot(left, right, preferred_element_type=jnp.float32)
    off = panel * PANEL % LANES
    for s in range(t_ref.shape[0]):
        held = t_ref[s, low:high, :]
        if s == panel * PANEL // LANES:
            lane = lax.broadcasted_iota(jnp.int32, held.shape, 1)
            held = jnp.where((lane >= off) & (lane < off + PANEL), 0.0, held)
        t_ref[s, low:high, :] = held - update[:, s * LANES:(s + 1) * LANES]


def factor_panel(panel, t_ref, f_ref, x_ref, cols, rows, late):
    tiles, order, _ = t_ref.shape
    first = panel * PANEL
    end = first + PANEL
    tile, off = first // LANES, first % LANES
    rows_in, rows_v, rows_w = (rows.at[panel % 2, k] for k in range(3))
    cols = cols.at[panel % 2]
    lane = lax.broadcasted_iota(jnp.int32, (PANEL, LANES), 1)
    sub = lax.broadcasted_iota(jnp.int32, (PANEL, LANES), 0)
    inside = (lane >= off) & (lane < off + PANEL)
    own = t_ref[tile, first:end, :]
    for j in range(PANEL):
        cols[j] = jnp.broadcast_to(own[:, off + j:off + j + 1], (PANEL, LANES))
    for s in range(tiles):
        block = t_ref[s, first:end, :]
        if s == tile:
            block = jnp.where(inside, jnp.where(lane - off == sub, 1.0, 0.0), block)
        rows_in[pl.ds(s, PANEL, stride=SUBS), :] = block
    rows_in[pl.ds(tiles, PANEL, stride=SUBS), :] = own
    y = [rows_in[i * SUBS:(i + 1) * SUBS, :] for i in range(PANEL)]
    late()
    near = min(end + PANEL, order)
    if end < order:
        left_near = left_pieces(panel, t_ref, end, near)
    if near < order:
        left_far = left_pieces(panel, t_ref, near, order)

    unit, recip = pivots(cols)
    for k in range(PANEL):
        for i in range(k + 1, PANEL):
            y[i] = y[i] - unit[i][k] * y[k]
    v = [recip[i] * y[i] for i in range(PANEL)]
    for j in reversed(range(PANEL)):
        for i in range(j):
            v[i] = v[i] - unit[j][i] * v[j]
    if end < order:
        for i in range(PANEL):
            rows_v[i * SUBS:(i + 1) * SUBS, :] = v[i]
        right = jnp.concatenate(
            [rows_v[pl.ds(s, PANEL, stride=SUBS), :] for s in range(tiles)], axis=1
        )
        right = right_pieces(panel, right)
        subtract(panel, t_ref, end, near, left_near, right)

    def rest():
        if near < order:
            subtract(panel, t_ref, near, order, left_far, right)

    def outputs():
        for i in range(PANEL):
            rows_w[i * SUBS:(i + 1) * SUBS, :] = jnp.sqrt(recip[i]) * y[i]
        zero = jnp.zeros((PANEL, LANES), jnp.float32)
        for s in range(tiles):
            span = slice(s * LANES, (s + 1) * LANES)
            part = rows_w[pl.ds(s, PANEL, stride=SUBS), :]
            if s == tile:
                whole = rows_w[pl.ds(tiles, PANEL, stride=SUBS), :]
                upper = jnp.where(inside, whole, part)
                f_ref[first:end, span] = jnp.where(lane >= off + sub, upper, 0.0)
                x_ref[first:end, span] = jnp.where(lane <= off + sub, part, 0.0)
            else:
                f_ref[first:end, span] = part if s > tile else zero
                x_ref[first:end, span] = part if s < tile else zero

    return rest, outputs


def factor_kernel(scale, *refs):
    sum_refs, refs = refs[:SPREAD], refs[SPREAD:]
    new_ref, old_ref, f_ref, out_ref, packed, t_ref, x_ref, cols, rows, *refs = refs
    x_pair, stack, mixed, staged, in_sem, out_sem = refs
    tiles, order, _ = t_ref.shape
    _, planes, rows_y, rows_z = out_ref.shape
    new_count = new_ref.shape[1]
    load_new = pltpu.make_async_copy(new_ref, stack.at[:, pl.ds(0, new_count)], in_sem.at[0])
    load_old = pltpu.make_async_copy(
        old_ref, stack.at[:, pl.ds(new_count, order - new_count)], in_sem.at[1]
    )
    load_new.start()
    load_old.start()
    share = lax.axis_index("blk") % SPREAD
    height = packed.shape[0] // SPREAD
    for flip in range(SPREAD):
        at = pl.multiple_of((share ^ flip) * height, SUBS)
        packed[pl.ds(at, height), :] = sum_refs[flip][...] * scale
    i = lax.broadcasted_iota(jnp.int32, (LANES, LANES), 0)
    j = lax.broadcasted_iota(jnp.int32, (LANES, LANES), 1)
    shared = packed[:LANES, :]
    right = packed[LANES:2 * LANES, :]
    upper = jnp.where(j >= i, shared, 0.0)
    lower = jnp.where(j < i, shared, 0.0)
    diagonal = packed[2 * LANES:2 * LANES + 1, :]
    t_ref[0, :LANES, :] = jnp.where(j >= i, shared, upper.T)
    t_ref[1, :LANES, :] = right
    t_ref[0, LANES:, :] = right.T
    corner = jnp.where(j < i, shared, lower.T)
    t_ref[1, LANES:, :] = jnp.where(i == j, diagonal, corner)
    rows[...] = jnp.zeros(rows.shape, jnp.float32)

    turn = turn_matrix(rows_y, 0.0)
    steps = rows_y // 2
    pairs = planes * steps
    starts = [sum(GROUPS[:k]) for k in range(len(GROUPS))]

    def split_rows(group):
        size = GROUPS[group]
        rows_here = x_ref[starts[group]:starts[group] + size, :]
        high = rows_here.astype(jnp.bfloat16)
        x_pair[group, :size, :] = high
        x_pair[group, size:2 * size, :] = (rows_here - high.astype(jnp.float32)).astype(jnp.bfloat16)

    def multiply(group, pair):
        size = GROUPS[group]
        depth = starts[group] + size
        sums = jnp.dot(
            x_pair[group, :2 * size, :depth],
            stack[pair, :depth, :],
            preferred_element_type=jnp.float32,
        )
        sums = (sums[:size] + sums[size:]).astype(jnp.bfloat16)
        sums = sums.reshape(size // rows_y, rows_y, 2 * rows_z)
        some = slice(starts[group] // rows_y, depth // rows_y)
        for half in (0, 1):
            y = 2 * (pair % steps) + half
            at = slice(y * rows_y, (y + 1) * rows_y)
            mixed[pair // steps, some, at, :] = sums[:, :, half * rows_z:(half + 1) * rows_z]

    def store(some):
        at = pl.ds(some * rows_y, rows_y)
        return pltpu.make_async_copy(staged.at[at], out_ref.at[at], out_sem.at[some])

    def finish(some):
        block = jnp.concatenate([mixed[plane, some] for plane in range(planes)], axis=1)
        turned = jnp.dot(turn, block, preferred_element_type=jnp.float32).astype(jnp.bfloat16)
        for plane in range(planes):
            part = turned[:, plane * rows_z:(plane + 1) * rows_z]
            staged[some * rows_y:(some + 1) * rows_y, plane] = part.reshape(rows_y, rows_y, rows_z)
        store(some).start()

    def nothing():
        pass

    late, outputs = nothing, nothing
    for group in range(len(GROUPS)):
        if group == 1:
            load_new.wait()
            load_old.wait()
        panels = GROUPS[group] // PANEL
        for step in range(panels):
            panel = starts[group] // PANEL + step
            before = outputs
            late, outputs = factor_panel(panel, t_ref, f_ref, x_ref, cols, rows, late)
            before()
            if group > 0:
                if step == 0:
                    split_rows(group - 1)
                for pair in range(step * pairs // panels, (step + 1) * pairs // panels):
                    multiply(group - 1, pair)
            if group > 1 and step == 0:
                for some in range(starts[group - 2] // rows_y, starts[group - 1] // rows_y):
                    finish(some)
    outputs()
    last = len(GROUPS) - 1
    split_rows(last)
    for some in range(starts[last - 1] // rows_y, starts[last] // rows_y):
        finish(some)
    for pair in range(pairs):
        multiply(last, pair)
    for some in range(starts[last] // rows_y, order // rows_y):
        finish(some)

    for some in range(order // rows_y):
        store(some).wait()


def factor_and_modes(sums, s_new, s_old, shape, cell_total):
    order, planes, rows_y, rows_z = shape
    height = sums[0].shape[0] * SPREAD
    vmem = pl.BlockSpec(memory_space=pltpu.VMEM)
    hbm = pl.BlockSpec(memory_space=pl.ANY)
    square = (order, order)
    pairs = planes * rows_y // 2
    return pl.pallas_call(
        functools.partial(factor_kernel, 1.0 / cell_total),
        out_shape=[
            jax.ShapeDtypeStruct(square, jnp.float32),
            jax.ShapeDtypeStruct(shape, jnp.bfloat16),
        ],
        in_specs=[vmem] * SPREAD + [hbm, hbm],
        out_specs=[vmem, hbm],
        scratch_shapes=[
            pltpu.VMEM((height, LANES), jnp.float32),
            pltpu.VMEM((order // LANES, order, LANES), jnp.float32),
            pltpu.VMEM(square, jnp.float32),
            pltpu.VMEM((2, PANEL, PANEL, LANES), jnp.float32),
            pltpu.VMEM((2, 3, PANEL * SUBS, LANES), jnp.float32),
            pltpu.VMEM((len(GROUPS), 2 * max(GROUPS), order), jnp.bfloat16),
            pltpu.VMEM((pairs, order, 2 * rows_z), jnp.bfloat16),
            pltpu.VMEM((planes, order // rows_y, rows_y * rows_y, rows_z), jnp.bfloat16),
            pltpu.VMEM(shape, jnp.bfloat16),
            pltpu.SemaphoreType.DMA((2,)),
            pltpu.SemaphoreType.DMA((order // rows_y,)),
        ],
        compiler_params=pltpu.CompilerParams(vmem_limit_bytes=VMEM_BYTES),
        name="factor",
    )(*sums, s_new, s_old)


def shards(snapshots, old_modes, mode_scales, plane_counts, links):
    new_count, planes, rows_y, rows_z = snapshots.shape
    order = new_count + old_modes.shape[0]
    peers = lax.axis_size("blk")
    up = [(i, (i + 1) % peers) for i in range(peers)]
    down = [(j, i) for i, j in up]
    first, last = edge_planes(snapshots, plane_counts)
    before = lax.ppermute(last, "blk", up)
    after = lax.ppermute(first, "blk", down)
    s_old, old_gram, inner, outer, turn = prepared_rows(
        old_modes, snapshots, mode_scales, plane_counts, links
    )
    s_new, *chunks = filtered_rows(before, after, inner, outer, turn, s_old, old_gram)
    sums = sum_chunks(chunks, "blk")
    factor, modes = factor_and_modes(
        sums, s_new, s_old, (order, planes, rows_y, rows_z), peers * planes * rows_y * rows_z
    )
    return (modes, factor)


def solution(mesh):
    return jax.shard_map(
        shards,
        mesh=mesh,
        in_specs=(
            P(None, ("groups", "blk"), None, None),
            P(None, ("groups", "blk"), None, None),
            P("groups"),
            P(("groups", "blk")),
            P(("groups", "blk"), None),
        ),
        out_specs=(P(None, ("groups", "blk"), None, None), P("groups", None)),
        check_vma=False,
    )
```
